32 devices in a mesh: dp: 2 (over x), row: 4 (over y, core), col: 4 (over z).
Axes of the slice: x: 2, y: 2, z: 4, core: 2. Of those that a mesh axis runs over, the one named last changes fastest.
Arguments:
- residual_in: bfloat16 [1576, 768], P(('dp', 'col'), 'row'), may hold values from -12 to 12
- cotangent: float32 [1576, 768], P(('dp', 'col'), 'row'), may hold values from -6 to 6
- qkv_weight: float32 [2, 768, 2304], P(None, 'row', 'col'), may hold values from -0.21875 to 0.21875
- proj_weight: float32 [2, 768, 768], P(None, 'col', 'row'), may hold values from -1.25 to 1.25
- up_weight: float32 [2, 768, 3072], P(None, 'row', 'col'), may hold values from -0.21875 to 0.21875
- down_weight: float32 [2, 3072, 768], P(None, 'col', 'row'), may hold values from -0.109375 to 0.109375
- norm_params: float32 [2, 4, 768], P(None, None, 'row')
- qkv_moment: float32 [2, 768, 2304], P(None, 'row', 'col')
- proj_moment: float32 [2, 768, 768], P(None, 'col', 'row')
- up_moment: float32 [2, 768, 3072], P(None, 'row', 'col')
- down_moment: float32 [2, 3072, 768], P(None, 'col', 'row')
- norm_moment: float32 [2, 4, 768], P(None, None, 'row')
Outputs:
- block_output: float32 [1576, 768], P(('dp', 'col'), 'row')
- input_grad: float32 [1576, 768], P(('dp', 'col'), 'row')
- qkv_grad: float32 [2, 768, 2304], P(None, 'row', 'col')
- proj_grad: float32 [2, 768, 768], P(None, 'col', 'row')
- up_grad: float32 [2, 768, 3072], P(None, 'row', 'col')
- down_grad: float32 [2, 3072, 768], P(None, 'col', 'row')
- norm_grad: float32 [2, 4, 768], P(None, None, 'row')
- qkv_moment_new: float32 [2, 768, 2304], P(None, 'row', 'col')
- proj_moment_new: float32 [2, 768, 768], P(None, 'col', 'row')
- up_moment_new: float32 [2, 768, 3072], P(None, 'row', 'col')
- down_moment_new: float32 [2, 3072, 768], P(None, 'col', 'row')
- norm_moment_new: float32 [2, 4, 768], P(None, None, 'row')
- qkv_new: float32 [2, 768, 2304], P(None, 'row', 'col')
- proj_new: float32 [2, 768, 768], P(None, 'col', 'row')
- up_new: float32 [2, 768, 3072], P(None, 'row', 'col')
- down_new: float32 [2, 3072, 768], P(None, 'col', 'row')
- norm_new: float32 [2, 4, 768], P(None, None, 'row')
The draws below stay inside these ranges and needn't reach their ends.
All inputs are finite; a program needn't handle non-finite values.
Results may differ from the reference program's by a relative error of at most 0.015.
Values may be sent and summed in bfloat16 or wider, within the bound.
No kernel may reach another device: no remote copies, remote signals or barrier semaphores. Data moves between devices by JAX's collectives and lax.ppermute only.
A program may use at most 256 MiB of HBM per device.

```python
import math
import jax
import jax.numpy as jnp
from jax import lax

D = 768
H = 12
HD = 64
FF = 3072
SEQ = 197
LAYERS = 2
IMG_DEV = 1
TOKENS = 1576
N_DP = 2
N_COL = 4


def draw_residual_in(key, part):
    key = jax.random.fold_in(key, 1)
    fraction = jnp.arange(D, dtype=jnp.float32) / D
    entries = jnp.clip(jax.random.normal(key, (TOKENS, D), jnp.float32), -4.0, 4.0) * (1.0 + 2.0 * fraction)
    return entries.astype(jnp.bfloat16)


def draw_norm_params(key, part):
    key = jax.random.fold_in(key, 2)
    entries = 0.3 * jnp.clip(jax.random.normal(key, (LAYERS, 4, D), jnp.float32), -1.5, 1.5)
    gain_rows = (jnp.arange(4) % 2 == 0).reshape(1, 4, 1)
    return jnp.where(gain_rows, 1.0 + entries, entries)


def draw_qkv_moment(key, part):
    key = jax.random.fold_in(key, 3)
    array_shape = (LAYERS, D, 3 * D)
    entries = jnp.clip(jax.random.normal(key, array_shape, jnp.float32), -4.0, 4.0)
    return entries * (0.5 * jnp.sqrt(jnp.float32(TOKENS)))


def draw_proj_moment(key, part):
    key = jax.random.fold_in(key, 4)
    array_shape = (LAYERS, D, D)
    entries = jnp.clip(jax.random.normal(key, array_shape, jnp.float32), -4.0, 4.0)
    return entries * (0.15 * jnp.sqrt(jnp.float32(TOKENS)))


def draw_up_moment(key, part):
    key = jax.random.fold_in(key, 5)
    array_shape = (LAYERS, D, FF)
    entries = jnp.clip(jax.random.normal(key, array_shape, jnp.float32), -4.0, 4.0)
    return entries * (0.5 * jnp.sqrt(jnp.float32(TOKENS)))


def draw_down_moment(key, part):
    key = jax.random.fold_in(key, 6)
    array_shape = (LAYERS, FF, D)
    entries = jnp.clip(jax.random.normal(key, array_shape, jnp.float32), -4.0, 4.0)
    return entries * (0.5 * jnp.sqrt(jnp.float32(TOKENS)))


def draw_norm_moment(key, part):
    key = jax.random.fold_in(key, 7)
    array_shape = (LAYERS, 4, D)
    entries = jnp.clip(jax.random.normal(key, array_shape, jnp.float32), -4.0, 4.0)
    return entries * (0.5 * jnp.sqrt(jnp.float32(TOKENS)))


def block_levels(own_key, shape, split, low, high):
    def one(dim, parts):
        heights = jax.random.uniform(jax.random.fold_in(jax.random.fold_in(own_key, 6), dim), (parts,), jnp.float32, low / len(split), high / len(split))
        return jnp.repeat(jnp.exp(heights), shape[dim] // parts).reshape((-1,) + (1,) * (len(shape) - dim - 1))

    factor_of = one(*split[0])
    for cut in split[1:]:
        factor_of = factor_of * one(*cut)
    return factor_of


def bell_draw(rng, shape, deviation, reach, pieces=(), kind=jnp.bfloat16):
    values = deviation * jax.random.normal(rng, shape, jnp.float32)
    if pieces:
        values = values * block_levels(rng, shape, pieces, -0.22, 0.18)
    return jnp.clip(values, -reach, reach).astype(kind)


def setup_inputs(seed: int = 0) -> dict:
    streams_of = jax.random.split(jax.random.key(seed), 13)
    return {
        "residual_in": draw_residual_in(jax.random.fold_in(streams_of[12], 71), 0),
        "cotangent": bell_draw(streams_of[1], (TOKENS, D), 1.0, 6.0, ((0, 8), (1, 4)), jnp.float32),
        "qkv_weight": bell_draw(streams_of[2], (LAYERS, D, 3 * D), D ** -0.5, 0.21875, ((1, 4), (2, 4)), jnp.float32),
        "proj_weight": bell_draw(streams_of[3], (LAYERS, D, D), (D // 32) ** -0.5, 1.25, ((1, 4), (2, 4)), jnp.float32),
        "up_weight": bell_draw(streams_of[4], (LAYERS, D, FF), D ** -0.5, 0.21875, ((1, 4), (2, 4)), jnp.float32),
        "down_weight": bell_draw(streams_of[5], (LAYERS, FF, D), FF ** -0.5, 0.109375, ((1, 4), (2, 4)), jnp.float32),
        "norm_params": draw_norm_params(jax.random.fold_in(streams_of[12], 71), 0),
        "qkv_moment": draw_qkv_moment(jax.random.fold_in(streams_of[12], 71), 0),
        "proj_moment": draw_proj_moment(jax.random.fold_in(streams_of[12], 71), 0),
        "up_moment": draw_up_moment(jax.random.fold_in(streams_of[12], 71), 0),
        "down_moment": draw_down_moment(jax.random.fold_in(streams_of[12], 71), 0),
        "norm_moment": draw_norm_moment(jax.random.fold_in(streams_of[12], 71), 0),
    }


@jax.custom_vjp
def low(v):
    return lax.optimization_barrier(v.astype(jnp.bfloat16)).astype(jnp.float32)

@jax.custom_vjp
def low_back(v):
    return v

def low_keep(v):
    return (low(v), None)

def low_pass(kept, grad):
    return (grad,)

def back_keep(v):
    return (v, None)

def back_low(kept, grad):
    return (low(grad),)
low.defvjp(low_keep, low_pass)
low_back.defvjp(back_keep, back_low)
norm_epsilon = 1e-06
moment_decay = 0.9
norm_rate = 0.05
step_rates = (1.7, 5.6, 2.0, 1.0)
schulz_first = 3.4445
schulz_second = -4.775
schulz_third = 2.0315
highest = lax.Precision.HIGHEST

def matmul(left_side, right_side):
    return jnp.dot(left_side, right_side, precision=highest)

def norm_apply(values, gain_row, bias_row):
    average = lax.optimization_barrier(jnp.mean(values, axis=1, keepdims=True))
    spread = lax.optimization_barrier(jnp.mean(values * values, axis=1, keepdims=True)) - average * average
    return (values - average) * lax.rsqrt(spread + norm_epsilon) * gain_row + bias_row

def attend_group(mixed):
    query_rows = mixed[:, :, :, 0, :]
    key_rows = mixed[:, :, :, 1, :]
    value_rows = mixed[:, :, :, 2, :]
    scores = low_back(jnp.einsum('bqhd,bkhd->bhqk', query_rows, key_rows, precision=highest) * HD ** (-0.5))
    row_top = lax.optimization_barrier(jnp.max(scores, axis=-1, keepdims=True))
    log_total = jnp.log(lax.optimization_barrier(jnp.sum(jnp.exp(scores - row_top), axis=-1, keepdims=True))) + row_top
    probs = low(jnp.exp(scores - log_total))
    return jnp.einsum('bhqk,bkhd->bqhd', probs, value_rows, precision=highest)

def forward(stream, qkv_weight, proj_weight, up_weight, down_weight, norm_params):
    for level_index in range(LAYERS):
        normed = low(norm_apply(stream, norm_params[level_index, 0], norm_params[level_index, 1]))
        mixed = low_back(low(matmul(normed, low(qkv_weight[level_index]))))
        grouped = mixed.reshape(N_DP, IMG_DEV * N_COL, SEQ, H, 3, HD)
        attended = lax.map(jax.checkpoint(attend_group), grouped).reshape(TOKENS, D)
        attended = low_back(low(attended))
        stream = stream + low_back(matmul(attended, low(proj_weight[level_index])))
        normed = low(norm_apply(stream, norm_params[level_index, 2], norm_params[level_index, 3]))
        hidden = low_back(matmul(normed, low(up_weight[level_index])))
        activated = low(jax.nn.gelu(hidden, approximate=False))
        stream = stream + low_back(matmul(activated, low(down_weight[level_index])))
    return stream

def schulz(matrix):
    current = matrix / (jnp.sqrt(jnp.sum(matrix * matrix)) + 1e-07)
    for sweep_index in range(5):
        gram_matrix = jnp.dot(current, current.T, precision=highest)
        square = schulz_second * gram_matrix + schulz_third * jnp.dot(gram_matrix, gram_matrix, precision=highest)
        current = schulz_first * current + jnp.dot(square, current, precision=highest)
    return current

def orthogonal(moments, flipped):
    if flipped:
        return jnp.stack([schulz(moments[level_index].T).T for level_index in range(LAYERS)])
    return jnp.stack([schulz(moments[level_index]) for level_index in range(LAYERS)])

def reference(residual_in, cotangent, qkv_weight, proj_weight, up_weight, down_weight, norm_params, qkv_moment, proj_moment, up_moment, down_moment, norm_moment):
    block_output, pullback = jax.vjp(forward, residual_in.astype(jnp.float32), qkv_weight, proj_weight, up_weight, down_weight, norm_params)
    input_grad, qkv_grad, proj_grad, up_grad, down_grad, norm_grad = pullback(cotangent)
    qkv_moment_new = moment_decay * qkv_moment + qkv_grad
    proj_moment_new = moment_decay * proj_moment + proj_grad
    up_moment_new = moment_decay * up_moment + up_grad
    down_moment_new = moment_decay * down_moment + down_grad
    norm_moment_new = moment_decay * norm_moment + norm_grad
    qkv_new = qkv_weight - step_rates[0] * orthogonal(qkv_moment_new, False)
    proj_new = proj_weight - step_rates[1] * orthogonal(proj_moment_new, True)
    up_new = up_weight - step_rates[2] * orthogonal(up_moment_new, False)
    down_new = down_weight - step_rates[3] * orthogonal(down_moment_new, True)
    norm_new = norm_params - norm_rate / math.sqrt(TOKENS) * norm_moment_new
    return (block_output, input_grad, qkv_grad, proj_grad, up_grad, down_grad, norm_grad, qkv_moment_new, proj_moment_new, up_moment_new, down_moment_new, norm_moment_new, qkv_new, proj_new, up_new, down_new, norm_new)
```

```python
import math

import jax
import jax.numpy as jnp
from jax import lax
from jax.sharding import PartitionSpec as P

HD = 64

norm_epsilon = 1e-06
moment_decay = 0.9
norm_rate = 0.05
step_rates = (1.7, 5.6, 2.0, 1.0)
schulz_first = 3.4445
schulz_second = -4.775
schulz_third = 2.0315
high = lax.Precision.HIGH
kinds = 4


def product(left_side, right_side):
    return lax.dot_general(
        left_side, right_side, (((1,), (0,)), ((), ())), preferred_element_type=jnp.float32
    )


def product_flipped(left_side, right_side):
    return lax.dot_general(
        left_side, right_side, (((1,), (1,)), ((), ())), preferred_element_type=jnp.float32
    )


def outer_grad(left_side, right_side):
    return lax.dot_general(
        left_side, right_side, (((0,), (0,)), ((), ())), preferred_element_type=jnp.float32
    )


def dot_high(left_side, right_side):
    return jnp.dot(left_side, right_side, precision=high)


def pad_rows(values, rows):
    return jnp.pad(values, ((0, rows - values.shape[0]), (0, 0)))


def pad_columns(values, columns):
    return jnp.pad(values, ((0, 0), (0, columns - values.shape[1])))


def norm_parts_of(values):
    average = jnp.mean(values, axis=1, keepdims=True)
    square = jnp.mean(values * values, axis=1, keepdims=True)
    inverse = lax.rsqrt(square - average * average + norm_epsilon)
    return ((values - average) * inverse, inverse)


def norm_backward(grad_out, plain, inverse, gain_row):
    scaled = grad_out * gain_row
    first = jnp.mean(scaled, axis=1, keepdims=True)
    second = jnp.mean(scaled * plain, axis=1, keepdims=True)
    return inverse * (scaled - first - plain * second)


def split_heads(mixed_low):
    token_count = mixed_low.shape[0]
    heads_here = mixed_low.shape[1] // (3 * HD)
    grouped = mixed_low.reshape(token_count, heads_here, 3, HD)
    return (grouped[:, :, 0, :], grouped[:, :, 1, :], grouped[:, :, 2, :])


def score_block(query_rows, key_rows):
    return jnp.einsum(
        "qhd,khd->hqk", query_rows, key_rows, preferred_element_type=jnp.float32
    ) * HD ** (-0.5)


def attend_forward(mixed_low):
    query_rows, key_rows, value_rows = split_heads(mixed_low)
    scores = score_block(query_rows, key_rows)
    row_top = jnp.max(scores, axis=-1, keepdims=True)
    log_total = jnp.log(jnp.sum(jnp.exp(scores - row_top), axis=-1, keepdims=True)) + row_top
    weights = jnp.exp(scores - log_total).astype(jnp.bfloat16)
    attended = jnp.einsum("hqk,khd->qhd", weights, value_rows, preferred_element_type=jnp.float32)
    return (attended.reshape(mixed_low.shape[0], -1).astype(jnp.bfloat16), log_total)


def attend_backward(mixed_low, log_total, grad_att):
    query_rows, key_rows, value_rows = split_heads(mixed_low)
    scores = score_block(query_rows, key_rows)
    probs = jnp.exp(scores - log_total)
    grad_out = grad_att.reshape(query_rows.shape)
    grad_probs = jnp.einsum(
        "qhd,khd->hqk", grad_out, value_rows, preferred_element_type=jnp.float32
    )
    grad_scores = (
        probs * (grad_probs - jnp.sum(probs * grad_probs, axis=-1, keepdims=True))
    ).astype(jnp.bfloat16)
    scaling = HD ** (-0.5)
    grad_query = (
        jnp.einsum("hqk,khd->qhd", grad_scores, key_rows, preferred_element_type=jnp.float32)
        * scaling
    )
    grad_key = (
        jnp.einsum("hqk,qhd->khd", grad_scores, query_rows, preferred_element_type=jnp.float32)
        * scaling
    )
    grad_value = jnp.einsum(
        "hqk,qhd->khd", probs.astype(jnp.bfloat16), grad_out, preferred_element_type=jnp.float32
    )
    stacked = jnp.stack((grad_query, grad_key, grad_value), axis=2)
    return stacked.reshape(mixed_low.shape[0], -1).astype(jnp.bfloat16)


def swap_row_col(values):
    size = lax.axis_size("row")
    pairs = [(i * size + j, j * size + i) for i in range(size) for j in range(size)]
    return lax.ppermute(values, ("row", "col"), pairs)


def from_partner(values, step):
    count = lax.axis_size("dp") * lax.axis_size("row")
    return lax.ppermute(values, ("dp", "row"), [(i, i ^ step) for i in range(count)])


def pick(stacked, index):
    return lax.dynamic_index_in_dim(stacked, index, 0, keepdims=False)


def gather_tokens(chunk):
    return lax.all_gather(chunk, "col", axis=0, tiled=True)


def sum_tokens(partial, padded):
    size = lax.axis_size("col")
    blocks = pad_rows(partial.astype(jnp.bfloat16), padded)
    blocks = blocks.reshape(size, padded // size, partial.shape[1])
    blocks = lax.all_to_all(blocks, "col", 0, 0)
    return jnp.sum(blocks.astype(jnp.float32), axis=0)


def schulz(raw):
    size = lax.axis_size("col")
    height = raw.shape[0]
    third = height // 3
    strips = [
        lax.dot_general(
            raw[i * third : (i + 1) * third],
            raw[i * third :],
            (((1,), (1,)), ((), ())),
            precision=high,
            preferred_element_type=jnp.float32,
        )
        for i in range(3)
    ]
    packed = jnp.concatenate(strips, axis=1)
    blocks = lax.all_to_all(packed.reshape(size, third // size, -1), "col", 0, 0)
    packed = lax.all_gather(jnp.sum(blocks, axis=0), "col", axis=0, tiled=True)
    first = packed[:, :height]
    second = packed[:, height : 2 * height - third]
    last = packed[:, 2 * height - third :]
    gram = jnp.concatenate(
        [
            first,
            jnp.concatenate([first[:, third : 2 * third].T, second], axis=1),
            jnp.concatenate([first[:, 2 * third :].T, second[:, third:].T, last], axis=1),
        ],
        axis=0,
    )
    eye = jnp.eye(height, dtype=jnp.float32)
    scale = 1.0 / (jnp.sqrt(jnp.sum(gram * eye)) + 1e-07)
    current = raw * scale
    gram = gram * (scale * scale)
    for sweep_index in range(5):
        square = schulz_second * gram + schulz_third * dot_high(gram, gram)
        if sweep_index < 4:
            both = jnp.concatenate([gram, current], axis=1)
            both = schulz_first * both + dot_high(square, both)
            half = both[:, :height]
            current = both[:, height:]
            gram = schulz_first * half + dot_high(half, square)
        else:
            current = schulz_first * current + dot_high(square, current)
    return current


def on_device(
    residual_in,
    cotangent,
    qkv_weight,
    proj_weight,
    up_weight,
    down_weight,
    norm_params,
    qkv_moment,
    proj_moment,
    up_moment,
    down_moment,
    norm_moment,
):
    tokens, width_row = residual_in.shape
    row_size = lax.axis_size("row")
    col_size = lax.axis_size("col")
    dp_size = lax.axis_size("dp")
    model_width = width_row * row_size
    levels = qkv_weight.shape[0]
    jobs = levels * kinds
    chunk = -(-tokens // (8 * col_size)) * 8
    padded = chunk * col_size
    sent_rows = -(-tokens // 16) * 16
    me = (lax.axis_index("dp") * row_size + lax.axis_index("row")) % jobs
    my_row = lax.axis_index("row")
    my_chunk = lax.axis_index("col") * chunk

    weights = (qkv_weight, proj_weight, up_weight, down_weight)
    moments = (qkv_moment, proj_moment, up_moment, down_moment)
    flipped = (False, True, False, True)

    def upright(array, kind_index, level_index):
        block = array[level_index]
        return block.T if flipped[kind_index] else block

    widths = [
        w.shape[1] if flipped[k] else w.shape[2] for k, w in enumerate(weights)
    ]
    widest = max(widths)

    def gathered_weights(level_index, which):
        parts = [upright(weights[k], k, level_index).astype(jnp.bfloat16) for k in which]
        whole = lax.all_gather(jnp.concatenate(parts, axis=1), "row", axis=0, tiled=True)
        result = []
        start = 0
        for k in which:
            result.append(whole[:, start : start + widths[k]])
            start += widths[k]
        return result

    def whole_image(values):
        gathered = swap_row_col(lax.all_gather(values, "row", axis=0, tiled=False))
        return gathered.transpose(1, 0, 2).reshape(tokens, model_width)

    def own_chunk(values):
        return lax.dynamic_slice_in_dim(pad_rows(values, padded), my_chunk, chunk, 0)

    all_norms = lax.all_gather(norm_params, "row", axis=2, tiled=True)
    image = whole_image(residual_in).astype(jnp.float32)
    weight_sets = []
    for level_index in range(levels):
        attention = gathered_weights(level_index, (0, 1))
        perceptron = gathered_weights(level_index, (2, 3))
        weight_sets.append(attention + perceptron)
    upstream_image = whole_image(cotangent)

    stacked_moment = jnp.stack(
        [
            pad_columns(upright(moments[j // levels], j // levels, j % levels), widest)
            for j in range(jobs)
        ]
    )
    moment_parts = [pick(stacked_moment, me)]
    for step in range(1, row_size):
        moment_parts.append(from_partner(pick(stacked_moment, me ^ step), step))
    moment_parts = jnp.stack(moment_parts)
    own_moment = jnp.concatenate([pick(moment_parts, my_row ^ i) for i in range(row_size)], axis=0)

    stream = own_chunk(image)
    saved = []
    early = []
    for level_index in range(levels):
        weight_qkv, weight_proj, weight_up, weight_down = weight_sets[level_index]
        gains = all_norms[level_index]
        plain_one, inverse_one = norm_parts_of(stream)
        if level_index == 0:
            normed_one = (norm_parts_of(image)[0] * gains[0] + gains[1]).astype(jnp.bfloat16)
        else:
            normed_one = gather_tokens(
                (plain_one * gains[0] + gains[1]).astype(jnp.bfloat16)
            )[:tokens]
        mixed_low = product(normed_one, weight_qkv).astype(jnp.bfloat16)
        attended, log_total = attend_forward(mixed_low)
        stream = stream + sum_tokens(product_flipped(attended, weight_proj), padded)
        plain_two, inverse_two = norm_parts_of(stream)
        normed_two = gather_tokens((plain_two * gains[2] + gains[3]).astype(jnp.bfloat16))[:tokens]
        hidden = product(normed_two, weight_up)
        activated = jax.nn.gelu(hidden, approximate=False).astype(jnp.bfloat16)
        stream = stream + sum_tokens(product_flipped(activated, weight_down), padded)
        saved.append((plain_one, inverse_one, mixed_low, log_total, plain_two, inverse_two, hidden))
        early.append((normed_one, attended, normed_two, activated))

    def job_stack(parts_of_levels):
        return jnp.stack(
            [
                pad_rows(pad_columns(parts_of_levels[j % levels][j // levels], widest), sent_rows)
                for j in range(jobs)
            ]
        )

    def exchanged(stacked):
        received = [pick(stacked, me)]
        for step in range(1, jobs):
            received.append(from_partner(pick(stacked, me ^ step), step))
        return jnp.concatenate(received, axis=0)

    early_all = exchanged(job_stack(early))

    upstream = own_chunk(upstream_image)
    back_two = upstream_image.astype(jnp.bfloat16)
    late = [None] * levels
    norm_sums = [None] * levels
    for level_index in reversed(range(levels)):
        weight_qkv, weight_proj, weight_up, weight_down = weight_sets[level_index]
        plain_one, inverse_one, mixed_low, log_total, plain_two, inverse_two, hidden = saved[
            level_index
        ]
        gains = all_norms[level_index]
        if level_index < levels - 1:
            back_two = gather_tokens(upstream.astype(jnp.bfloat16))[:tokens]
        act_grad = product(back_two, weight_down)
        hidden_grad = jax.vjp(lambda inner: jax.nn.gelu(inner, approximate=False), hidden)[1](
            act_grad
        )[0].astype(jnp.bfloat16)
        normed_grad_two = sum_tokens(product_flipped(hidden_grad, weight_up), padded)
        upstream = upstream + norm_backward(normed_grad_two, plain_two, inverse_two, gains[2])
        back_one = gather_tokens(upstream.astype(jnp.bfloat16))[:tokens]
        att_grad = product(back_one, weight_proj).astype(jnp.bfloat16)
        mixed_grad = attend_backward(mixed_low, log_total, att_grad)
        normed_grad_one = sum_tokens(product_flipped(mixed_grad, weight_qkv), padded)
        upstream = upstream + norm_backward(normed_grad_one, plain_one, inverse_one, gains[0])
        norm_sums[level_index] = jnp.stack(
            (
                jnp.sum(normed_grad_one * plain_one, axis=0),
                jnp.sum(normed_grad_one, axis=0),
                jnp.sum(normed_grad_two * plain_two, axis=0),
                jnp.sum(normed_grad_two, axis=0),
            )
        )
        late[level_index] = (mixed_grad, back_one, hidden_grad, back_two)

    late_all = exchanged(job_stack(late))
    norm_whole = lax.psum(jnp.stack(norm_sums), ("dp", "row", "col"))
    norm_grad = lax.dynamic_slice_in_dim(norm_whole, my_row * width_row, width_row, 2)
    norm_moment_new = moment_decay * norm_moment + norm_grad

    turned = (me // levels) % 2 == 1
    model_side = jnp.where(turned, late_all, early_all)
    hidden_side = jnp.where(turned, early_all, late_all)
    own_grad = outer_grad(model_side, hidden_side)
    step = jobs // row_size
    while step < dp_size:
        pairs = [(i, i ^ step) for i in range(dp_size)]
        own_grad = own_grad + lax.ppermute(own_grad, "dp", pairs)
        step *= 2

    def returned(whole):
        blocks = whole.astype(jnp.bfloat16).reshape(row_size, width_row, widest)
        received = [pick(blocks, my_row)]
        for step in range(1, jobs):
            received.append(from_partner(pick(blocks, (me ^ step) % row_size), step))
        received = jnp.stack(received)
        return [pick(received, me ^ j).astype(jnp.float32) for j in range(jobs)]

    grads = returned(own_grad)
    orths = returned(schulz(moment_decay * own_moment + own_grad))

    grad_outs = []
    moment_outs = []
    new_outs = []
    for kind_index in range(kinds):
        grad_levels = []
        orth_levels = []
        for level_index in range(levels):
            job = kind_index * levels + level_index
            grad_here = grads[job][:, : widths[kind_index]]
            orth_here = orths[job][:, : widths[kind_index]]
            if flipped[kind_index]:
                grad_here = grad_here.T
                orth_here = orth_here.T
            grad_levels.append(grad_here)
            orth_levels.append(orth_here)
        grad_out = jnp.stack(grad_levels)
        grad_outs.append(grad_out)
        moment_outs.append(moment_decay * moments[kind_index] + grad_out)
        new_outs.append(weights[kind_index] - step_rates[kind_index] * jnp.stack(orth_levels))

    def placed(chunk_values):
        blocks = chunk_values.reshape(chunk, col_size, width_row).transpose(1, 0, 2)
        blocks = lax.all_to_all(blocks, "col", 0, 0)
        return swap_row_col(blocks.reshape(padded, width_row)[:tokens])

    tokens_all = tokens * col_size * dp_size
    norm_new = norm_params - norm_rate / math.sqrt(tokens_all) * norm_moment_new
    return (
        placed(stream),
        placed(upstream),
        *grad_outs,
        norm_grad,
        *moment_outs,
        norm_moment_new,
        *new_outs,
        norm_new,
    )


def solution(mesh):
    tokens_spec = P(("dp", "col"), "row")
    wide = P(None, "row", "col")
    tall = P(None, "col", "row")
    norms = P(None, None, "row")
    return jax.shard_map(
        on_device,
        mesh=mesh,
        in_specs=(tokens_spec, tokens_spec) + (wide, tall, wide, tall, norms) * 2,
        out_specs=(tokens_spec, tokens_spec) + (wide, tall, wide, tall, norms) * 3,
        check_vma=False,
    )
```

```python
import math

import jax
import jax.numpy as jnp
from jax import lax
from jax.sharding import PartitionSpec as P

HD = 64

norm_epsilon = 1e-06
moment_decay = 0.9
norm_rate = 0.05
step_rates = (1.7, 5.6, 2.0, 1.0)
schulz_first = 3.4445
schulz_second = -4.775
schulz_third = 2.0315
high = lax.Precision.HIGH
kinds = 4


def product(left_side, right_side):
    return lax.dot_general(
        left_side, right_side, (((1,), (0,)), ((), ())), preferred_element_type=jnp.float32
    )


def product_flipped(left_side, right_side):
    return lax.dot_general(
        left_side, right_side, (((1,), (1,)), ((), ())), preferred_element_type=jnp.float32
    )


def outer_grad(left_side, right_side):
    return lax.dot_general(
        left_side, right_side, (((0,), (0,)), ((), ())), preferred_element_type=jnp.float32
    )


def dot_high(left_side, right_side):
    return jnp.dot(left_side, right_side, precision=high)


def pad_rows(values, rows):
    return jnp.pad(values, ((0, rows - values.shape[0]), (0, 0)))


def pad_columns(values, columns):
    return jnp.pad(values, ((0, 0), (0, columns - values.shape[1])))


def norm_parts_of(values):
    average = jnp.mean(values, axis=1, keepdims=True)
    square = jnp.mean(values * values, axis=1, keepdims=True)
    inverse = lax.rsqrt(square - average * average + norm_epsilon)
    return ((values - average) * inverse, inverse)


def norm_backward(grad_out, plain, inverse, gain_row):
    scaled = grad_out * gain_row
    first = jnp.mean(scaled, axis=1, keepdims=True)
    second = jnp.mean(scaled * plain, axis=1, keepdims=True)
    return inverse * (scaled - first - plain * second)


def split_heads(mixed_low):
    token_count = mixed_low.shape[0]
    heads_here = mixed_low.shape[1] // (3 * HD)
    grouped = mixed_low.reshape(token_count, heads_here, 3, HD)
    return (grouped[:, :, 0, :], grouped[:, :, 1, :], grouped[:, :, 2, :])


def score_block(query_rows, key_rows):
    return jnp.einsum(
        "qhd,khd->hqk", query_rows, key_rows, preferred_element_type=jnp.float32
    ) * HD ** (-0.5)


def attend_forward(mixed_low):
    query_rows, key_rows, value_rows = split_heads(mixed_low)
    scores = score_block(query_rows, key_rows)
    row_top = jnp.max(scores, axis=-1, keepdims=True)
    log_total = jnp.log(jnp.sum(jnp.exp(scores - row_top), axis=-1, keepdims=True)) + row_top
    weights = jnp.exp(scores - log_total).astype(jnp.bfloat16)
    attended = jnp.einsum("hqk,khd->qhd", weights, value_rows, preferred_element_type=jnp.float32)
    return (attended.reshape(mixed_low.shape[0], -1).astype(jnp.bfloat16), log_total)


def attend_backward(mixed_low, log_total, grad_att):
    query_rows, key_rows, value_rows = split_heads(mixed_low)
    scores = score_block(query_rows, key_rows)
    probs = jnp.exp(scores - log_total)
    grad_out = grad_att.reshape(query_rows.shape)
    grad_probs = jnp.einsum(
        "qhd,khd->hqk", grad_out, value_rows, preferred_element_type=jnp.float32
    )
    grad_scores = (
        probs * (grad_probs - jnp.sum(probs * grad_probs, axis=-1, keepdims=True))
    ).astype(jnp.bfloat16)
    scaling = HD ** (-0.5)
    grad_query = (
        jnp.einsum("hqk,khd->qhd", grad_scores, key_rows, preferred_element_type=jnp.float32)
        * scaling
    )
    grad_key = (
        jnp.einsum("hqk,qhd->khd", grad_scores, query_rows, preferred_element_type=jnp.float32)
        * scaling
    )
    grad_value = jnp.einsum(
        "hqk,qhd->khd", probs.astype(jnp.bfloat16), grad_out, preferred_element_type=jnp.float32
    )
    stacked = jnp.stack((grad_query, grad_key, grad_value), axis=2)
    return stacked.reshape(mixed_low.shape[0], -1).astype(jnp.bfloat16)


def swap_row_col(values):
    size = lax.axis_size("row")
    pairs = [(i * size + j, j * size + i) for i in range(size) for j in range(size)]
    return lax.ppermute(values, ("row", "col"), pairs)


def from_partner(values, step, axes=("dp", "row"), wanted=None):
    count = math.prod(lax.axis_size(a) for a in axes)
    pairs = [(i, i ^ step) for i in range(count) if wanted is None or wanted(i ^ step)]
    return lax.ppermute(values, axes, pairs)


def pick(stacked, index):
    return lax.dynamic_index_in_dim(stacked, index, 0, keepdims=False)


def placed_blocks(blocks, places):
    result = jnp.zeros((len(blocks),) + blocks[0].shape, blocks[0].dtype)
    for block, place in zip(blocks, places):
        result = lax.dynamic_update_index_in_dim(result, block, place, 0)
    return result


def gather_by_pairs(values, axis):
    step = lax.axis_size(axis) // 2
    me = lax.axis_index(axis)
    blocks, places = [values], [me]
    while step:
        sent = blocks[0][None] if len(blocks) == 1 else jnp.stack(blocks)
        received = from_partner(sent, step, (axis,))
        blocks = blocks + [received[i] for i in range(len(blocks))]
        places = places + [p ^ step for p in places]
        step //= 2
    return placed_blocks(blocks, places)


def sum_by_pairs(values, axis):
    step = 1
    while step < lax.axis_size(axis):
        values = values + from_partner(values, step, (axis,))
        step *= 2
    return values


def to_all(block, axis):
    size = lax.axis_size(axis)
    return lax.all_to_all(jnp.broadcast_to(block[None], (size,) + block.shape), axis, 0, 0)


def gather_tokens(chunk):
    blocks = to_all(chunk, "col")
    return blocks.reshape(-1, chunk.shape[1])


def sum_tokens(partial, padded):
    size = lax.axis_size("col")
    blocks = pad_rows(partial.astype(jnp.bfloat16), padded)
    blocks = blocks.reshape(size, padded // size, partial.shape[1])
    blocks = lax.all_to_all(blocks, "col", 0, 0)
    return jnp.sum(blocks.astype(jnp.float32), axis=0)


def schulz(raw):
    size = lax.axis_size("col")
    height = raw.shape[0]
    third = height // 3
    strips = [
        lax.dot_general(
            raw[i * third : (i + 1) * third],
            raw[i * third :],
            (((1,), (1,)), ((), ())),
            precision=high,
            preferred_element_type=jnp.float32,
        )
        for i in range(3)
    ]
    packed = jnp.concatenate(strips, axis=1)
    blocks = lax.all_to_all(packed.reshape(size, third // size, -1), "col", 0, 0)
    packed = to_all(jnp.sum(blocks, axis=0), "col").reshape(third, -1)
    first = packed[:, :height]
    second = packed[:, height : 2 * height - third]
    last = packed[:, 2 * height - third :]
    gram = jnp.concatenate(
        [
            first,
            jnp.concatenate([first[:, third : 2 * third].T, second], axis=1),
            jnp.concatenate([first[:, 2 * third :].T, second[:, third:].T, last], axis=1),
        ],
        axis=0,
    )
    eye = jnp.eye(height, dtype=jnp.float32)
    scale = 1.0 / (jnp.sqrt(jnp.sum(gram * eye)) + 1e-07)
    current = raw * scale
    gram = gram * (scale * scale)
    for sweep_index in range(5):
        square = schulz_second * gram + schulz_third * dot_high(gram, gram)
        if sweep_index < 4:
            both = jnp.concatenate([gram, current], axis=1)
            both = schulz_first * both + dot_high(square, both)
            half = both[:, :height]
            current = both[:, height:]
            gram = schulz_first * half + dot_high(half, square)
        else:
            current = schulz_first * current + dot_high(square, current)
    return current


def on_device(
    residual_in,
    cotangent,
    qkv_weight,
    proj_weight,
    up_weight,
    down_weight,
    norm_params,
    qkv_moment,
    proj_moment,
    up_moment,
    down_moment,
    norm_moment,
):
    tokens, width_row = residual_in.shape
    row_size = lax.axis_size("row")
    col_size = lax.axis_size("col")
    dp_size = lax.axis_size("dp")
    model_width = width_row * row_size
    levels = qkv_weight.shape[0]
    jobs = levels * kinds
    chunk = -(-tokens // (8 * col_size)) * 8
    padded = chunk * col_size
    sent_rows = -(-tokens // 16) * 16
    me = (lax.axis_index("dp") * row_size + lax.axis_index("row")) % jobs
    my_row = lax.axis_index("row")
    my_chunk = lax.axis_index("col") * chunk

    weights = (qkv_weight, proj_weight, up_weight, down_weight)
    moments = (qkv_moment, proj_moment, up_moment, down_moment)
    flipped = (False, True, False, True)

    def upright(array, kind_index, level_index):
        block = array[level_index]
        return block.T if flipped[kind_index] else block

    widths = [
        w.shape[1] if flipped[k] else w.shape[2] for k, w in enumerate(weights)
    ]
    widest = max(widths)

    def gathered_weights(level_index, which):
        parts = [upright(weights[k], k, level_index).astype(jnp.bfloat16) for k in which]
        whole = gather_by_pairs(jnp.concatenate(parts, axis=1), "row")
        whole = whole.reshape(model_width, -1)
        result = []
        start = 0
        for k in which:
            result.append(whole[:, start : start + widths[k]])
            start += widths[k]
        return result

    def features_first(blocks):
        return blocks.transpose(1, 0, 2).reshape(blocks.shape[1], model_width)

    def own_chunk(values):
        return lax.dynamic_slice_in_dim(pad_rows(values, padded), my_chunk, chunk, 0)

    all_norms = gather_by_pairs(norm_params, "row")
    all_norms = all_norms.transpose(1, 2, 0, 3).reshape(levels, kinds, model_width)
    image = features_first(to_all(swap_row_col(residual_in), "col")).astype(jnp.float32)
    weight_sets = []
    for level_index in range(levels):
        attention = gathered_weights(level_index, (0, 1))
        perceptron = gathered_weights(level_index, (2, 3))
        weight_sets.append(attention + perceptron)
    upstream_image = features_first(gather_by_pairs(swap_row_col(cotangent), "col"))

    stacked_moment = jnp.stack(
        [
            pad_columns(upright(moments[j // levels], j // levels, j % levels), widest)
            for j in range(jobs)
        ]
    )
    moment_parts = [pick(stacked_moment, me)]
    for step in range(1, row_size):
        moment_parts.append(from_partner(pick(stacked_moment, me ^ step), step))
    own_moment = placed_blocks(moment_parts, [my_row ^ i for i in range(row_size)])
    own_moment = own_moment.reshape(model_width, widest)

    stream = own_chunk(image)
    saved = []
    early = []
    for level_index in range(levels):
        weight_qkv, weight_proj, weight_up, weight_down = weight_sets[level_index]
        gains = all_norms[level_index]
        plain_one, inverse_one = norm_parts_of(stream)
        if level_index == 0:
            normed_one = (norm_parts_of(image)[0] * gains[0] + gains[1]).astype(jnp.bfloat16)
        else:
            normed_one = gather_tokens(
                (plain_one * gains[0] + gains[1]).astype(jnp.bfloat16)
            )[:tokens]
        mixed_low = product(normed_one, weight_qkv).astype(jnp.bfloat16)
        attended, log_total = attend_forward(mixed_low)
        stream = stream + sum_tokens(product_flipped(attended, weight_proj), padded)
        plain_two, inverse_two = norm_parts_of(stream)
        normed_two = gather_tokens((plain_two * gains[2] + gains[3]).astype(jnp.bfloat16))[:tokens]
        hidden = product(normed_two, weight_up)
        activated = jax.nn.gelu(hidden, approximate=False).astype(jnp.bfloat16)
        stream = stream + sum_tokens(product_flipped(activated, weight_down), padded)
        saved.append((plain_one, inverse_one, mixed_low, log_total, plain_two, inverse_two, hidden))
        early.append((normed_one, attended, normed_two, activated))

    def sent_form(values):
        return pad_rows(pad_columns(values, widest), sent_rows)

    early_stack = jnp.stack([sent_form(early[j % levels][j // levels]) for j in range(jobs)])
    early_all = [pick(early_stack, me)]
    for step in range(1, jobs):
        early_all.append(from_partner(pick(early_stack, me ^ step), step))

    def send_late(parts, level_index):
        stack = jnp.stack([sent_form(part) for part in parts])
        received = [pick(stack, me // levels)]
        for step in range(1, jobs):
            received.append(
                from_partner(
                    pick(stack, (me ^ step) // levels),
                    step,
                    wanted=lambda i: i % levels == level_index,
                )
            )
        return received

    upstream = own_chunk(upstream_image)
    back_two = upstream_image.astype(jnp.bfloat16)
    upstream, own_moment = lax.optimization_barrier((upstream, own_moment))
    late = [None] * levels
    norm_sums = [None] * levels
    for level_index in reversed(range(levels)):
        weight_qkv, weight_proj, weight_up, weight_down = weight_sets[level_index]
        plain_one, inverse_one, mixed_low, log_total, plain_two, inverse_two, hidden = saved[
            level_index
        ]
        gains = all_norms[level_index]
        if level_index < levels - 1:
            back_two = gather_tokens(upstream.astype(jnp.bfloat16))[:tokens]
        act_grad = product(back_two, weight_down)
        hidden_grad = jax.vjp(lambda inner: jax.nn.gelu(inner, approximate=False), hidden)[1](
            act_grad
        )[0].astype(jnp.bfloat16)
        normed_grad_two = sum_tokens(product_flipped(hidden_grad, weight_up), padded)
        upstream = upstream + norm_backward(normed_grad_two, plain_two, inverse_two, gains[2])
        if level_index == levels - 1:
            upstream, early_all = lax.optimization_barrier((upstream, early_all))
        else:
            upstream, late[level_index + 1] = lax.optimization_barrier(
                (upstream, late[level_index + 1])
            )
        back_one = gather_tokens(upstream.astype(jnp.bfloat16))[:tokens]
        att_grad = product(back_one, weight_proj).astype(jnp.bfloat16)
        mixed_grad = attend_backward(mixed_low, log_total, att_grad)
        normed_grad_one = sum_tokens(product_flipped(mixed_grad, weight_qkv), padded)
        upstream = upstream + norm_backward(normed_grad_one, plain_one, inverse_one, gains[0])
        norm_sums[level_index] = jnp.stack(
            (
                jnp.sum(normed_grad_one * plain_one, axis=0),
                jnp.sum(normed_grad_one, axis=0),
                jnp.sum(normed_grad_two * plain_two, axis=0),
                jnp.sum(normed_grad_two, axis=0),
            )
        )
        late[level_index] = send_late(
            (mixed_grad, back_one, hidden_grad, back_two), level_index
        )

    norm_whole = jnp.stack(norm_sums)
    for axis in ("row", "col", "dp"):
        norm_whole = sum_by_pairs(norm_whole, axis)
    norm_grad = lax.dynamic_slice_in_dim(norm_whole, my_row * width_row, width_row, 2)
    norm_moment_new = moment_decay * norm_moment + norm_grad

    early_all = jnp.concatenate(early_all, axis=0)
    late_all = jnp.concatenate(late[0], axis=0)
    for level_index in range(1, levels):
        late_all = jnp.where(
            me % levels == level_index, jnp.concatenate(late[level_index], axis=0), late_all
        )
    turned = (me // levels) % 2 == 1
    model_side = jnp.where(turned, late_all, early_all)
    hidden_side = jnp.where(turned, early_all, late_all)
    own_grad = outer_grad(model_side, hidden_side)
    step = jobs // row_size
    while step < dp_size:
        pairs = [(i, i ^ step) for i in range(dp_size)]
        own_grad = own_grad + lax.ppermute(own_grad, "dp", pairs)
        step *= 2

    def returned(whole):
        blocks = whole.astype(jnp.bfloat16).reshape(row_size, width_row, widest)
        received = [pick(blocks, my_row)]
        for step in range(1, jobs):
            received.append(from_partner(pick(blocks, (me ^ step) % row_size), step))
        received = placed_blocks(received, [me ^ j for j in range(jobs)])
        return [received[j].astype(jnp.float32) for j in range(jobs)]

    grads = returned(own_grad)
    orths = returned(schulz(moment_decay * own_moment + own_grad))

    grad_outs = []
    moment_outs = []
    new_outs = []
    for kind_index in range(kinds):
        grad_levels = []
        orth_levels = []
        for level_index in range(levels):
            job = kind_index * levels + level_index
            grad_here = grads[job][:, : widths[kind_index]]
            orth_here = orths[job][:, : widths[kind_index]]
            if flipped[kind_index]:
                grad_here = grad_here.T
                orth_here = orth_here.T
            grad_levels.append(grad_here)
            orth_levels.append(orth_here)
        grad_out = jnp.stack(grad_levels)
        grad_outs.append(grad_out)
        moment_outs.append(moment_decay * moments[kind_index] + grad_out)
        new_outs.append(weights[kind_index] - step_rates[kind_index] * jnp.stack(orth_levels))

    def placed(chunk_values):
        blocks = chunk_values.reshape(chunk, col_size, width_row).transpose(1, 0, 2)
        blocks = lax.all_to_all(blocks, "col", 0, 0)
        return swap_row_col(blocks.reshape(padded, width_row)[:tokens])

    tokens_all = tokens * col_size * dp_size
    norm_new = norm_params - norm_rate / math.sqrt(tokens_all) * norm_moment_new
    return (
        placed(stream),
        placed(upstream),
        *grad_outs,
        norm_grad,
        *moment_outs,
        norm_moment_new,
        *new_outs,
        norm_new,
    )


def solution(mesh):
    tokens_spec = P(("dp", "col"), "row")
    wide = P(None, "row", "col")
    tall = P(None, "col", "row")
    norms = P(None, None, "row")
    return jax.shard_map(
        on_device,
        mesh=mesh,
        in_specs=(tokens_spec, tokens_spec) + (wide, tall, wide, tall, norms) * 2,
        out_specs=(tokens_spec, tokens_spec) + (wide, tall, wide, tall, norms) * 3,
        check_vma=False,
    )
```

```python
import math

import jax
import jax.numpy as jnp
from jax import lax
from jax.sharding import PartitionSpec as P

HD = 64

norm_epsilon = 1e-06
moment_decay = 0.9
norm_rate = 0.05
step_rates = (1.7, 5.6, 2.0, 1.0)
schulz_first = 3.4445
schulz_second = -4.775
schulz_third = 2.0315
high = lax.Precision.HIGH
kinds = 4


def product(left_side, right_side):
    return lax.dot_general(
        left_side, right_side, (((1,), (0,)), ((), ())), preferred_element_type=jnp.float32
    )


def product_flipped(left_side, right_side):
    return lax.dot_general(
        left_side, right_side, (((1,), (1,)), ((), ())), preferred_element_type=jnp.float32
    )


def outer_grad(left_side, right_side):
    return lax.dot_general(
        left_side, right_side, (((0,), (0,)), ((), ())), preferred_element_type=jnp.float32
    )


def dot_high(left_side, right_side):
    return jnp.dot(left_side, right_side, precision=high)


def pad_rows(values, rows):
    return jnp.pad(values, ((0, rows - values.shape[0]), (0, 0)))


def pad_columns(values, columns):
    return jnp.pad(values, ((0, 0), (0, columns - values.shape[1])))


def norm_parts_of(values):
    average = jnp.mean(values, axis=1, keepdims=True)
    square = jnp.mean(values * values, axis=1, keepdims=True)
    inverse = lax.rsqrt(square - average * average + norm_epsilon)
    return ((values - average) * inverse, inverse)


def norm_backward(grad_out, plain, inverse, gain_row):
    scaled = grad_out * gain_row
    first = jnp.mean(scaled, axis=1, keepdims=True)
    second = jnp.mean(scaled * plain, axis=1, keepdims=True)
    return inverse * (scaled - first - plain * second)


def split_heads(mixed_low):
    token_count = mixed_low.shape[0]
    heads_here = mixed_low.shape[1] // (3 * HD)
    grouped = mixed_low.reshape(token_count, heads_here, 3, HD)
    return (grouped[:, :, 0, :], grouped[:, :, 1, :], grouped[:, :, 2, :])


def score_block(query_rows, key_rows):
    return jnp.einsum(
        "qhd,khd->hqk", query_rows, key_rows, preferred_element_type=jnp.float32
    ) * HD ** (-0.5)


def attend_forward(mixed_low):
    query_rows, key_rows, value_rows = split_heads(mixed_low)
    scores = score_block(query_rows, key_rows)
    row_top = jnp.max(scores, axis=-1, keepdims=True)
    log_total = jnp.log(jnp.sum(jnp.exp(scores - row_top), axis=-1, keepdims=True)) + row_top
    weights = jnp.exp(scores - log_total).astype(jnp.bfloat16)
    attended = jnp.einsum("hqk,khd->qhd", weights, value_rows, preferred_element_type=jnp.float32)
    return (attended.reshape(mixed_low.shape[0], -1).astype(jnp.bfloat16), log_total)


def attend_backward(mixed_low, log_total, grad_att):
    query_rows, key_rows, value_rows = split_heads(mixed_low)
    scores = score_block(query_rows, key_rows)
    probs = jnp.exp(scores - log_total)
    grad_out = grad_att.reshape(query_rows.shape)
    grad_probs = jnp.einsum(
        "qhd,khd->hqk", grad_out, value_rows, preferred_element_type=jnp.float32
    )
    grad_scores = (
        probs * (grad_probs - jnp.sum(probs * grad_probs, axis=-1, keepdims=True))
    ).astype(jnp.bfloat16)
    scaling = HD ** (-0.5)
    grad_query = (
        jnp.einsum("hqk,khd->qhd", grad_scores, key_rows, preferred_element_type=jnp.float32)
        * scaling
    )
    grad_key = (
        jnp.einsum("hqk,qhd->khd", grad_scores, query_rows, preferred_element_type=jnp.float32)
        * scaling
    )
    grad_value = jnp.einsum(
        "hqk,qhd->khd", probs.astype(jnp.bfloat16), grad_out, preferred_element_type=jnp.float32
    )
    stacked = jnp.stack((grad_query, grad_key, grad_value), axis=2)
    return stacked.reshape(mixed_low.shape[0], -1).astype(jnp.bfloat16)


def swap_row_col(values):
    size = lax.axis_size("row")
    pairs = [(i * size + j, j * size + i) for i in range(size) for j in range(size)]
    return lax.ppermute(values, ("row", "col"), pairs)


def from_partner(values, step, axes=("dp", "row"), wanted=None):
    count = math.prod(lax.axis_size(a) for a in axes)
    pairs = [(i, i ^ step) for i in range(count) if wanted is None or wanted(i ^ step)]
    return lax.ppermute(values, axes, pairs)


def pick(stacked, index):
    return lax.dynamic_index_in_dim(stacked, index, 0, keepdims=False)


def placed_blocks(blocks, places):
    result = jnp.zeros((len(blocks),) + blocks[0].shape, blocks[0].dtype)
    for block, place in zip(blocks, places):
        result = lax.dynamic_update_index_in_dim(result, block, place, 0)
    return result


def gather_by_pairs(values, axis):
    step = lax.axis_size(axis) // 2
    me = lax.axis_index(axis)
    blocks, places = [values], [me]
    while step:
        sent = blocks[0][None] if len(blocks) == 1 else jnp.stack(blocks)
        received = from_partner(sent, step, (axis,))
        blocks = blocks + [received[i] for i in range(len(blocks))]
        places = places + [p ^ step for p in places]
        step //= 2
    return placed_blocks(blocks, places)


def sum_by_pairs(values, axis):
    step = 1
    while step < lax.axis_size(axis):
        values = values + from_partner(values, step, (axis,))
        step *= 2
    return values


def to_all(block, axis):
    size = lax.axis_size(axis)
    return lax.all_to_all(jnp.broadcast_to(block[None], (size,) + block.shape), axis, 0, 0)


def gather_tokens(chunk):
    blocks = to_all(chunk, "col")
    return blocks.reshape(-1, chunk.shape[1])


def sum_tokens(partial, padded):
    size = lax.axis_size("col")
    blocks = pad_rows(partial.astype(jnp.bfloat16), padded)
    blocks = blocks.reshape(size, padded // size, partial.shape[1])
    blocks = lax.all_to_all(blocks, "col", 0, 0)
    return jnp.sum(blocks.astype(jnp.float32), axis=0)


def gram_of(raw):
    size = lax.axis_size("col")
    height = raw.shape[0]
    third = height // 3
    strips = [
        lax.dot_general(
            raw[i * third : (i + 1) * third],
            raw[i * third :],
            (((1,), (1,)), ((), ())),
            precision=high,
            preferred_element_type=jnp.float32,
        )
        for i in range(3)
    ]
    packed = jnp.concatenate(strips, axis=1)
    blocks = lax.all_to_all(packed.reshape(size, third // size, -1), "col", 0, 0)
    packed = to_all(jnp.sum(blocks, axis=0), "col").reshape(third, -1)
    first = packed[:, :height]
    second = packed[:, height : 2 * height - third]
    last = packed[:, 2 * height - third :]
    return jnp.concatenate(
        [
            first,
            jnp.concatenate([first[:, third : 2 * third].T, second], axis=1),
            jnp.concatenate([first[:, 2 * third :].T, second[:, third:].T, last], axis=1),
        ],
        axis=0,
    )


def schulz(raw, gram):
    height = raw.shape[0]
    eye = jnp.eye(height, dtype=jnp.float32)
    scale = 1.0 / (jnp.sqrt(jnp.sum(gram * eye)) + 1e-07)
    current = raw * scale
    gram = gram * (scale * scale)
    for sweep_index in range(5):
        square = schulz_second * gram + schulz_third * dot_high(gram, gram)
        if sweep_index < 4:
            both = jnp.concatenate([gram, current], axis=1)
            both = schulz_first * both + dot_high(square, both)
            half = both[:, :height]
            current = both[:, height:]
            gram = schulz_first * half + dot_high(half, square)
        else:
            current = schulz_first * current + dot_high(square, current)
    return current


def on_device(
    residual_in,
    cotangent,
    qkv_weight,
    proj_weight,
    up_weight,
    down_weight,
    norm_params,
    qkv_moment,
    proj_moment,
    up_moment,
    down_moment,
    norm_moment,
):
    tokens, width_row = residual_in.shape
    row_size = lax.axis_size("row")
    col_size = lax.axis_size("col")
    dp_size = lax.axis_size("dp")
    model_width = width_row * row_size
    levels = qkv_weight.shape[0]
    jobs = levels * kinds
    chunk = -(-tokens // (8 * col_size)) * 8
    padded = chunk * col_size
    sent_rows = -(-tokens // 16) * 16
    me = (lax.axis_index("dp") * row_size + lax.axis_index("row")) % jobs
    my_row = lax.axis_index("row")
    my_chunk = lax.axis_index("col") * chunk

    weights = (qkv_weight, proj_weight, up_weight, down_weight)
    moments = (qkv_moment, proj_moment, up_moment, down_moment)
    flipped = (False, True, False, True)

    def upright(array, kind_index, level_index):
        block = array[level_index]
        return block.T if flipped[kind_index] else block

    widths = [
        w.shape[1] if flipped[k] else w.shape[2] for k, w in enumerate(weights)
    ]
    widest = max(widths)

    def gathered_weights(level_index, which):
        parts = [upright(weights[k], k, level_index).astype(jnp.bfloat16) for k in which]
        whole = gather_by_pairs(jnp.concatenate(parts, axis=1), "row")
        whole = whole.reshape(model_width, -1)
        result = []
        start = 0
        for k in which:
            result.append(whole[:, start : start + widths[k]])
            start += widths[k]
        return result

    def features_first(blocks):
        return blocks.transpose(1, 0, 2).reshape(blocks.shape[1], model_width)

    def own_chunk(values):
        return lax.dynamic_slice_in_dim(pad_rows(values, padded), my_chunk, chunk, 0)

    all_norms = gather_by_pairs(norm_params, "row")
    all_norms = all_norms.transpose(1, 2, 0, 3).reshape(levels, kinds, model_width)
    image = features_first(to_all(swap_row_col(residual_in), "col")).astype(jnp.float32)
    weight_sets = []
    for level_index in range(levels):
        attention = gathered_weights(level_index, (0, 1))
        perceptron = gathered_weights(level_index, (2, 3))
        weight_sets.append(attention + perceptron)
    cotangent_blocks = pad_rows(swap_row_col(cotangent), padded)
    cotangent_blocks = cotangent_blocks.reshape(col_size, chunk, width_row)
    upstream = features_first(lax.all_to_all(cotangent_blocks, "col", 0, 0))

    upper = (me // row_size) % 2 == 1
    half = jobs // 2
    near_moments = []
    for j in range(half):
        low_job, high_job = [
            pad_columns(upright(moments[i // levels], i // levels, i % levels), widest)
            for i in (j, j + half)
        ]
        near_moments.append(jnp.where(upper, high_job, low_job))
    stacked_moment = jnp.stack(near_moments)
    moment_parts = [pick(stacked_moment, me % half)]
    for step in range(1, row_size):
        moment_parts.append(from_partner(pick(stacked_moment, (me ^ step) % half), step))
    own_moment = placed_blocks(moment_parts, [my_row ^ i for i in range(row_size)])
    own_moment = own_moment.reshape(model_width, widest)

    stream = own_chunk(image)
    saved = []
    early = []
    for level_index in range(levels):
        weight_qkv, weight_proj, weight_up, weight_down = weight_sets[level_index]
        gains = all_norms[level_index]
        plain_one, inverse_one = norm_parts_of(stream)
        if level_index == 0:
            normed_one = (norm_parts_of(image)[0] * gains[0] + gains[1]).astype(jnp.bfloat16)
        else:
            normed_one = gather_tokens(
                (plain_one * gains[0] + gains[1]).astype(jnp.bfloat16)
            )[:tokens]
        mixed_low = product(normed_one, weight_qkv).astype(jnp.bfloat16)
        attended, log_total = attend_forward(mixed_low)
        stream = stream + sum_tokens(product_flipped(attended, weight_proj), padded)
        plain_two, inverse_two = norm_parts_of(stream)
        normed_two = gather_tokens((plain_two * gains[2] + gains[3]).astype(jnp.bfloat16))[:tokens]
        hidden = product(normed_two, weight_up)
        activated = jax.nn.gelu(hidden, approximate=False).astype(jnp.bfloat16)
        stream = stream + sum_tokens(product_flipped(activated, weight_down), padded)
        saved.append((plain_one, inverse_one, mixed_low, log_total, plain_two, inverse_two, hidden))
        early.append((normed_one, attended, normed_two, activated))

    def sent_form(values):
        return pad_rows(pad_columns(values, widest), sent_rows)

    early_stack = jnp.stack([sent_form(early[j % levels][j // levels]) for j in range(jobs)])
    early_all = [pick(early_stack, me)]
    for step in range(1, jobs):
        early_all.append(from_partner(pick(early_stack, me ^ step), step))

    def send_late(parts, level_index):
        stack = jnp.stack([sent_form(part) for part in parts])
        received = [pick(stack, me // levels)]
        for step in range(1, jobs):
            received.append(
                from_partner(
                    pick(stack, (me ^ step) // levels),
                    step,
                    wanted=lambda i: i % levels == level_index,
                )
            )
        return received

    upstream, own_moment = lax.optimization_barrier((upstream, own_moment))
    late = [None] * levels
    norm_sums = [None] * levels
    for level_index in reversed(range(levels)):
        weight_qkv, weight_proj, weight_up, weight_down = weight_sets[level_index]
        plain_one, inverse_one, mixed_low, log_total, plain_two, inverse_two, hidden = saved[
            level_index
        ]
        gains = all_norms[level_index]
        back_two = gather_tokens(upstream.astype(jnp.bfloat16))[:tokens]
        act_grad = product(back_two, weight_down)
        hidden_grad = jax.vjp(lambda inner: jax.nn.gelu(inner, approximate=False), hidden)[1](
            act_grad
        )[0].astype(jnp.bfloat16)
        normed_grad_two = sum_tokens(product_flipped(hidden_grad, weight_up), padded)
        upstream = upstream + norm_backward(normed_grad_two, plain_two, inverse_two, gains[2])
        if level_index == levels - 1:
            upstream, early_all = lax.optimization_barrier((upstream, early_all))
        else:
            upstream, late[level_index + 1] = lax.optimization_barrier(
                (upstream, late[level_index + 1])
            )
        back_one = gather_tokens(upstream.astype(jnp.bfloat16))[:tokens]
        att_grad = product(back_one, weight_proj).astype(jnp.bfloat16)
        mixed_grad = attend_backward(mixed_low, log_total, att_grad)
        normed_grad_one = sum_tokens(product_flipped(mixed_grad, weight_qkv), padded)
        upstream = upstream + norm_backward(normed_grad_one, plain_one, inverse_one, gains[0])
        norm_sums[level_index] = jnp.stack(
            (
                jnp.sum(normed_grad_one * plain_one, axis=0),
                jnp.sum(normed_grad_one, axis=0),
                jnp.sum(normed_grad_two * plain_two, axis=0),
                jnp.sum(normed_grad_two, axis=0),
            )
        )
        late[level_index] = send_late(
            (mixed_grad, back_one, hidden_grad, back_two), level_index
        )

    early_all = jnp.concatenate(early_all, axis=0)
    late_all = jnp.concatenate(late[0], axis=0)
    for level_index in range(1, levels):
        late_all = jnp.where(
            me % levels == level_index, jnp.concatenate(late[level_index], axis=0), late_all
        )
    turned = (me // levels) % 2 == 1
    model_side = jnp.where(turned, late_all, early_all)
    hidden_side = jnp.where(turned, early_all, late_all)
    own_grad = outer_grad(model_side, hidden_side)
    step = jobs // row_size
    while step < dp_size:
        pairs = [(i, i ^ step) for i in range(dp_size)]
        own_grad = own_grad + lax.ppermute(own_grad, "dp", pairs)
        step *= 2

    def returned(whole):
        blocks = whole.astype(jnp.bfloat16).reshape(row_size, width_row, widest)
        received = [pick(blocks, my_row)]
        for step in range(1, jobs):
            received.append(from_partner(pick(blocks, (me ^ step) % row_size), step))
        received = placed_blocks(received, [me ^ j for j in range(jobs)])
        return [received[j].astype(jnp.float32) for j in range(jobs)]

    own_raw = moment_decay * own_moment + own_grad
    gram, own_grad, stream, upstream, norm_sums = lax.optimization_barrier(
        (gram_of(own_raw), own_grad, stream, upstream, norm_sums)
    )
    grads = returned(own_grad)
    norm_whole = jnp.stack(norm_sums)
    for axis in ("row", "col", "dp"):
        norm_whole = sum_by_pairs(norm_whole, axis)
    norm_grad = lax.dynamic_slice_in_dim(norm_whole, my_row * width_row, width_row, 2)
    norm_moment_new = moment_decay * norm_moment + norm_grad

    orths = returned(schulz(own_raw, gram))

    grad_outs = []
    moment_outs = []
    new_outs = []
    for kind_index in range(kinds):
        grad_levels = []
        orth_levels = []
        for level_index in range(levels):
            job = kind_index * levels + level_index
            grad_here = grads[job][:, : widths[kind_index]]
            orth_here = orths[job][:, : widths[kind_index]]
            if flipped[kind_index]:
                grad_here = grad_here.T
                orth_here = orth_here.T
            grad_levels.append(grad_here)
            orth_levels.append(orth_here)
        grad_out = jnp.stack(grad_levels)
        grad_outs.append(grad_out)
        moment_outs.append(moment_decay * moments[kind_index] + grad_out)
        new_outs.append(weights[kind_index] - step_rates[kind_index] * jnp.stack(orth_levels))

    def placed(chunk_values):
        blocks = chunk_values.reshape(chunk, col_size, width_row).transpose(1, 0, 2)
        blocks = lax.all_to_all(blocks, "col", 0, 0)
        return swap_row_col(blocks.reshape(padded, width_row)[:tokens])

    tokens_all = tokens * col_size * dp_size
    norm_new = norm_params - norm_rate / math.sqrt(tokens_all) * norm_moment_new
    return (
        placed(stream),
        placed(upstream),
        *grad_outs,
        norm_grad,
        *moment_outs,
        norm_moment_new,
        *new_outs,
        norm_new,
    )


def solution(mesh):
    tokens_spec = P(("dp", "col"), "row")
    wide = P(None, "row", "col")
    tall = P(None, "col", "row")
    norms = P(None, None, "row")
    return jax.shard_map(
        on_device,
        mesh=mesh,
        in_specs=(tokens_spec, tokens_spec) + (wide, tall, wide, tall, norms) * 2,
        out_specs=(tokens_spec, tokens_spec) + (wide, tall, wide, tall, norms) * 3,
        check_vma=False,
    )
```

```python
import functools
import math

import jax
import jax.numpy as jnp
from jax import lax
from jax.experimental import pallas as pl
from jax.experimental.pallas import tpu as pltpu
from jax.sharding import PartitionSpec as P

HD = 64

norm_epsilon = 1e-06
moment_decay = 0.9
norm_rate = 0.05
step_rates = (1.7, 5.6, 2.0, 1.0)
schulz_first = 3.4445
schulz_second = -4.775
schulz_third = 2.0315
high = lax.Precision.HIGH
kinds = 4


def outer_grad(left_side, right_side):
    return lax.dot_general(
        left_side, right_side, (((0,), (0,)), ((), ())), preferred_element_type=jnp.float32
    )


def dot_high(left_side, right_side):
    return jnp.dot(left_side, right_side, precision=high)


def pad_rows(values, rows):
    return jnp.pad(values, ((0, rows - values.shape[0]), (0, 0)))


def pad_columns(values, columns):
    return jnp.pad(values, ((0, 0), (0, columns - values.shape[1])))


def norm_parts_of(values):
    average = jnp.mean(values, axis=1, keepdims=True)
    square = jnp.mean(values * values, axis=1, keepdims=True)
    inverse = lax.rsqrt(square - average * average + norm_epsilon)
    return ((values - average) * inverse, inverse)


def norm_backward(grad_out, plain, inverse, gain_row):
    scaled = grad_out * gain_row
    first = jnp.mean(scaled, axis=1, keepdims=True)
    second = jnp.mean(scaled * plain, axis=1, keepdims=True)
    return inverse * (scaled - first - plain * second)


def wide_dot(left_side, right_side, left_dim, right_dim):
    return lax.dot_general(
        left_side,
        right_side,
        (((left_dim,), (right_dim,)), ((), ())),
        preferred_element_type=jnp.float32,
    )


def in_vmem(count):
    return [pl.BlockSpec(memory_space=pltpu.VMEM)] * count


def kernel_call(body, inputs, outputs, scratch, flops, position=None):
    specs = in_vmem(len(inputs))
    operands = list(inputs)
    if position is not None:
        specs = [pl.BlockSpec(memory_space=pltpu.SMEM)] + specs
        operands = [position] + operands
    moved = sum(math.prod(o.shape) * o.dtype.itemsize for o in list(inputs) + list(outputs))
    return pl.pallas_call(
        body,
        out_shape=list(outputs),
        in_specs=specs,
        out_specs=in_vmem(len(outputs)),
        scratch_shapes=scratch,
        compiler_params=pltpu.CompilerParams(vmem_limit_bytes=32 * 1024 * 1024),
        cost_estimate=pl.CostEstimate(flops=flops, bytes_accessed=moved, transcendentals=0),
    )(*operands)


def put_chunks(position_ref, chunk_refs, whole_ref):
    chunk = chunk_refs[0].shape[0]
    for k, chunk_ref in enumerate(chunk_refs):
        start = pl.multiple_of((position_ref[0] ^ k) * chunk, 8)
        whole_ref[pl.ds(start, chunk), :] = chunk_ref[...].astype(jnp.float32)


def take_chunks(position_ref, whole_ref, chunk_refs):
    chunk = chunk_refs[0].shape[0]
    for k, chunk_ref in enumerate(chunk_refs):
        start = pl.multiple_of((position_ref[0] ^ k) * chunk, 8)
        chunk_ref[...] = whole_ref[pl.ds(start, chunk), :].astype(chunk_ref.dtype)


def keep_rows(values, tokens):
    rows = lax.broadcasted_iota(jnp.int32, values.shape, 0)
    return jnp.where(rows < tokens, values, jnp.zeros_like(values))


def head_probs(mixed, head, tokens):
    start = head * 3 * HD
    query = mixed[:, start : start + HD]
    key = mixed[:, start + HD : start + 2 * HD]
    value = mixed[:, start + 2 * HD : start + 3 * HD]
    scores = wide_dot(query, key, 1, 1) * HD ** (-0.5)
    columns = lax.broadcasted_iota(jnp.int32, scores.shape, 1)
    scores = jnp.where(columns < tokens, scores, -jnp.inf)
    exps = jnp.exp(scores - jnp.max(scores, axis=1, keepdims=True))
    probs = exps / jnp.sum(exps, axis=1, keepdims=True)
    return (query, key, value, probs)


def attend_kernel(tokens, heads, position, *refs):
    size = (len(refs) - 7) // 2
    chunks, (w_qkv, w_proj) = refs[:size], refs[size : size + 2]
    outs = refs[size + 2 : 2 * size + 2]
    mixed_out, normed_out, att_out, whole, att_all = refs[2 * size + 2 :]
    put_chunks(position, chunks, whole)
    normed = keep_rows(whole[...], tokens).astype(jnp.bfloat16)
    normed_out[...] = normed[: normed_out.shape[0]]
    mixed = wide_dot(normed, w_qkv[...], 1, 0).astype(jnp.bfloat16)
    mixed_out[...] = mixed
    for head in range(heads):
        _, _, value, probs = head_probs(mixed, head, tokens)
        att_all[:, head * HD : (head + 1) * HD] = wide_dot(probs.astype(jnp.bfloat16), value, 1, 0)
    attended = keep_rows(att_all[...], tokens).astype(jnp.bfloat16)
    att_out[...] = jnp.zeros_like(att_out)
    att_out[:, : heads * HD] = attended[: att_out.shape[0]]
    whole[...] = wide_dot(attended, w_proj[...], 1, 1)
    take_chunks(position, whole, outs)


def attend_back_kernel(tokens, heads, position, *refs):
    size = (len(refs) - 7) // 2
    chunks, (mixed_ref, w_qkv, w_proj) = refs[:size], refs[size : size + 3]
    outs = refs[size + 3 : 2 * size + 3]
    mixed_grad_out, back_out, whole, mixed_grad = refs[2 * size + 3 :]
    put_chunks(position, chunks, whole)
    back = whole[...].astype(jnp.bfloat16)
    back_out[...] = back[: back_out.shape[0]]
    att_grad = wide_dot(back, w_proj[...], 1, 0).astype(jnp.bfloat16)
    mixed = mixed_ref[...]
    scaling = HD ** (-0.5)
    for head in range(heads):
        query, key, value, probs = head_probs(mixed, head, tokens)
        grad = att_grad[:, head * HD : (head + 1) * HD]
        probs_grad = wide_dot(grad, value, 1, 1)
        inner = jnp.sum(probs * probs_grad, axis=1, keepdims=True)
        scores_grad = (probs * (probs_grad - inner)).astype(jnp.bfloat16)
        start = head * 3 * HD
        mixed_grad[:, start : start + HD] = wide_dot(scores_grad, key, 1, 0) * scaling
        mixed_grad[:, start + HD : start + 2 * HD] = wide_dot(scores_grad, query, 0, 0) * scaling
        mixed_grad[:, start + 2 * HD : start + 3 * HD] = wide_dot(
            probs.astype(jnp.bfloat16), grad, 0, 0
        )
    grads = mixed_grad[...].astype(jnp.bfloat16)
    mixed_grad_out[...] = jnp.zeros_like(mixed_grad_out)
    mixed_grad_out[:, : grads.shape[1]] = grads[: mixed_grad_out.shape[0]]
    whole[...] = wide_dot(grads, w_qkv[...], 1, 1)
    take_chunks(position, whole, outs)


def norm_kernel(level_index, first_row, size, *refs):
    parts, (stream_ref, norms) = refs[:size], refs[size : size + 2]
    stream_out, normed_out = refs[size + 2 :]
    stream = stream_ref[...]
    for part in parts:
        stream = stream + part[...].astype(jnp.float32)
    stream_out[...] = stream
    plain, _ = norm_parts_of(stream)
    gain = norms[level_index, first_row : first_row + 1, :]
    bias = norms[level_index, first_row + 1 : first_row + 2, :]
    normed_out[...] = (plain * gain + bias).astype(jnp.bfloat16)


def norm_back_kernel(level_index, first_row, size, *refs):
    parts, (stream_ref, upstream_ref, norms) = refs[:size], refs[size : size + 3]
    upstream_out, low_out, sums_out = refs[size + 3 :]
    grad = parts[0][...].astype(jnp.float32)
    for part in parts[1:]:
        grad = grad + part[...].astype(jnp.float32)
    plain, inverse = norm_parts_of(stream_ref[...])
    gain = norms[level_index, first_row : first_row + 1, :]
    upstream = upstream_ref[...] + norm_backward(grad, plain, inverse, gain)
    upstream_out[...] = upstream
    low_out[...] = upstream.astype(jnp.bfloat16)
    sums_out[0:1, :] = jnp.sum(grad * plain, axis=0, keepdims=True)
    sums_out[1:2, :] = jnp.sum(grad, axis=0, keepdims=True)


def first_kernel(tokens, position, blocks, norms, *refs):
    outs, stream_out, whole = refs[:-2], refs[-2], refs[-1]
    size, _, width = blocks.shape
    whole[...] = jnp.zeros_like(whole)
    for i in range(size):
        whole[0:tokens, i * width : (i + 1) * width] = blocks[i].astype(jnp.float32)
    chunk = stream_out.shape[0]
    start = pl.multiple_of(position[0] * chunk, 8)
    stream_out[...] = whole[pl.ds(start, chunk), :]
    plain, _ = norm_parts_of(whole[...])
    whole[...] = plain * norms[0, 0:1, :] + norms[0, 1:2, :]
    take_chunks(position, whole, outs)


def mlp_kernel(tokens, position, *refs):
    size = (len(refs) - 6) // 2
    chunks, (w_up, w_down) = refs[:size], refs[size : size + 2]
    outs = refs[size + 2 : 2 * size + 2]
    slope_out, normed_out, act_out, whole = refs[2 * size + 2 :]
    put_chunks(position, chunks, whole)
    normed = keep_rows(whole[...], tokens).astype(jnp.bfloat16)
    normed_out[...] = normed[: normed_out.shape[0]]
    hidden = wide_dot(normed, w_up[...], 1, 0)
    below = 0.5 + 0.5 * lax.erf(hidden * math.sqrt(0.5))
    slope_out[...] = below + hidden * jnp.exp(-0.5 * hidden * hidden) * (
        1.0 / math.sqrt(2.0 * math.pi)
    )
    activated = keep_rows(hidden * below, tokens).astype(jnp.bfloat16)
    act_out[...] = activated[: act_out.shape[0]]
    whole[...] = wide_dot(activated, w_down[...], 1, 1)
    take_chunks(position, whole, outs)


def mlp_back_kernel(position, *refs):
    size = (len(refs) - 6) // 2
    chunks, (slope, w_up, w_down) = refs[:size], refs[size : size + 3]
    outs = refs[size + 3 : 2 * size + 3]
    hidden_grad_out, back_out, whole = refs[2 * size + 3 :]
    put_chunks(position, chunks, whole)
    back = whole[...].astype(jnp.bfloat16)
    back_out[...] = back[: back_out.shape[0]]
    hidden_grad = (wide_dot(back, w_down[...], 1, 0) * slope[...]).astype(jnp.bfloat16)
    hidden_grad_out[...] = hidden_grad[: hidden_grad_out.shape[0]]
    whole[...] = wide_dot(hidden_grad, w_up[...], 1, 1)
    take_chunks(position, whole, outs)


def swap_row_col(values):
    size = lax.axis_size("row")
    pairs = [(i * size + j, j * size + i) for i in range(size) for j in range(size)]
    return lax.ppermute(values, ("row", "col"), pairs)


def from_partner(values, step, axes=("dp", "row"), wanted=None):
    count = math.prod(lax.axis_size(a) for a in axes)
    pairs = [(i, i ^ step) for i in range(count) if wanted is None or wanted(i ^ step)]
    return lax.ppermute(values, axes, pairs)


def pick(stacked, index):
    return lax.dynamic_index_in_dim(stacked, index, 0, keepdims=False)


def placed_blocks(blocks, places):
    result = jnp.zeros((len(blocks),) + blocks[0].shape, blocks[0].dtype)
    for block, place in zip(blocks, places):
        result = lax.dynamic_update_index_in_dim(result, block, place, 0)
    return result


def gather_by_pairs(values, axis):
    step = lax.axis_size(axis) // 2
    me = lax.axis_index(axis)
    blocks, places = [values], [me]
    while step:
        sent = blocks[0][None] if len(blocks) == 1 else jnp.stack(blocks)
        received = from_partner(sent, step, (axis,))
        blocks = blocks + [received[i] for i in range(len(blocks))]
        places = places + [p ^ step for p in places]
        step //= 2
    return placed_blocks(blocks, places)


def sum_by_pairs(values, axis):
    step = 1
    while step < lax.axis_size(axis):
        values = values + from_partner(values, step, (axis,))
        step *= 2
    return values


def to_all(block, axis):
    size = lax.axis_size(axis)
    return lax.all_to_all(jnp.broadcast_to(block[None], (size,) + block.shape), axis, 0, 0)


def to_partners(chunk):
    size = lax.axis_size("col")
    return [chunk] + [from_partner(chunk, k, ("col",)) for k in range(1, size)]


def swap_parts(parts):
    return [parts[0]] + [from_partner(parts[k], k, ("col",)) for k in range(1, len(parts))]


def gram_of(raw):
    size = lax.axis_size("col")
    height = raw.shape[0]
    third = height // 3
    strips = [
        lax.dot_general(
            raw[i * third : (i + 1) * third],
            raw[i * third :],
            (((1,), (1,)), ((), ())),
            precision=high,
            preferred_element_type=jnp.float32,
        )
        for i in range(3)
    ]
    packed = jnp.concatenate(strips, axis=1)
    blocks = lax.all_to_all(packed.reshape(size, third // size, -1), "col", 0, 0)
    packed = to_all(jnp.sum(blocks, axis=0), "col").reshape(third, -1)
    first = packed[:, :height]
    second = packed[:, height : 2 * height - third]
    last = packed[:, 2 * height - third :]
    return jnp.concatenate(
        [
            first,
            jnp.concatenate([first[:, third : 2 * third].T, second], axis=1),
            jnp.concatenate([first[:, 2 * third :].T, second[:, third:].T, last], axis=1),
        ],
        axis=0,
    )


def schulz(raw, gram):
    height = raw.shape[0]
    eye = jnp.eye(height, dtype=jnp.float32)
    scale = 1.0 / (jnp.sqrt(jnp.sum(gram * eye)) + 1e-07)
    current = raw * scale
    gram = gram * (scale * scale)
    for sweep_index in range(5):
        square = schulz_second * gram + schulz_third * dot_high(gram, gram)
        if sweep_index < 4:
            both = jnp.concatenate([gram, current], axis=1)
            both = schulz_first * both + dot_high(square, both)
            half = both[:, :height]
            current = both[:, height:]
            gram = schulz_first * half + dot_high(half, square)
        else:
            current = schulz_first * current + dot_high(square, current)
    return current


def on_device(
    residual_in,
    cotangent,
    qkv_weight,
    proj_weight,
    up_weight,
    down_weight,
    norm_params,
    qkv_moment,
    proj_moment,
    up_moment,
    down_moment,
    norm_moment,
):
    tokens, width_row = residual_in.shape
    row_size = lax.axis_size("row")
    col_size = lax.axis_size("col")
    dp_size = lax.axis_size("dp")
    model_width = width_row * row_size
    levels = qkv_weight.shape[0]
    jobs = levels * kinds
    chunk = -(-tokens // (8 * col_size)) * 8
    padded = chunk * col_size
    sent_rows = -(-tokens // 16) * 16
    me = (lax.axis_index("dp") * row_size + lax.axis_index("row")) % jobs
    my_row = lax.axis_index("row")
    my_chunk = lax.axis_index("col") * chunk

    weights = (qkv_weight, proj_weight, up_weight, down_weight)
    moments = (qkv_moment, proj_moment, up_moment, down_moment)
    flipped = (False, True, False, True)

    def upright(array, kind_index, level_index):
        block = array[level_index]
        return block.T if flipped[kind_index] else block

    widths = [
        w.shape[1] if flipped[k] else w.shape[2] for k, w in enumerate(weights)
    ]
    widest = max(widths)

    def gathered_weights(level_index, which):
        parts = [upright(weights[k], k, level_index).astype(jnp.bfloat16) for k in which]
        whole = gather_by_pairs(jnp.concatenate(parts, axis=1), "row")
        whole = whole.reshape(model_width, -1)
        result = []
        start = 0
        for k in which:
            result.append(whole[:, start : start + widths[k]])
            start += widths[k]
        return result

    def features_first(blocks):
        return blocks.transpose(1, 0, 2).reshape(blocks.shape[1], model_width)

    all_norms = gather_by_pairs(norm_params, "row")
    all_norms = all_norms.transpose(1, 2, 0, 3).reshape(levels, kinds, model_width)
    image_blocks = to_all(swap_row_col(residual_in), "col")
    weight_sets = []
    for level_index in range(levels):
        attention = gathered_weights(level_index, (0, 1))
        perceptron = gathered_weights(level_index, (2, 3))
        weight_sets.append(attention + perceptron)
    cotangent_blocks = pad_rows(swap_row_col(cotangent), padded)
    cotangent_blocks = cotangent_blocks.reshape(col_size, chunk, width_row)
    upstream = features_first(lax.all_to_all(cotangent_blocks, "col", 0, 0))

    upper = (me // row_size) % 2 == 1
    half = jobs // 2
    near_moments = []
    for j in range(half):
        low_job, high_job = [
            pad_columns(upright(moments[i // levels], i // levels, i % levels), widest)
            for i in (j, j + half)
        ]
        near_moments.append(jnp.where(upper, high_job, low_job))
    stacked_moment = jnp.stack(near_moments)
    moment_parts = [pick(stacked_moment, me % half)]
    for step in range(1, row_size):
        moment_parts.append(from_partner(pick(stacked_moment, (me ^ step) % half), step))
    own_moment = placed_blocks(moment_parts, [my_row ^ i for i in range(row_size)])
    own_moment = own_moment.reshape(model_width, widest)

    position = lax.axis_index("col").astype(jnp.int32).reshape(1)
    heads = widths[0] // (3 * HD)

    def shaped(rows, columns, kind):
        return jax.ShapeDtypeStruct((rows, columns), kind)

    low_chunk = shaped(chunk, model_width, jnp.bfloat16)
    full_chunk = shaped(chunk, model_width, jnp.float32)
    low_chunks = [low_chunk] * col_size
    sent = shaped(sent_rows, widest, jnp.bfloat16)
    sent_model = shaped(sent_rows, model_width, jnp.bfloat16)
    whole_scratch = pltpu.VMEM((padded, model_width), jnp.float32)
    attention_flops = 2 * padded * (
        model_width * (widths[0] + widths[1]) + 2 * padded * widths[1]
    )
    perceptron_flops = 2 * padded * model_width * (widths[2] + widths[3])
    chunk_flops = 20 * chunk * model_width

    def norm_step(parts, stream, level_index, first_row):
        return kernel_call(
            functools.partial(norm_kernel, level_index, first_row, len(parts)),
            [*parts, stream, all_norms],
            [full_chunk, low_chunk],
            [],
            chunk_flops,
        )

    def norm_back_step(parts, stream, upstream, level_index, first_row):
        return kernel_call(
            functools.partial(norm_back_kernel, level_index, first_row, len(parts)),
            [*parts, stream, upstream, all_norms],
            [full_chunk, low_chunk, shaped(2, model_width, jnp.float32)],
            [],
            chunk_flops,
        )

    *chunks, stream = kernel_call(
        functools.partial(first_kernel, tokens),
        [image_blocks, all_norms],
        low_chunks + [full_chunk],
        [whole_scratch],
        20 * padded * model_width,
        position,
    )
    saved = []
    early = []
    for level_index in range(levels):
        weight_qkv, weight_proj, weight_up, weight_down = weight_sets[level_index]
        stream_one = stream
        *parts, mixed, normed_one, attended = kernel_call(
            functools.partial(attend_kernel, tokens, heads),
            [*chunks, weight_qkv, weight_proj],
            low_chunks + [shaped(padded, widths[0], jnp.bfloat16), sent_model, sent],
            [whole_scratch, pltpu.VMEM((padded, widths[1]), jnp.float32)],
            attention_flops,
            position,
        )
        stream_two, normed = norm_step(swap_parts(parts), stream, level_index, 2)
        chunks = to_partners(normed)
        *parts, slope, normed_two, activated = kernel_call(
            functools.partial(mlp_kernel, tokens),
            [*chunks, weight_up, weight_down],
            low_chunks + [shaped(padded, widths[2], jnp.float32), sent_model, sent],
            [whole_scratch],
            perceptron_flops,
            position,
        )
        parts = swap_parts(parts)
        if level_index < levels - 1:
            stream, normed = norm_step(parts, stream_two, level_index + 1, 0)
            chunks = to_partners(normed)
        else:
            stream = stream_two
            for part in parts:
                stream = stream + part.astype(jnp.float32)
        saved.append((stream_one, stream_two, mixed, slope))
        early.append((normed_one, attended, normed_two, activated))

    early_stack = jnp.stack([early[j % levels][j // levels] for j in range(jobs)])
    early_all = [pick(early_stack, me)]
    for step in range(1, jobs):
        early_all.append(from_partner(pick(early_stack, me ^ step), step))

    def send_late(parts, level_index):
        stack = jnp.stack(parts)
        received = [pick(stack, me // levels)]
        for step in range(1, jobs):
            received.append(
                from_partner(
                    pick(stack, (me ^ step) // levels),
                    step,
                    wanted=lambda i: i % levels == level_index,
                )
            )
        return received

    upstream, own_moment = lax.optimization_barrier((upstream, own_moment))
    late = [None] * levels
    norm_sums = [None] * levels
    back_low = upstream.astype(jnp.bfloat16)
    for level_index in reversed(range(levels)):
        weight_qkv, weight_proj, weight_up, weight_down = weight_sets[level_index]
        stream_one, stream_two, mixed, slope = saved[level_index]
        *parts, hidden_grad, back_two = kernel_call(
            mlp_back_kernel,
            [*to_partners(back_low), slope, weight_up, weight_down],
            low_chunks + [sent, sent_model],
            [whole_scratch],
            perceptron_flops,
            position,
        )
        upstream, back_low, sums_two = norm_back_step(
            swap_parts(parts), stream_two, upstream, level_index, 2
        )
        if level_index == levels - 1:
            back_low, early_all = lax.optimization_barrier((back_low, early_all))
        else:
            back_low, late[level_index + 1] = lax.optimization_barrier(
                (back_low, late[level_index + 1])
            )
        *parts, mixed_grad, back_one = kernel_call(
            functools.partial(attend_back_kernel, tokens, heads),
            [*to_partners(back_low), mixed, weight_qkv, weight_proj],
            low_chunks + [sent, sent_model],
            [whole_scratch, pltpu.VMEM((padded, widths[0]), jnp.float32)],
            3 * attention_flops,
            position,
        )
        late[level_index] = send_late(
            (mixed_grad, back_one, hidden_grad, back_two), level_index
        )
        if level_index:
            upstream, back_low, sums_one = norm_back_step(
                swap_parts(parts), stream_one, upstream, level_index, 0
            )
            norm_sums[level_index] = jnp.concatenate([sums_one, sums_two])

    early_all = jnp.concatenate(early_all, axis=0)
    late_all = jnp.concatenate(late[0], axis=0)
    for level_index in range(1, levels):
        late_all = jnp.where(
            me % levels == level_index, jnp.concatenate(late[level_index], axis=0), late_all
        )
    turned = (me // levels) % 2 == 1
    model_side = jnp.where(turned, late_all, early_all)
    hidden_side = jnp.where(turned, early_all, late_all)
    own_grad = outer_grad(model_side, hidden_side)
    step = jobs // row_size
    while step < dp_size:
        pairs = [(i, i ^ step) for i in range(dp_size)]
        own_grad = own_grad + lax.ppermute(own_grad, "dp", pairs)
        step *= 2

    def returned(whole):
        blocks = whole.astype(jnp.bfloat16).reshape(row_size, width_row, widest)
        received = [pick(blocks, my_row)]
        for step in range(1, jobs):
            received.append(from_partner(pick(blocks, (me ^ step) % row_size), step))
        received = placed_blocks(received, [me ^ j for j in range(jobs)])
        return [received[j].astype(jnp.float32) for j in range(jobs)]

    own_raw = moment_decay * own_moment + own_grad
    gram, own_grad, stream, parts = lax.optimization_barrier(
        (gram_of(own_raw), own_grad, stream, parts)
    )
    upstream, _, sums_one = norm_back_step(swap_parts(parts), stream_one, upstream, 0, 0)
    norm_sums[0] = jnp.concatenate([sums_one, sums_two])
    grads = returned(own_grad)
    norm_whole = jnp.stack(norm_sums)
    for axis in ("row", "col", "dp"):
        norm_whole = sum_by_pairs(norm_whole, axis)
    norm_grad = lax.dynamic_slice_in_dim(norm_whole, my_row * width_row, width_row, 2)
    norm_moment_new = moment_decay * norm_moment + norm_grad

    orths = returned(schulz(own_raw, gram))

    grad_outs = []
    moment_outs = []
    new_outs = []
    for kind_index in range(kinds):
        grad_levels = []
        orth_levels = []
        for level_index in range(levels):
            job = kind_index * levels + level_index
            grad_here = grads[job][:, : widths[kind_index]]
            orth_here = orths[job][:, : widths[kind_index]]
            if flipped[kind_index]:
                grad_here = grad_here.T
                orth_here = orth_here.T
            grad_levels.append(grad_here)
            orth_levels.append(orth_here)
        grad_out = jnp.stack(grad_levels)
        grad_outs.append(grad_out)
        moment_outs.append(moment_decay * moments[kind_index] + grad_out)
        new_outs.append(weights[kind_index] - step_rates[kind_index] * jnp.stack(orth_levels))

    def placed(chunk_values):
        blocks = chunk_values.reshape(chunk, col_size, width_row).transpose(1, 0, 2)
        blocks = lax.all_to_all(blocks, "col", 0, 0)
        return swap_row_col(blocks.reshape(padded, width_row)[:tokens])

    tokens_all = tokens * col_size * dp_size
    norm_new = norm_params - norm_rate / math.sqrt(tokens_all) * norm_moment_new
    return (
        placed(stream),
        placed(upstream),
        *grad_outs,
        norm_grad,
        *moment_outs,
        norm_moment_new,
        *new_outs,
        norm_new,
    )


def solution(mesh):
    tokens_spec = P(("dp", "col"), "row")
    wide = P(None, "row", "col")
    tall = P(None, "col", "row")
    norms = P(None, None, "row")
    return jax.shard_map(
        on_device,
        mesh=mesh,
        in_specs=(tokens_spec, tokens_spec) + (wide, tall, wide, tall, norms) * 2,
        out_specs=(tokens_spec, tokens_spec) + (wide, tall, wide, tall, norms) * 3,
        check_vma=False,
    )
```

```python
import functools
import math

import jax
import jax.numpy as jnp
from jax import lax
from jax.experimental import pallas as pl
from jax.experimental.pallas import tpu as pltpu
from jax.sharding import PartitionSpec as P

HD = 64

norm_epsilon = 1e-06
moment_decay = 0.9
norm_rate = 0.05
step_rates = (1.7, 5.6, 2.0, 1.0)
schulz_first = 3.4445
schulz_second = -4.775
schulz_third = 2.0315
kinds = 4


def outer_grad(left_side, right_side):
    return lax.dot_general(
        left_side, right_side, (((0,), (0,)), ((), ())), preferred_element_type=jnp.float32
    )


def pad_rows(values, rows):
    return jnp.pad(values, ((0, rows - values.shape[0]), (0, 0)))


def pad_columns(values, columns):
    return jnp.pad(values, ((0, 0), (0, columns - values.shape[1])))


def norm_parts_of(values):
    average = jnp.mean(values, axis=1, keepdims=True)
    square = jnp.mean(values * values, axis=1, keepdims=True)
    inverse = lax.rsqrt(square - average * average + norm_epsilon)
    return ((values - average) * inverse, inverse)


def norm_backward(grad_out, plain, inverse, gain_row):
    scaled = grad_out * gain_row
    first = jnp.mean(scaled, axis=1, keepdims=True)
    second = jnp.mean(scaled * plain, axis=1, keepdims=True)
    return inverse * (scaled - first - plain * second)


def wide_dot(left_side, right_side, left_dim, right_dim):
    return lax.dot_general(
        left_side,
        right_side,
        (((left_dim,), (right_dim,)), ((), ())),
        preferred_element_type=jnp.float32,
    )


def in_vmem(count):
    return [pl.BlockSpec(memory_space=pltpu.VMEM)] * count


def kernel_call(body, inputs, outputs, scratch, flops, position=None):
    specs = in_vmem(len(inputs))
    operands = list(inputs)
    if position is not None:
        specs = [pl.BlockSpec(memory_space=pltpu.SMEM)] + specs
        operands = [position] + operands
    moved = sum(math.prod(o.shape) * o.dtype.itemsize for o in list(inputs) + list(outputs))
    return pl.pallas_call(
        body,
        out_shape=list(outputs),
        in_specs=specs,
        out_specs=in_vmem(len(outputs)),
        scratch_shapes=scratch,
        compiler_params=pltpu.CompilerParams(vmem_limit_bytes=40 * 1024 * 1024),
        cost_estimate=pl.CostEstimate(flops=flops, bytes_accessed=moved, transcendentals=0),
    )(*operands)


def put_chunks(position_ref, chunk_refs, whole_ref):
    chunk = chunk_refs[0].shape[0]
    for k, chunk_ref in enumerate(chunk_refs):
        start = pl.multiple_of((position_ref[0] ^ k) * chunk, 8)
        whole_ref[pl.ds(start, chunk), :] = chunk_ref[...].astype(jnp.float32)


def take_chunks(position_ref, whole_ref, chunk_refs):
    chunk = chunk_refs[0].shape[0]
    for k, chunk_ref in enumerate(chunk_refs):
        start = pl.multiple_of((position_ref[0] ^ k) * chunk, 8)
        chunk_ref[...] = whole_ref[pl.ds(start, chunk), :].astype(chunk_ref.dtype)


def keep_rows(values, tokens):
    rows = lax.broadcasted_iota(jnp.int32, values.shape, 0)
    return jnp.where(rows < tokens, values, jnp.zeros_like(values))


def head_probs(mixed, head, tokens):
    start = head * 3 * HD
    query = mixed[:, start : start + HD]
    key = mixed[:, start + HD : start + 2 * HD]
    value = mixed[:, start + 2 * HD : start + 3 * HD]
    scores = wide_dot(query, key, 1, 1) * HD ** (-0.5)
    columns = lax.broadcasted_iota(jnp.int32, scores.shape, 1)
    scores = jnp.where(columns < tokens, scores, -jnp.inf)
    exps = jnp.exp(scores - jnp.max(scores, axis=1, keepdims=True))
    probs = exps / jnp.sum(exps, axis=1, keepdims=True)
    return (query, key, value, probs)


def attend_kernel(tokens, heads, position, *refs):
    size = (len(refs) - 7) // 2
    chunks, (w_qkv, w_proj) = refs[:size], refs[size : size + 2]
    outs = refs[size + 2 : 2 * size + 2]
    mixed_out, normed_out, att_out, whole, att_all = refs[2 * size + 2 :]
    put_chunks(position, chunks, whole)
    normed = keep_rows(whole[...], tokens).astype(jnp.bfloat16)
    normed_out[...] = normed[: normed_out.shape[0]]
    mixed = wide_dot(normed, w_qkv[...], 1, 0).astype(jnp.bfloat16)
    mixed_out[...] = mixed
    for head in range(heads):
        _, _, value, probs = head_probs(mixed, head, tokens)
        att_all[:, head * HD : (head + 1) * HD] = wide_dot(probs.astype(jnp.bfloat16), value, 1, 0)
    attended = keep_rows(att_all[...], tokens).astype(jnp.bfloat16)
    att_out[...] = jnp.zeros_like(att_out)
    att_out[:, : heads * HD] = attended[: att_out.shape[0]]
    whole[...] = wide_dot(attended, w_proj[...], 1, 1)
    take_chunks(position, whole, outs)


def attend_back_kernel(tokens, heads, position, *refs):
    size = (len(refs) - 7) // 2
    chunks, (mixed_ref, w_qkv, w_proj) = refs[:size], refs[size : size + 3]
    outs = refs[size + 3 : 2 * size + 3]
    mixed_grad_out, back_out, whole, mixed_grad = refs[2 * size + 3 :]
    put_chunks(position, chunks, whole)
    back = whole[...].astype(jnp.bfloat16)
    back_out[...] = back[: back_out.shape[0]]
    att_grad = wide_dot(back, w_proj[...], 1, 0).astype(jnp.bfloat16)
    mixed = mixed_ref[...]
    scaling = HD ** (-0.5)
    for head in range(heads):
        query, key, value, probs = head_probs(mixed, head, tokens)
        grad = att_grad[:, head * HD : (head + 1) * HD]
        probs_grad = wide_dot(grad, value, 1, 1)
        inner = jnp.sum(probs * probs_grad, axis=1, keepdims=True)
        scores_grad = (probs * (probs_grad - inner)).astype(jnp.bfloat16)
        start = head * 3 * HD
        mixed_grad[:, start : start + HD] = wide_dot(scores_grad, key, 1, 0) * scaling
        mixed_grad[:, start + HD : start + 2 * HD] = wide_dot(scores_grad, query, 0, 0) * scaling
        mixed_grad[:, start + 2 * HD : start + 3 * HD] = wide_dot(
            probs.astype(jnp.bfloat16), grad, 0, 0
        )
    grads = mixed_grad[...].astype(jnp.bfloat16)
    mixed_grad_out[...] = jnp.zeros_like(mixed_grad_out)
    mixed_grad_out[:, : grads.shape[1]] = grads[: mixed_grad_out.shape[0]]
    whole[...] = wide_dot(grads, w_qkv[...], 1, 1)
    take_chunks(position, whole, outs)


def norm_kernel(level_index, first_row, size, *refs):
    parts, (stream_ref, norms) = refs[:size], refs[size : size + 2]
    stream_out, normed_out = refs[size + 2 :]
    stream = stream_ref[...]
    for part in parts:
        stream = stream + part[...].astype(jnp.float32)
    stream_out[...] = stream
    plain, _ = norm_parts_of(stream)
    gain = norms[level_index, first_row : first_row + 1, :]
    bias = norms[level_index, first_row + 1 : first_row + 2, :]
    normed_out[...] = (plain * gain + bias).astype(jnp.bfloat16)


def norm_back_kernel(level_index, first_row, size, *refs):
    parts, (stream_ref, upstream_ref, norms) = refs[:size], refs[size : size + 3]
    upstream_out, low_out, sums_out = refs[size + 3 :]
    grad = parts[0][...].astype(jnp.float32)
    for part in parts[1:]:
        grad = grad + part[...].astype(jnp.float32)
    plain, inverse = norm_parts_of(stream_ref[...])
    gain = norms[level_index, first_row : first_row + 1, :]
    upstream = upstream_ref[...] + norm_backward(grad, plain, inverse, gain)
    upstream_out[...] = upstream
    low_out[...] = upstream.astype(jnp.bfloat16)
    sums_out[0:1, :] = jnp.sum(grad * plain, axis=0, keepdims=True)
    sums_out[1:2, :] = jnp.sum(grad, axis=0, keepdims=True)


def first_kernel(tokens, position, blocks, norms, *refs):
    outs, stream_out, whole = refs[:-2], refs[-2], refs[-1]
    size, _, width = blocks.shape
    whole[...] = jnp.zeros_like(whole)
    for i in range(size):
        whole[0:tokens, i * width : (i + 1) * width] = blocks[i].astype(jnp.float32)
    chunk = stream_out.shape[0]
    start = pl.multiple_of(position[0] * chunk, 8)
    stream_out[...] = whole[pl.ds(start, chunk), :]
    plain, _ = norm_parts_of(whole[...])
    whole[...] = plain * norms[0, 0:1, :] + norms[0, 1:2, :]
    take_chunks(position, whole, outs)


def mlp_kernel(tokens, position, *refs):
    size = (len(refs) - 6) // 2
    chunks, (w_up, w_down) = refs[:size], refs[size : size + 2]
    outs = refs[size + 2 : 2 * size + 2]
    slope_out, normed_out, act_out, whole = refs[2 * size + 2 :]
    put_chunks(position, chunks, whole)
    normed = keep_rows(whole[...], tokens).astype(jnp.bfloat16)
    normed_out[...] = normed[: normed_out.shape[0]]
    hidden = wide_dot(normed, w_up[...], 1, 0)
    below = 0.5 + 0.5 * lax.erf(hidden * math.sqrt(0.5))
    slope_out[...] = below + hidden * jnp.exp(-0.5 * hidden * hidden) * (
        1.0 / math.sqrt(2.0 * math.pi)
    )
    activated = keep_rows(hidden * below, tokens).astype(jnp.bfloat16)
    act_out[...] = activated[: act_out.shape[0]]
    whole[...] = wide_dot(activated, w_down[...], 1, 1)
    take_chunks(position, whole, outs)


def mlp_back_kernel(position, *refs):
    size = (len(refs) - 6) // 2
    chunks, (slope, w_up, w_down) = refs[:size], refs[size : size + 3]
    outs = refs[size + 3 : 2 * size + 3]
    hidden_grad_out, back_out, whole = refs[2 * size + 3 :]
    put_chunks(position, chunks, whole)
    back = whole[...].astype(jnp.bfloat16)
    back_out[...] = back[: back_out.shape[0]]
    hidden_grad = (wide_dot(back, w_down[...], 1, 0) * slope[...]).astype(jnp.bfloat16)
    hidden_grad_out[...] = hidden_grad[: hidden_grad_out.shape[0]]
    whole[...] = wide_dot(hidden_grad, w_up[...], 1, 1)
    take_chunks(position, whole, outs)


def swap_row_col(values):
    size = lax.axis_size("row")
    pairs = [(i * size + j, j * size + i) for i in range(size) for j in range(size)]
    return lax.ppermute(values, ("row", "col"), pairs)


def from_partner(values, step, axes=("dp", "row"), wanted=None):
    count = math.prod(lax.axis_size(a) for a in axes)
    pairs = [(i, i ^ step) for i in range(count) if wanted is None or wanted(i ^ step)]
    return lax.ppermute(values, axes, pairs)


def pick(stacked, index):
    return lax.dynamic_index_in_dim(stacked, index, 0, keepdims=False)


def placed_blocks(blocks, places):
    result = jnp.zeros((len(blocks),) + blocks[0].shape, blocks[0].dtype)
    for block, place in zip(blocks, places):
        result = lax.dynamic_update_index_in_dim(result, block, place, 0)
    return result


def gather_by_pairs(values, axis):
    step = lax.axis_size(axis) // 2
    me = lax.axis_index(axis)
    blocks, places = [values], [me]
    while step:
        sent = blocks[0][None] if len(blocks) == 1 else jnp.stack(blocks)
        received = from_partner(sent, step, (axis,))
        blocks = blocks + [received[i] for i in range(len(blocks))]
        places = places + [p ^ step for p in places]
        step //= 2
    return placed_blocks(blocks, places)


def sum_by_pairs(values, axis):
    step = 1
    while step < lax.axis_size(axis):
        values = values + from_partner(values, step, (axis,))
        step *= 2
    return values


def to_all(block, axis):
    size = lax.axis_size(axis)
    return lax.all_to_all(jnp.broadcast_to(block[None], (size,) + block.shape), axis, 0, 0)


def to_partners(chunk):
    size = lax.axis_size("col")
    return [chunk] + [from_partner(chunk, k, ("col",)) for k in range(1, size)]


def swap_parts(parts):
    return [parts[0]] + [from_partner(parts[k], k, ("col",)) for k in range(1, len(parts))]


def gram_strips(raw):
    size = lax.axis_size("col")
    third = raw.shape[0] // 3
    strips = [
        lax.dot_general(
            raw[i * third : (i + 1) * third],
            raw[i * third :],
            (((1,), (1,)), ((), ())),
            precision=lax.Precision.HIGH,
            preferred_element_type=jnp.float32,
        )
        for i in range(3)
    ]
    packed = jnp.concatenate(strips, axis=1)
    blocks = lax.all_to_all(packed.reshape(size, third // size, -1), "col", 0, 0)
    return to_all(jnp.sum(blocks, axis=0), "col").reshape(third, -1)


def halves(values):
    high = values.astype(jnp.bfloat16)
    return (high, (values - high.astype(jnp.float32)).astype(jnp.bfloat16))


def put_halves(refs, rows, columns, values):
    for ref, half in zip(refs, halves(values)):
        ref[rows, columns] = half


def dot_halves(left, rows, right, columns):
    left_high, left_low = left[0][rows, :], left[1][rows, :]
    right_high, right_low = right[0][:, columns], right[1][:, columns]
    return (
        wide_dot(left_high, right_high, 1, 0)
        + wide_dot(left_high, right_low, 1, 0)
        + wide_dot(left_low, right_high, 1, 0)
    )


def schulz_kernel(sweeps, packed, raw, out, gram, half, current, *pairs):
    gram_pair, square_pair, half_pair, current_pair = [pairs[i : i + 2] for i in range(0, 8, 2)]
    height = raw.shape[0]
    third = height // 3
    bands = [slice(i * third, (i + 1) * third) for i in range(3)]
    tails = [slice(i * third, height) for i in range(3)]
    everything = slice(0, height)

    def put_symmetric(pair, i, values):
        put_halves(pair, bands[i], tails[i], values)
        for j in range(i + 1, 3):
            block = values[:, (j - i) * third : (j - i + 1) * third]
            put_halves(pair, bands[j], bands[i], block.T)

    total = jnp.zeros((1, 1), jnp.float32)
    start = 0
    for i in range(3):
        strip = packed[:, start : start + height - i * third]
        start += height - i * third
        gram[bands[i], tails[i]] = strip
        rows = lax.broadcasted_iota(jnp.int32, (third, third), 0)
        columns = lax.broadcasted_iota(jnp.int32, (third, third), 1)
        diagonal = jnp.where(rows == columns, strip[:, :third], 0.0)
        total = total + jnp.sum(jnp.sum(diagonal, axis=1, keepdims=True), axis=0, keepdims=True)
    scale = 1.0 / (jnp.sqrt(total) + 1e-07)
    for i in range(3):
        values = gram[bands[i], tails[i]] * (scale * scale)
        gram[bands[i], tails[i]] = values
        put_symmetric(gram_pair, i, values)
        values = raw[bands[i], :] * scale
        current[bands[i], :] = values
        put_halves(current_pair, bands[i], everything, values)

    def sweep(index, carry):
        for i in range(3):
            product = dot_halves(gram_pair, bands[i], gram_pair, tails[i])
            square = schulz_second * gram[bands[i], tails[i]] + schulz_third * product
            put_symmetric(square_pair, i, square)
        for i in range(3):
            product = dot_halves(square_pair, bands[i], current_pair, everything)
            current[bands[i], :] = schulz_first * current[bands[i], :] + product

        @pl.when(index < sweeps - 1)
        def _():
            for i in range(3):
                put_halves(current_pair, bands[i], everything, current[bands[i], :])
                product = dot_halves(square_pair, bands[i], gram_pair, tails[i])
                values = schulz_first * gram[bands[i], tails[i]] + product
                half[bands[i], tails[i]] = values
                put_symmetric(half_pair, i, values)
            for i in range(3):
                product = dot_halves(square_pair, bands[i], half_pair, tails[i])
                values = schulz_first * half[bands[i], tails[i]] + product
                gram[bands[i], tails[i]] = values
                put_symmetric(gram_pair, i, values)

        return carry

    lax.fori_loop(0, sweeps, sweep, 0)
    out[...] = current[...].astype(out.dtype)


def schulz(raw, packed):
    height, width = raw.shape
    square_shape = (height, height)
    whole = [pltpu.VMEM(square_shape, jnp.float32)] * 2 + [pltpu.VMEM(raw.shape, jnp.float32)]
    pairs = [pltpu.VMEM(square_shape, jnp.bfloat16)] * 6 + [pltpu.VMEM(raw.shape, jnp.bfloat16)] * 2
    return kernel_call(
        functools.partial(schulz_kernel, 5),
        [packed, raw],
        [jax.ShapeDtypeStruct(raw.shape, jnp.bfloat16)],
        whole + pairs,
        2 * 3 * 14 * height * height * width,
    )[0]


def on_device(
    residual_in,
    cotangent,
    qkv_weight,
    proj_weight,
    up_weight,
    down_weight,
    norm_params,
    qkv_moment,
    proj_moment,
    up_moment,
    down_moment,
    norm_moment,
):
    tokens, width_row = residual_in.shape
    row_size = lax.axis_size("row")
    col_size = lax.axis_size("col")
    dp_size = lax.axis_size("dp")
    model_width = width_row * row_size
    levels = qkv_weight.shape[0]
    jobs = levels * kinds
    chunk = -(-tokens // (8 * col_size)) * 8
    padded = chunk * col_size
    sent_rows = -(-tokens // 16) * 16
    me = (lax.axis_index("dp") * row_size + lax.axis_index("row")) % jobs
    my_row = lax.axis_index("row")
    my_chunk = lax.axis_index("col") * chunk

    weights = (qkv_weight, proj_weight, up_weight, down_weight)
    moments = (qkv_moment, proj_moment, up_moment, down_moment)
    flipped = (False, True, False, True)

    def upright(array, kind_index, level_index):
        block = array[level_index]
        return block.T if flipped[kind_index] else block

    widths = [
        w.shape[1] if flipped[k] else w.shape[2] for k, w in enumerate(weights)
    ]
    widest = max(widths)

    def own_weights(level_index, which):
        parts = [upright(weights[k], k, level_index).astype(jnp.bfloat16) for k in which]
        return jnp.concatenate(parts, axis=1)

    def gathered_weights(own, which):
        whole = gather_by_pairs(own, "row")
        whole = whole.reshape(model_width, -1)
        result = []
        start = 0
        for k in which:
            result.append(whole[:, start : start + widths[k]])
            start += widths[k]
        return result

    def features_first(blocks):
        return blocks.transpose(1, 0, 2).reshape(blocks.shape[1], model_width)

    all_norms = gather_by_pairs(norm_params, "row")
    all_norms = all_norms.transpose(1, 2, 0, 3).reshape(levels, kinds, model_width)
    image_blocks = to_all(swap_row_col(residual_in), "col")
    position = lax.axis_index("col").astype(jnp.int32).reshape(1)
    heads = widths[0] // (3 * HD)

    def shaped(rows, columns, kind):
        return jax.ShapeDtypeStruct((rows, columns), kind)

    low_chunk = shaped(chunk, model_width, jnp.bfloat16)
    full_chunk = shaped(chunk, model_width, jnp.float32)
    low_chunks = [low_chunk] * col_size
    sent = shaped(sent_rows, widest, jnp.bfloat16)
    sent_model = shaped(sent_rows, model_width, jnp.bfloat16)
    whole_scratch = pltpu.VMEM((padded, model_width), jnp.float32)
    attention_flops = 2 * padded * (
        model_width * (widths[0] + widths[1]) + 2 * padded * widths[1]
    )
    perceptron_flops = 2 * padded * model_width * (widths[2] + widths[3])
    chunk_flops = 20 * chunk * model_width

    def norm_step(parts, stream, level_index, first_row):
        return kernel_call(
            functools.partial(norm_kernel, level_index, first_row, len(parts)),
            [*parts, stream, all_norms],
            [full_chunk, low_chunk],
            [],
            chunk_flops,
        )

    def norm_back_step(parts, stream, upstream, level_index, first_row):
        return kernel_call(
            functools.partial(norm_back_kernel, level_index, first_row, len(parts)),
            [*parts, stream, upstream, all_norms],
            [full_chunk, low_chunk, shaped(2, model_width, jnp.float32)],
            [],
            chunk_flops,
        )

    *chunks, stream = kernel_call(
        functools.partial(first_kernel, tokens),
        [image_blocks, all_norms],
        low_chunks + [full_chunk],
        [whole_scratch],
        20 * padded * model_width,
        position,
    )
    groups = ((0, 1), (2, 3))

    def weights_of(own_groups):
        return sum([gathered_weights(own, which) for own, which in zip(own_groups, groups)], [])

    own_groups = [[own_weights(i, which) for which in groups] for i in range(levels)]
    weight_sets = [weights_of(own_groups[0])] + [None] * (levels - 1)
    chunks, own_groups[1:] = lax.optimization_barrier((chunks, own_groups[1:]))
    for level_index in range(1, levels):
        weight_sets[level_index] = weights_of(own_groups[level_index])
    saved = []
    early = [None] * levels
    for level_index in range(levels):
        weight_qkv, weight_proj, weight_up, weight_down = weight_sets[level_index]
        stream_one = stream
        *parts, mixed, normed_one, attended = kernel_call(
            functools.partial(attend_kernel, tokens, heads),
            [*chunks, weight_qkv, weight_proj],
            low_chunks + [shaped(padded, widths[0], jnp.bfloat16), sent_model, sent],
            [whole_scratch, pltpu.VMEM((padded, widths[1]), jnp.float32)],
            attention_flops,
            position,
        )
        stream_two, normed = norm_step(swap_parts(parts), stream, level_index, 2)
        chunks = to_partners(normed)
        *parts, slope, normed_two, activated = kernel_call(
            functools.partial(mlp_kernel, tokens),
            [*chunks, weight_up, weight_down],
            low_chunks + [shaped(padded, widths[2], jnp.float32), sent_model, sent],
            [whole_scratch],
            perceptron_flops,
            position,
        )
        parts = swap_parts(parts)
        early[level_index] = (normed_one, attended, normed_two, activated)
        if level_index < levels - 1:
            stream, normed = norm_step(parts, stream_two, level_index + 1, 0)
            if level_index == 0:
                normed, late_me, cotangent = lax.optimization_barrier((normed, me, cotangent))
            chunks = to_partners(normed)
        else:
            stream = stream_two
            for part in parts:
                stream = stream + part.astype(jnp.float32)
        saved.append((stream_one, stream_two, mixed, slope))

    def send_level(parts, level_index):
        stack = jnp.stack(parts)
        received = [pick(stack, me // levels)]
        for step in range(1, jobs):
            received.append(
                from_partner(
                    pick(stack, (me ^ step) // levels),
                    step,
                    wanted=lambda i: i % levels == level_index,
                )
            )
        return received

    upper = (late_me // row_size) % 2 == 1
    half = jobs // 2
    near_moments = []
    for j in range(half):
        low_job, high_job = [
            pad_columns(upright(moments[i // levels], i // levels, i % levels), widest)
            for i in (j, j + half)
        ]
        near_moments.append(jnp.where(upper, high_job, low_job))
    stacked_moment = jnp.stack(near_moments)
    moment_parts = [pick(stacked_moment, me % half)]
    for step in range(1, row_size):
        moment_parts.append(from_partner(pick(stacked_moment, (me ^ step) % half), step))
    own_moment = placed_blocks(moment_parts, [my_row ^ i for i in range(row_size)])
    own_moment = own_moment.reshape(model_width, widest)

    cotangent_blocks = pad_rows(swap_row_col(cotangent), padded)
    cotangent_blocks = cotangent_blocks.reshape(col_size, chunk, width_row)
    upstream = features_first(lax.all_to_all(cotangent_blocks, "col", 0, 0))

    early = [send_level(early[i], i) for i in range(levels)]
    upstream, own_moment, early[0] = lax.optimization_barrier((upstream, own_moment, early[0]))
    late = [None] * levels
    norm_sums = [None] * levels
    back_low = upstream.astype(jnp.bfloat16)
    for level_index in reversed(range(levels)):
        weight_qkv, weight_proj, weight_up, weight_down = weight_sets[level_index]
        stream_one, stream_two, mixed, slope = saved[level_index]
        *parts, hidden_grad, back_two = kernel_call(
            mlp_back_kernel,
            [*to_partners(back_low), slope, weight_up, weight_down],
            low_chunks + [sent, sent_model],
            [whole_scratch],
            perceptron_flops,
            position,
        )
        upstream, back_low, sums_two = norm_back_step(
            swap_parts(parts), stream_two, upstream, level_index, 2
        )
        if level_index < levels - 1:
            back_low, late[level_index + 1] = lax.optimization_barrier(
                (back_low, late[level_index + 1])
            )
        *parts, mixed_grad, back_one = kernel_call(
            functools.partial(attend_back_kernel, tokens, heads),
            [*to_partners(back_low), mixed, weight_qkv, weight_proj],
            low_chunks + [sent, sent_model],
            [whole_scratch, pltpu.VMEM((padded, widths[0]), jnp.float32)],
            3 * attention_flops,
            position,
        )
        late[level_index] = send_level(
            (mixed_grad, back_one, hidden_grad, back_two), level_index
        )
        if level_index:
            upstream, back_low, sums_one = norm_back_step(
                swap_parts(parts), stream_one, upstream, level_index, 0
            )
            norm_sums[level_index] = jnp.concatenate([sums_one, sums_two])
            back_low, early[level_index] = lax.optimization_barrier((back_low, early[level_index]))

    def own_level(sets):
        result = jnp.concatenate(sets[0], axis=0)
        for level_index in range(1, levels):
            other = jnp.concatenate(sets[level_index], axis=0)
            result = jnp.where(me % levels == level_index, other, result)
        return result

    early_all = own_level(early)
    late_all = own_level(late)
    turned = (me // levels) % 2 == 1
    model_side = jnp.where(turned, late_all, early_all)
    hidden_side = jnp.where(turned, early_all, late_all)
    own_grad = outer_grad(model_side, hidden_side)
    step = jobs // row_size
    while step < dp_size:
        pairs = [(i, i ^ step) for i in range(dp_size)]
        own_grad = own_grad + lax.ppermute(own_grad, "dp", pairs)
        step *= 2

    def returned(whole):
        blocks = whole.astype(jnp.bfloat16).reshape(row_size, width_row, widest)
        received = [pick(blocks, my_row)]
        for step in range(1, jobs):
            received.append(from_partner(pick(blocks, (me ^ step) % row_size), step))
        received = placed_blocks(received, [me ^ j for j in range(jobs)])
        return [received[j].astype(jnp.float32) for j in range(jobs)]

    own_raw = moment_decay * own_moment + own_grad
    gram, own_grad, stream, parts = lax.optimization_barrier(
        (gram_strips(own_raw), own_grad, stream, parts)
    )
    upstream, _, sums_one = norm_back_step(swap_parts(parts), stream_one, upstream, 0, 0)
    norm_sums[0] = jnp.concatenate([sums_one, sums_two])
    grads = returned(own_grad)
    norm_whole = jnp.stack(norm_sums)
    for axis in ("row", "col", "dp"):
        norm_whole = sum_by_pairs(norm_whole, axis)
    norm_grad = lax.dynamic_slice_in_dim(norm_whole, my_row * width_row, width_row, 2)
    norm_moment_new = moment_decay * norm_moment + norm_grad

    orths = returned(schulz(own_raw, gram))

    grad_outs = []
    moment_outs = []
    new_outs = []
    for kind_index in range(kinds):
        grad_levels = []
        orth_levels = []
        for level_index in range(levels):
            job = kind_index * levels + level_index
            grad_here = grads[job][:, : widths[kind_index]]
            orth_here = orths[job][:, : widths[kind_index]]
            if flipped[kind_index]:
                grad_here = grad_here.T
                orth_here = orth_here.T
            grad_levels.append(grad_here)
            orth_levels.append(orth_here)
        grad_out = jnp.stack(grad_levels)
        grad_outs.append(grad_out)
        moment_outs.append(moment_decay * moments[kind_index] + grad_out)
        new_outs.append(weights[kind_index] - step_rates[kind_index] * jnp.stack(orth_levels))

    def placed(chunk_values):
        blocks = chunk_values.reshape(chunk, col_size, width_row).transpose(1, 0, 2)
        blocks = lax.all_to_all(blocks, "col", 0, 0)
        return swap_row_col(blocks.reshape(padded, width_row)[:tokens])

    tokens_all = tokens * col_size * dp_size
    norm_new = norm_params - norm_rate / math.sqrt(tokens_all) * norm_moment_new
    return (
        placed(stream),
        placed(upstream),
        *grad_outs,
        norm_grad,
        *moment_outs,
        norm_moment_new,
        *new_outs,
        norm_new,
    )


def solution(mesh):
    tokens_spec = P(("dp", "col"), "row")
    wide = P(None, "row", "col")
    tall = P(None, "col", "row")
    norms = P(None, None, "row")
    return jax.shard_map(
        on_device,
        mesh=mesh,
        in_specs=(tokens_spec, tokens_spec) + (wide, tall, wide, tall, norms) * 2,
        out_specs=(tokens_spec, tokens_spec) + (wide, tall, wide, tall, norms) * 3,
        check_vma=False,
    )
```

```python
import functools
import math

import jax
import jax.numpy as jnp
from jax import lax
from jax.experimental import pallas as pl
from jax.experimental.pallas import tpu as pltpu
from jax.sharding import PartitionSpec as P

HD = 64

norm_epsilon = 1e-06
moment_decay = 0.9
norm_rate = 0.05
step_rates = (1.7, 5.6, 2.0, 1.0)
schulz_first = 3.4445
schulz_second = -4.775
schulz_third = 2.0315
kinds = 4


def outer_grad(left_side, right_side):
    return lax.dot_general(
        left_side, right_side, (((0,), (0,)), ((), ())), preferred_element_type=jnp.float32
    )


def pad_rows(values, rows):
    return jnp.pad(values, ((0, rows - values.shape[0]), (0, 0)))


def pad_columns(values, columns):
    return jnp.pad(values, ((0, 0), (0, columns - values.shape[1])))


def norm_parts_of(values):
    average = jnp.mean(values, axis=1, keepdims=True)
    square = jnp.mean(values * values, axis=1, keepdims=True)
    inverse = lax.rsqrt(square - average * average + norm_epsilon)
    return ((values - average) * inverse, inverse)


def norm_backward(grad_out, plain, inverse, gain_row):
    scaled = grad_out * gain_row
    first = jnp.mean(scaled, axis=1, keepdims=True)
    second = jnp.mean(scaled * plain, axis=1, keepdims=True)
    return inverse * (scaled - first - plain * second)


def wide_dot(left_side, right_side, left_dim, right_dim):
    return lax.dot_general(
        left_side,
        right_side,
        (((left_dim,), (right_dim,)), ((), ())),
        preferred_element_type=jnp.float32,
    )


def in_vmem(count):
    return [pl.BlockSpec(memory_space=pltpu.VMEM)] * count


def kernel_call(body, inputs, outputs, scratch, flops, position=None):
    specs = in_vmem(len(inputs))
    operands = list(inputs)
    if position is not None:
        specs = [pl.BlockSpec(memory_space=pltpu.SMEM)] + specs
        operands = [position] + operands
    moved = sum(math.prod(o.shape) * o.dtype.itemsize for o in list(inputs) + list(outputs))
    return pl.pallas_call(
        body,
        out_shape=list(outputs),
        in_specs=specs,
        out_specs=in_vmem(len(outputs)),
        scratch_shapes=scratch,
        compiler_params=pltpu.CompilerParams(vmem_limit_bytes=40 * 1024 * 1024),
        cost_estimate=pl.CostEstimate(flops=flops, bytes_accessed=moved, transcendentals=0),
    )(*operands)


def put_chunks(position_ref, chunk_refs, whole_ref):
    chunk = chunk_refs[0].shape[0]
    for k, chunk_ref in enumerate(chunk_refs):
        start = pl.multiple_of((position_ref[0] ^ k) * chunk, 8)
        whole_ref[pl.ds(start, chunk), :] = chunk_ref[...].astype(jnp.float32)


def take_chunks(position_ref, whole_ref, chunk_refs):
    chunk = chunk_refs[0].shape[0]
    for k, chunk_ref in enumerate(chunk_refs):
        start = pl.multiple_of((position_ref[0] ^ k) * chunk, 8)
        chunk_ref[...] = whole_ref[pl.ds(start, chunk), :].astype(chunk_ref.dtype)


def keep_rows(values, tokens):
    rows = lax.broadcasted_iota(jnp.int32, values.shape, 0)
    return jnp.where(rows < tokens, values, jnp.zeros_like(values))


def head_probs(mixed, head, tokens):
    start = head * 3 * HD
    query = mixed[:, start : start + HD]
    key = mixed[:, start + HD : start + 2 * HD]
    value = mixed[:, start + 2 * HD : start + 3 * HD]
    scores = wide_dot(query, key, 1, 1) * HD ** (-0.5)
    columns = lax.broadcasted_iota(jnp.int32, scores.shape, 1)
    scores = jnp.where(columns < tokens, scores, -jnp.inf)
    exps = jnp.exp(scores - jnp.max(scores, axis=1, keepdims=True))
    probs = exps / jnp.sum(exps, axis=1, keepdims=True)
    return (query, key, value, probs)


def attend_kernel(tokens, heads, position, *refs):
    size = (len(refs) - 7) // 2
    chunks, (w_qkv, w_proj) = refs[:size], refs[size : size + 2]
    outs = refs[size + 2 : 2 * size + 2]
    mixed_out, normed_out, att_out, whole, att_all = refs[2 * size + 2 :]
    put_chunks(position, chunks, whole)
    normed = keep_rows(whole[...], tokens).astype(jnp.bfloat16)
    normed_out[...] = normed[: normed_out.shape[0]]
    mixed = wide_dot(normed, w_qkv[...], 1, 0).astype(jnp.bfloat16)
    mixed_out[...] = mixed
    for head in range(heads):
        _, _, value, probs = head_probs(mixed, head, tokens)
        att_all[:, head * HD : (head + 1) * HD] = wide_dot(probs.astype(jnp.bfloat16), value, 1, 0)
    attended = keep_rows(att_all[...], tokens).astype(jnp.bfloat16)
    att_out[...] = jnp.zeros_like(att_out)
    att_out[:, : heads * HD] = attended[: att_out.shape[0]]
    whole[...] = wide_dot(attended, w_proj[...], 1, 1)
    take_chunks(position, whole, outs)


def attend_back_kernel(tokens, heads, position, *refs):
    size = (len(refs) - 7) // 2
    chunks, (mixed_ref, w_qkv, w_proj) = refs[:size], refs[size : size + 3]
    outs = refs[size + 3 : 2 * size + 3]
    mixed_grad_out, back_out, whole, mixed_grad = refs[2 * size + 3 :]
    put_chunks(position, chunks, whole)
    back = whole[...].astype(jnp.bfloat16)
    back_out[...] = back[: back_out.shape[0]]
    att_grad = wide_dot(back, w_proj[...], 1, 0).astype(jnp.bfloat16)
    mixed = mixed_ref[...]
    scaling = HD ** (-0.5)
    for head in range(heads):
        query, key, value, probs = head_probs(mixed, head, tokens)
        grad = att_grad[:, head * HD : (head + 1) * HD]
        probs_grad = wide_dot(grad, value, 1, 1)
        inner = jnp.sum(probs * probs_grad, axis=1, keepdims=True)
        scores_grad = (probs * (probs_grad - inner)).astype(jnp.bfloat16)
        start = head * 3 * HD
        mixed_grad[:, start : start + HD] = wide_dot(scores_grad, key, 1, 0) * scaling
        mixed_grad[:, start + HD : start + 2 * HD] = wide_dot(scores_grad, query, 0, 0) * scaling
        mixed_grad[:, start + 2 * HD : start + 3 * HD] = wide_dot(
            probs.astype(jnp.bfloat16), grad, 0, 0
        )
    grads = mixed_grad[...].astype(jnp.bfloat16)
    mixed_grad_out[...] = jnp.zeros_like(mixed_grad_out)
    mixed_grad_out[:, : grads.shape[1]] = grads[: mixed_grad_out.shape[0]]
    whole[...] = wide_dot(grads, w_qkv[...], 1, 1)
    take_chunks(position, whole, outs)


def norm_kernel(level_index, first_row, size, *refs):
    parts, (stream_ref, norms) = refs[:size], refs[size : size + 2]
    stream_out, normed_out = refs[size + 2 :]
    stream = stream_ref[...]
    for part in parts:
        stream = stream + part[...].astype(jnp.float32)
    stream_out[...] = stream
    plain, _ = norm_parts_of(stream)
    gain = norms[level_index, first_row : first_row + 1, :]
    bias = norms[level_index, first_row + 1 : first_row + 2, :]
    normed_out[...] = (plain * gain + bias).astype(jnp.bfloat16)


def norm_back_kernel(level_index, first_row, size, *refs):
    parts, (stream_ref, upstream_ref, norms) = refs[:size], refs[size : size + 3]
    upstream_out, low_out, sums_out = refs[size + 3 :]
    grad = parts[0][...].astype(jnp.float32)
    for part in parts[1:]:
        grad = grad + part[...].astype(jnp.float32)
    plain, inverse = norm_parts_of(stream_ref[...])
    gain = norms[level_index, first_row : first_row + 1, :]
    upstream = upstream_ref[...] + norm_backward(grad, plain, inverse, gain)
    upstream_out[...] = upstream
    low_out[...] = upstream.astype(jnp.bfloat16)
    sums_out[0:1, :] = jnp.sum(grad * plain, axis=0, keepdims=True)
    sums_out[1:2, :] = jnp.sum(grad, axis=0, keepdims=True)


def first_kernel(tokens, position, blocks, norms, *refs):
    outs, stream_out, whole = refs[:-2], refs[-2], refs[-1]
    size, _, width = blocks.shape
    whole[...] = jnp.zeros_like(whole)
    for i in range(size):
        whole[0:tokens, i * width : (i + 1) * width] = blocks[i].astype(jnp.float32)
    chunk = stream_out.shape[0]
    start = pl.multiple_of(position[0] * chunk, 8)
    stream_out[...] = whole[pl.ds(start, chunk), :]
    plain, _ = norm_parts_of(whole[...])
    whole[...] = plain * norms[0, 0:1, :] + norms[0, 1:2, :]
    take_chunks(position, whole, outs)


def mlp_kernel(tokens, position, *refs):
    size = (len(refs) - 6) // 2
    chunks, (w_up, w_down) = refs[:size], refs[size : size + 2]
    outs = refs[size + 2 : 2 * size + 2]
    slope_out, normed_out, act_out, whole = refs[2 * size + 2 :]
    put_chunks(position, chunks, whole)
    normed = keep_rows(whole[...], tokens).astype(jnp.bfloat16)
    normed_out[...] = normed[: normed_out.shape[0]]
    hidden = wide_dot(normed, w_up[...], 1, 0)
    below = 0.5 + 0.5 * lax.erf(hidden * math.sqrt(0.5))
    slope_out[...] = below + hidden * jnp.exp(-0.5 * hidden * hidden) * (
        1.0 / math.sqrt(2.0 * math.pi)
    )
    activated = keep_rows(hidden * below, tokens).astype(jnp.bfloat16)
    act_out[...] = activated[: act_out.shape[0]]
    whole[...] = wide_dot(activated, w_down[...], 1, 1)
    take_chunks(position, whole, outs)


def mlp_back_kernel(position, *refs):
    size = (len(refs) - 6) // 2
    chunks, (slope, w_up, w_down) = refs[:size], refs[size : size + 3]
    outs = refs[size + 3 : 2 * size + 3]
    hidden_grad_out, back_out, whole = refs[2 * size + 3 :]
    put_chunks(position, chunks, whole)
    back = whole[...].astype(jnp.bfloat16)
    back_out[...] = back[: back_out.shape[0]]
    hidden_grad = (wide_dot(back, w_down[...], 1, 0) * slope[...]).astype(jnp.bfloat16)
    hidden_grad_out[...] = hidden_grad[: hidden_grad_out.shape[0]]
    whole[...] = wide_dot(hidden_grad, w_up[...], 1, 1)
    take_chunks(position, whole, outs)


def swap_row_col(values):
    size = lax.axis_size("row")
    pairs = [(i * size + j, j * size + i) for i in range(size) for j in range(size)]
    return lax.ppermute(values, ("row", "col"), pairs)


def from_partner(values, step, axes=("dp", "row"), wanted=None):
    count = math.prod(lax.axis_size(a) for a in axes)
    pairs = [(i, i ^ step) for i in range(count) if wanted is None or wanted(i ^ step)]
    return lax.ppermute(values, axes, pairs)


def pick(stacked, index):
    return lax.dynamic_index_in_dim(stacked, index, 0, keepdims=False)


def placed_blocks(blocks, places):
    result = jnp.zeros((len(blocks),) + blocks[0].shape, blocks[0].dtype)
    for block, place in zip(blocks, places):
        result = lax.dynamic_update_index_in_dim(result, block, place, 0)
    return result


def gather_by_pairs(values, axis):
    step = lax.axis_size(axis) // 2
    me = lax.axis_index(axis)
    blocks, places = [values], [me]
    while step:
        sent = blocks[0][None] if len(blocks) == 1 else jnp.stack(blocks)
        received = from_partner(sent, step, (axis,))
        blocks = blocks + [received[i] for i in range(len(blocks))]
        places = places + [p ^ step for p in places]
        step //= 2
    return placed_blocks(blocks, places)


def sum_by_pairs(values, axis):
    step = 1
    while step < lax.axis_size(axis):
        values = values + from_partner(values, step, (axis,))
        step *= 2
    return values


def to_all(block, axis):
    size = lax.axis_size(axis)
    return lax.all_to_all(jnp.broadcast_to(block[None], (size,) + block.shape), axis, 0, 0)


def to_partners(chunk):
    size = lax.axis_size("col")
    return [chunk] + [from_partner(chunk, k, ("col",)) for k in range(1, size)]


def swap_parts(parts):
    return [parts[0]] + [from_partner(parts[k], k, ("col",)) for k in range(1, len(parts))]


def gram_strips(raw):
    size = lax.axis_size("col")
    third = raw.shape[0] // 3
    strips = [
        lax.dot_general(
            raw[i * third : (i + 1) * third],
            raw[i * third :],
            (((1,), (1,)), ((), ())),
            precision=lax.Precision.HIGH,
            preferred_element_type=jnp.float32,
        )
        for i in range(3)
    ]
    packed = jnp.concatenate(strips, axis=1)
    blocks = lax.all_to_all(packed.reshape(size, third // size, -1), "col", 0, 0)
    return to_all(jnp.sum(blocks, axis=0), "col").reshape(third, -1)


def halves(values):
    high = values.astype(jnp.bfloat16)
    return (high, (values - high.astype(jnp.float32)).astype(jnp.bfloat16))


def put_halves(refs, rows, columns, values):
    for ref, half in zip(refs, halves(values)):
        ref[rows, columns] = half


def dot_halves(left, rows, right, columns):
    left_high, left_low = left[0][rows, :], left[1][rows, :]
    right_high, right_low = right[0][:, columns], right[1][:, columns]
    return (
        wide_dot(left_high, right_high, 1, 0)
        + wide_dot(left_high, right_low, 1, 0)
        + wide_dot(left_low, right_high, 1, 0)
    )


def schulz_kernel(sweeps, packed, raw, out, gram, half, current, *pairs):
    gram_pair, square_pair, half_pair, current_pair = [pairs[i : i + 2] for i in range(0, 8, 2)]
    height = raw.shape[0]
    third = height // 3
    bands = [slice(i * third, (i + 1) * third) for i in range(3)]
    tails = [slice(i * third, height) for i in range(3)]
    everything = slice(0, height)

    def put_symmetric(pair, i, values):
        put_halves(pair, bands[i], tails[i], values)
        for j in range(i + 1, 3):
            block = values[:, (j - i) * third : (j - i + 1) * third]
            put_halves(pair, bands[j], bands[i], block.T)

    total = jnp.zeros((1, 1), jnp.float32)
    start = 0
    for i in range(3):
        strip = packed[:, start : start + height - i * third]
        start += height - i * third
        gram[bands[i], tails[i]] = strip
        rows = lax.broadcasted_iota(jnp.int32, (third, third), 0)
        columns = lax.broadcasted_iota(jnp.int32, (third, third), 1)
        diagonal = jnp.where(rows == columns, strip[:, :third], 0.0)
        total = total + jnp.sum(jnp.sum(diagonal, axis=1, keepdims=True), axis=0, keepdims=True)
    scale = 1.0 / (jnp.sqrt(total) + 1e-07)
    for i in range(3):
        values = gram[bands[i], tails[i]] * (scale * scale)
        gram[bands[i], tails[i]] = values
        put_symmetric(gram_pair, i, values)
        values = raw[bands[i], :] * scale
        current[bands[i], :] = values
        put_halves(current_pair, bands[i], everything, values)

    def sweep(index, carry):
        for i in range(3):
            product = dot_halves(gram_pair, bands[i], gram_pair, tails[i])
            square = schulz_second * gram[bands[i], tails[i]] + schulz_third * product
            put_symmetric(square_pair, i, square)
        for i in range(3):
            product = dot_halves(square_pair, bands[i], current_pair, everything)
            current[bands[i], :] = schulz_first * current[bands[i], :] + product

        @pl.when(index < sweeps - 1)
        def _():
            for i in range(3):
                put_halves(current_pair, bands[i], everything, current[bands[i], :])
                product = dot_halves(square_pair, bands[i], gram_pair, tails[i])
                values = schulz_first * gram[bands[i], tails[i]] + product
                half[bands[i], tails[i]] = values
                put_symmetric(half_pair, i, values)
            for i in range(3):
                product = dot_halves(square_pair, bands[i], half_pair, tails[i])
                values = schulz_first * half[bands[i], tails[i]] + product
                gram[bands[i], tails[i]] = values
                put_symmetric(gram_pair, i, values)

        return carry

    lax.fori_loop(0, sweeps, sweep, 0)
    out[...] = current[...].astype(out.dtype)


def schulz(raw, packed):
    height, width = raw.shape
    square_shape = (height, height)
    whole = [pltpu.VMEM(square_shape, jnp.float32)] * 2 + [pltpu.VMEM(raw.shape, jnp.float32)]
    pairs = [pltpu.VMEM(square_shape, jnp.bfloat16)] * 6 + [pltpu.VMEM(raw.shape, jnp.bfloat16)] * 2
    return kernel_call(
        functools.partial(schulz_kernel, 5),
        [packed, raw],
        [jax.ShapeDtypeStruct(raw.shape, jnp.bfloat16)],
        whole + pairs,
        2 * 3 * 14 * height * height * width,
    )[0]


def on_device(
    residual_in,
    cotangent,
    qkv_weight,
    proj_weight,
    up_weight,
    down_weight,
    norm_params,
    qkv_moment,
    proj_moment,
    up_moment,
    down_moment,
    norm_moment,
):
    tokens, width_row = residual_in.shape
    row_size = lax.axis_size("row")
    col_size = lax.axis_size("col")
    dp_size = lax.axis_size("dp")
    model_width = width_row * row_size
    levels = qkv_weight.shape[0]
    jobs = levels * kinds
    chunk = -(-tokens // (8 * col_size)) * 8
    padded = chunk * col_size
    sent_rows = -(-tokens // 16) * 16
    me = (lax.axis_index("dp") * row_size + lax.axis_index("row")) % jobs
    my_row = lax.axis_index("row")
    my_chunk = lax.axis_index("col") * chunk

    weights = (qkv_weight, proj_weight, up_weight, down_weight)
    moments = (qkv_moment, proj_moment, up_moment, down_moment)
    flipped = (False, True, False, True)

    def upright(array, kind_index, level_index):
        block = array[level_index]
        return block.T if flipped[kind_index] else block

    widths = [
        w.shape[1] if flipped[k] else w.shape[2] for k, w in enumerate(weights)
    ]
    widest = max(widths)

    def own_weights(level_index, which):
        parts = [upright(weights[k], k, level_index).astype(jnp.bfloat16) for k in which]
        return jnp.concatenate(parts, axis=1)

    def gathered_weights(own, which):
        whole = gather_by_pairs(own, "row")
        whole = whole.reshape(model_width, -1)
        result = []
        start = 0
        for k in which:
            result.append(whole[:, start : start + widths[k]])
            start += widths[k]
        return result

    def features_first(blocks):
        return blocks.transpose(1, 0, 2).reshape(blocks.shape[1], model_width)

    all_norms = gather_by_pairs(norm_params, "row")
    all_norms = all_norms.transpose(1, 2, 0, 3).reshape(levels, kinds, model_width)
    image_blocks = to_all(swap_row_col(residual_in), "col")
    position = lax.axis_index("col").astype(jnp.int32).reshape(1)
    heads = widths[0] // (3 * HD)

    def shaped(rows, columns, kind):
        return jax.ShapeDtypeStruct((rows, columns), kind)

    low_chunk = shaped(chunk, model_width, jnp.bfloat16)
    full_chunk = shaped(chunk, model_width, jnp.float32)
    low_chunks = [low_chunk] * col_size
    sent = shaped(sent_rows, widest, jnp.bfloat16)
    sent_model = shaped(sent_rows, model_width, jnp.bfloat16)
    whole_scratch = pltpu.VMEM((padded, model_width), jnp.float32)
    attention_flops = 2 * padded * (
        model_width * (widths[0] + widths[1]) + 2 * padded * widths[1]
    )
    perceptron_flops = 2 * padded * model_width * (widths[2] + widths[3])
    chunk_flops = 20 * chunk * model_width

    def norm_step(parts, stream, level_index, first_row):
        return kernel_call(
            functools.partial(norm_kernel, level_index, first_row, len(parts)),
            [*parts, stream, all_norms],
            [full_chunk, low_chunk],
            [],
            chunk_flops,
        )

    def norm_back_step(parts, stream, upstream, level_index, first_row):
        return kernel_call(
            functools.partial(norm_back_kernel, level_index, first_row, len(parts)),
            [*parts, stream, upstream, all_norms],
            [full_chunk, low_chunk, shaped(2, model_width, jnp.float32)],
            [],
            chunk_flops,
        )

    *chunks, stream = kernel_call(
        functools.partial(first_kernel, tokens),
        [image_blocks, all_norms],
        low_chunks + [full_chunk],
        [whole_scratch],
        20 * padded * model_width,
        position,
    )
    groups = ((0, 1), (2, 3))

    def weights_of(own_groups):
        return sum([gathered_weights(own, which) for own, which in zip(own_groups, groups)], [])

    own_groups = [[own_weights(i, which) for which in groups] for i in range(levels)]
    weight_sets = [weights_of(own_groups[0])] + [None] * (levels - 1)
    chunks, own_groups[1:] = lax.optimization_barrier((chunks, own_groups[1:]))
    for level_index in range(1, levels):
        weight_sets[level_index] = weights_of(own_groups[level_index])
    saved = []
    early = [None] * levels
    for level_index in range(levels):
        weight_qkv, weight_proj, weight_up, weight_down = weight_sets[level_index]
        stream_one = stream
        *parts, mixed, normed_one, attended = kernel_call(
            functools.partial(attend_kernel, tokens, heads),
            [*chunks, weight_qkv, weight_proj],
            low_chunks + [shaped(padded, widths[0], jnp.bfloat16), sent_model, sent],
            [whole_scratch, pltpu.VMEM((padded, widths[1]), jnp.float32)],
            attention_flops,
            position,
        )
        stream_two, normed = norm_step(swap_parts(parts), stream, level_index, 2)
        chunks = to_partners(normed)
        *parts, slope, normed_two, activated = kernel_call(
            functools.partial(mlp_kernel, tokens),
            [*chunks, weight_up, weight_down],
            low_chunks + [shaped(padded, widths[2], jnp.float32), sent_model, sent],
            [whole_scratch],
            perceptron_flops,
            position,
        )
        parts = swap_parts(parts)
        early[level_index] = (normed_one, attended, normed_two, activated)
        if level_index < levels - 1:
            stream, normed = norm_step(parts, stream_two, level_index + 1, 0)
            if level_index == 0:
                normed, late_me, cotangent = lax.optimization_barrier((normed, me, cotangent))
            chunks = to_partners(normed)
        else:
            stream = stream_two
            for part in parts:
                stream = stream + part.astype(jnp.float32)
        saved.append((stream_one, stream_two, mixed, slope))

    def placed(chunk_values):
        blocks = chunk_values.reshape(chunk, col_size, width_row).transpose(1, 0, 2)
        col = lax.axis_index("col")
        received = [pick(blocks, col)]
        for k in range(1, col_size):
            received.append(from_partner(pick(blocks, col ^ k), k, ("col",)))
        whole = placed_blocks(received, [col ^ k for k in range(col_size)])
        return swap_row_col(whole.reshape(padded, width_row)[:tokens])

    groups_of_jobs = dp_size * row_size // jobs

    def spread(parts_of_levels):
        stack = jnp.stack([parts_of_levels[j % levels][j // levels] for j in range(jobs)])
        stack = jnp.concatenate([stack] * groups_of_jobs) if groups_of_jobs > 1 else stack
        return lax.all_to_all(stack, ("dp", "row"), 0, 0).reshape(-1, widest)

    upper = (late_me // row_size) % 2 == 1
    half = jobs // 2
    near_moments = []
    for j in range(half):
        low_job, high_job = [
            pad_columns(upright(moments[i // levels], i // levels, i % levels), widest)
            for i in (j, j + half)
        ]
        near_moments.append(jnp.where(upper, high_job, low_job))
    stacked_moment = jnp.stack(near_moments)
    own_moment = lax.all_to_all(stacked_moment, "row", 0, 0).reshape(model_width, widest)

    cotangent_blocks = pad_rows(swap_row_col(cotangent), padded)
    cotangent_blocks = cotangent_blocks.reshape(col_size, chunk, width_row)
    upstream = features_first(lax.all_to_all(cotangent_blocks, "col", 0, 0))

    block_output = placed(stream)
    upstream, own_moment, block_output = lax.optimization_barrier(
        (upstream, own_moment, block_output)
    )
    early_all = spread(early)
    late = [None] * levels
    norm_sums = [None] * levels
    back_low = upstream.astype(jnp.bfloat16)
    for level_index in reversed(range(levels)):
        weight_qkv, weight_proj, weight_up, weight_down = weight_sets[level_index]
        stream_one, stream_two, mixed, slope = saved[level_index]
        *parts, hidden_grad, back_two = kernel_call(
            mlp_back_kernel,
            [*to_partners(back_low), slope, weight_up, weight_down],
            low_chunks + [sent, sent_model],
            [whole_scratch],
            perceptron_flops,
            position,
        )
        upstream, back_low, sums_two = norm_back_step(
            swap_parts(parts), stream_two, upstream, level_index, 2
        )
        *parts, mixed_grad, back_one = kernel_call(
            functools.partial(attend_back_kernel, tokens, heads),
            [*to_partners(back_low), mixed, weight_qkv, weight_proj],
            low_chunks + [sent, sent_model],
            [whole_scratch, pltpu.VMEM((padded, widths[0]), jnp.float32)],
            3 * attention_flops,
            position,
        )
        late[level_index] = (mixed_grad, back_one, hidden_grad, back_two)
        if level_index == 0:
            late_all = spread(late)
        upstream, back_low, sums_one = norm_back_step(
            swap_parts(parts), stream_one, upstream, level_index, 0
        )
        norm_sums[level_index] = jnp.concatenate([sums_one, sums_two])

    norm_whole = jnp.stack(norm_sums)
    for axis in ("row", "col", "dp"):
        norm_whole = sum_by_pairs(norm_whole, axis)
    norm_grad = lax.dynamic_slice_in_dim(norm_whole, my_row * width_row, width_row, 2)
    norm_moment_new = moment_decay * norm_moment + norm_grad
    late_all, norm_grad, norm_moment_new = lax.optimization_barrier(
        (late_all, norm_grad, norm_moment_new)
    )

    turned = (me // levels) % 2 == 1
    model_side = jnp.where(turned, late_all, early_all)
    hidden_side = jnp.where(turned, early_all, late_all)
    own_grad = outer_grad(model_side, hidden_side)

    def returned(whole):
        blocks = whole.astype(jnp.bfloat16).reshape(row_size, width_row, widest)
        blocks = jnp.concatenate([blocks] * dp_size)
        received = lax.all_to_all(blocks, ("dp", "row"), 0, 0)
        return [received[j].astype(jnp.float32) for j in range(jobs)]

    own_raw = moment_decay * own_moment + own_grad
    gram, own_grad = lax.optimization_barrier((gram_strips(own_raw), own_grad))
    grads = returned(own_grad)
    orths = returned(schulz(own_raw, gram))

    grad_outs = []
    moment_outs = []
    new_outs = []
    for kind_index in range(kinds):
        grad_levels = []
        orth_levels = []
        for level_index in range(levels):
            job = kind_index * levels + level_index
            grad_here = grads[job][:, : widths[kind_index]]
            orth_here = orths[job][:, : widths[kind_index]]
            if flipped[kind_index]:
                grad_here = grad_here.T
                orth_here = orth_here.T
            grad_levels.append(grad_here)
            orth_levels.append(orth_here)
        grad_out = jnp.stack(grad_levels)
        grad_outs.append(grad_out)
        moment_outs.append(moment_decay * moments[kind_index] + grad_out)
        new_outs.append(weights[kind_index] - step_rates[kind_index] * jnp.stack(orth_levels))

    tokens_all = tokens * col_size * dp_size
    norm_new = norm_params - norm_rate / math.sqrt(tokens_all) * norm_moment_new
    return (
        block_output,
        placed(upstream),
        *grad_outs,
        norm_grad,
        *moment_outs,
        norm_moment_new,
        *new_outs,
        norm_new,
    )


def solution(mesh):
    tokens_spec = P(("dp", "col"), "row")
    wide = P(None, "row", "col")
    tall = P(None, "col", "row")
    norms = P(None, None, "row")
    return jax.shard_map(
        on_device,
        mesh=mesh,
        in_specs=(tokens_spec, tokens_spec) + (wide, tall, wide, tall, norms) * 2,
        out_specs=(tokens_spec, tokens_spec) + (wide, tall, wide, tall, norms) * 3,
        check_vma=False,
    )
```

```python
import functools
import math

import jax
import jax.numpy as jnp
from jax import lax
from jax.experimental import pallas as pl
from jax.experimental.pallas import tpu as pltpu
from jax.sharding import PartitionSpec as P

HD = 64

norm_epsilon = 1e-06
moment_decay = 0.9
norm_rate = 0.05
step_rates = (1.7, 5.6, 2.0, 1.0)
schulz_first = 3.4445
schulz_second = -4.775
schulz_third = 2.0315
kinds = 4


def outer_grad(left_side, right_side):
    return lax.dot_general(
        left_side, right_side, (((0,), (0,)), ((), ())), preferred_element_type=jnp.float32
    )


def pad_rows(values, rows):
    return jnp.pad(values, ((0, rows - values.shape[0]), (0, 0)))


def pad_columns(values, columns):
    return jnp.pad(values, ((0, 0), (0, columns - values.shape[1])))


def norm_parts_of(values):
    average = jnp.mean(values, axis=1, keepdims=True)
    square = jnp.mean(values * values, axis=1, keepdims=True)
    inverse = lax.rsqrt(square - average * average + norm_epsilon)
    return ((values - average) * inverse, inverse)


def norm_backward(grad_out, plain, inverse, gain_row):
    scaled = grad_out * gain_row
    first = jnp.mean(scaled, axis=1, keepdims=True)
    second = jnp.mean(scaled * plain, axis=1, keepdims=True)
    return inverse * (scaled - first - plain * second)


def wide_dot(left_side, right_side, left_dim, right_dim):
    return lax.dot_general(
        left_side,
        right_side,
        (((left_dim,), (right_dim,)), ((), ())),
        preferred_element_type=jnp.float32,
    )


def in_vmem(count):
    return [pl.BlockSpec(memory_space=pltpu.VMEM)] * count


def kernel_call(body, inputs, outputs, scratch, flops, position=None):
    specs = in_vmem(len(inputs))
    operands = list(inputs)
    if position is not None:
        specs = [pl.BlockSpec(memory_space=pltpu.SMEM)] + specs
        operands = [position] + operands
    moved = sum(math.prod(o.shape) * o.dtype.itemsize for o in list(inputs) + list(outputs))
    return pl.pallas_call(
        body,
        out_shape=list(outputs),
        in_specs=specs,
        out_specs=in_vmem(len(outputs)),
        scratch_shapes=scratch,
        compiler_params=pltpu.CompilerParams(vmem_limit_bytes=40 * 1024 * 1024),
        cost_estimate=pl.CostEstimate(flops=flops, bytes_accessed=moved, transcendentals=0),
    )(*operands)


def put_chunks(position_ref, chunk_refs, whole_ref):
    chunk = chunk_refs[0].shape[0]
    for k, chunk_ref in enumerate(chunk_refs):
        start = pl.multiple_of((position_ref[0] ^ k) * chunk, 8)
        whole_ref[pl.ds(start, chunk), :] = chunk_ref[...].astype(jnp.float32)


def take_chunks(position_ref, whole_ref, chunk_refs):
    chunk = chunk_refs[0].shape[0]
    for k, chunk_ref in enumerate(chunk_refs):
        start = pl.multiple_of((position_ref[0] ^ k) * chunk, 8)
        chunk_ref[...] = whole_ref[pl.ds(start, chunk), :].astype(chunk_ref.dtype)


def keep_rows(values, tokens):
    rows = lax.broadcasted_iota(jnp.int32, values.shape, 0)
    return jnp.where(rows < tokens, values, jnp.zeros_like(values))


def head_probs(mixed, head, tokens):
    start = head * 3 * HD
    query = mixed[:, start : start + HD]
    key = mixed[:, start + HD : start + 2 * HD]
    value = mixed[:, start + 2 * HD : start + 3 * HD]
    scores = wide_dot(query, key, 1, 1) * HD ** (-0.5)
    columns = lax.broadcasted_iota(jnp.int32, scores.shape, 1)
    scores = jnp.where(columns < tokens, scores, -jnp.inf)
    exps = jnp.exp(scores - jnp.max(scores, axis=1, keepdims=True))
    probs = exps / jnp.sum(exps, axis=1, keepdims=True)
    return (query, key, value, probs)


def attend_kernel(tokens, heads, position, *refs):
    size = (len(refs) - 7) // 2
    chunks, (w_qkv, w_proj) = refs[:size], refs[size : size + 2]
    outs = refs[size + 2 : 2 * size + 2]
    mixed_out, normed_out, att_out, whole, att_all = refs[2 * size + 2 :]
    put_chunks(position, chunks, whole)
    normed = keep_rows(whole[...], tokens).astype(jnp.bfloat16)
    normed_out[...] = normed[: normed_out.shape[0]]
    mixed = wide_dot(normed, w_qkv[...], 1, 0).astype(jnp.bfloat16)
    mixed_out[...] = mixed
    for head in range(heads):
        _, _, value, probs = head_probs(mixed, head, tokens)
        att_all[:, head * HD : (head + 1) * HD] = wide_dot(probs.astype(jnp.bfloat16), value, 1, 0)
    attended = keep_rows(att_all[...], tokens).astype(jnp.bfloat16)
    att_out[...] = jnp.zeros_like(att_out)
    att_out[:, : heads * HD] = attended[: att_out.shape[0]]
    whole[...] = wide_dot(attended, w_proj[...], 1, 1)
    take_chunks(position, whole, outs)


def attend_back_kernel(tokens, heads, position, *refs):
    size = (len(refs) - 7) // 2
    chunks, (mixed_ref, w_qkv, w_proj) = refs[:size], refs[size : size + 3]
    outs = refs[size + 3 : 2 * size + 3]
    mixed_grad_out, back_out, whole, mixed_grad = refs[2 * size + 3 :]
    put_chunks(position, chunks, whole)
    back = whole[...].astype(jnp.bfloat16)
    back_out[...] = back[: back_out.shape[0]]
    att_grad = wide_dot(back, w_proj[...], 1, 0).astype(jnp.bfloat16)
    mixed = mixed_ref[...]
    scaling = HD ** (-0.5)
    for head in range(heads):
        query, key, value, probs = head_probs(mixed, head, tokens)
        grad = att_grad[:, head * HD : (head + 1) * HD]
        probs_grad = wide_dot(grad, value, 1, 1)
        inner = jnp.sum(probs * probs_grad, axis=1, keepdims=True)
        scores_grad = (probs * (probs_grad - inner)).astype(jnp.bfloat16)
        start = head * 3 * HD
        mixed_grad[:, start : start + HD] = wide_dot(scores_grad, key, 1, 0) * scaling
        mixed_grad[:, start + HD : start + 2 * HD] = wide_dot(scores_grad, query, 0, 0) * scaling
        mixed_grad[:, start + 2 * HD : start + 3 * HD] = wide_dot(
            probs.astype(jnp.bfloat16), grad, 0, 0
        )
    grads = mixed_grad[...].astype(jnp.bfloat16)
    mixed_grad_out[...] = jnp.zeros_like(mixed_grad_out)
    mixed_grad_out[:, : grads.shape[1]] = grads[: mixed_grad_out.shape[0]]
    whole[...] = wide_dot(grads, w_qkv[...], 1, 1)
    take_chunks(position, whole, outs)


def norm_kernel(level_index, first_row, size, *refs):
    parts, (stream_ref, norms) = refs[:size], refs[size : size + 2]
    stream_out, normed_out = refs[size + 2 :]
    stream = stream_ref[...]
    for part in parts:
        stream = stream + part[...].astype(jnp.float32)
    stream_out[...] = stream
    plain, _ = norm_parts_of(stream)
    gain = norms[level_index, first_row : first_row + 1, :]
    bias = norms[level_index, first_row + 1 : first_row + 2, :]
    normed_out[...] = (plain * gain + bias).astype(jnp.bfloat16)


def norm_back_kernel(level_index, first_row, size, *refs):
    parts, (stream_ref, upstream_ref, norms) = refs[:size], refs[size : size + 3]
    upstream_out, low_out, sums_out = refs[size + 3 :]
    grad = parts[0][...].astype(jnp.float32)
    for part in parts[1:]:
        grad = grad + part[...].astype(jnp.float32)
    plain, inverse = norm_parts_of(stream_ref[...])
    gain = norms[level_index, first_row : first_row + 1, :]
    upstream = upstream_ref[...] + norm_backward(grad, plain, inverse, gain)
    upstream_out[...] = upstream
    low_out[...] = upstream.astype(jnp.bfloat16)
    sums_out[0:1, :] = jnp.sum(grad * plain, axis=0, keepdims=True)
    sums_out[1:2, :] = jnp.sum(grad, axis=0, keepdims=True)


def first_kernel(tokens, position, blocks, norms, *refs):
    outs, stream_out, whole = refs[:-2], refs[-2], refs[-1]
    size, _, width = blocks.shape
    whole[...] = jnp.zeros_like(whole)
    for i in range(size):
        whole[0:tokens, i * width : (i + 1) * width] = blocks[i].astype(jnp.float32)
    chunk = stream_out.shape[0]
    start = pl.multiple_of(position[0] * chunk, 8)
    stream_out[...] = whole[pl.ds(start, chunk), :]
    plain, _ = norm_parts_of(whole[...])
    whole[...] = plain * norms[0, 0:1, :] + norms[0, 1:2, :]
    take_chunks(position, whole, outs)


def mlp_kernel(tokens, position, *refs):
    size = (len(refs) - 6) // 2
    chunks, (w_up, w_down) = refs[:size], refs[size : size + 2]
    outs = refs[size + 2 : 2 * size + 2]
    slope_out, normed_out, act_out, whole = refs[2 * size + 2 :]
    put_chunks(position, chunks, whole)
    normed = keep_rows(whole[...], tokens).astype(jnp.bfloat16)
    normed_out[...] = normed[: normed_out.shape[0]]
    hidden = wide_dot(normed, w_up[...], 1, 0)
    below = 0.5 + 0.5 * lax.erf(hidden * math.sqrt(0.5))
    slope_out[...] = below + hidden * jnp.exp(-0.5 * hidden * hidden) * (
        1.0 / math.sqrt(2.0 * math.pi)
    )
    activated = keep_rows(hidden * below, tokens).astype(jnp.bfloat16)
    act_out[...] = activated[: act_out.shape[0]]
    whole[...] = wide_dot(activated, w_down[...], 1, 1)
    take_chunks(position, whole, outs)


def mlp_back_kernel(position, *refs):
    size = (len(refs) - 6) // 2
    chunks, (slope, w_up, w_down) = refs[:size], refs[size : size + 3]
    outs = refs[size + 3 : 2 * size + 3]
    hidden_grad_out, back_out, whole = refs[2 * size + 3 :]
    put_chunks(position, chunks, whole)
    back = whole[...].astype(jnp.bfloat16)
    back_out[...] = back[: back_out.shape[0]]
    hidden_grad = (wide_dot(back, w_down[...], 1, 0) * slope[...]).astype(jnp.bfloat16)
    hidden_grad_out[...] = hidden_grad[: hidden_grad_out.shape[0]]
    whole[...] = wide_dot(hidden_grad, w_up[...], 1, 1)
    take_chunks(position, whole, outs)


def swap_row_col(values):
    size = lax.axis_size("row")
    pairs = [(i * size + j, j * size + i) for i in range(size) for j in range(size)]
    return lax.ppermute(values, ("row", "col"), pairs)


def from_partner(values, step, axes=("dp", "row"), wanted=None):
    count = math.prod(lax.axis_size(a) for a in axes)
    pairs = [(i, i ^ step) for i in range(count) if wanted is None or wanted(i ^ step)]
    return lax.ppermute(values, axes, pairs)


def pick(stacked, index):
    return lax.dynamic_index_in_dim(stacked, index, 0, keepdims=False)


def placed_blocks(blocks, places):
    result = jnp.zeros((len(blocks),) + blocks[0].shape, blocks[0].dtype)
    for block, place in zip(blocks, places):
        result = lax.dynamic_update_index_in_dim(result, block, place, 0)
    return result


def gather_by_pairs(values, axis):
    step = lax.axis_size(axis) // 2
    me = lax.axis_index(axis)
    blocks, places = [values], [me]
    while step:
        sent = blocks[0][None] if len(blocks) == 1 else jnp.stack(blocks)
        received = from_partner(sent, step, (axis,))
        blocks = blocks + [received[i] for i in range(len(blocks))]
        places = places + [p ^ step for p in places]
        step //= 2
    return placed_blocks(blocks, places)


def sum_by_pairs(values, axis):
    step = 1
    while step < lax.axis_size(axis):
        values = values + from_partner(values, step, (axis,))
        step *= 2
    return values


def to_all(block, axis):
    size = lax.axis_size(axis)
    return lax.all_to_all(jnp.broadcast_to(block[None], (size,) + block.shape), axis, 0, 0)


def to_partners(chunk):
    size = lax.axis_size("col")
    return [chunk] + [from_partner(chunk, k, ("col",)) for k in range(1, size)]


def swap_parts(parts):
    return [parts[0]] + [from_partner(parts[k], k, ("col",)) for k in range(1, len(parts))]


def gram_strips(raw):
    size = lax.axis_size("col")
    third = raw.shape[0] // 3
    strips = [
        lax.dot_general(
            raw[i * third : (i + 1) * third],
            raw[i * third :],
            (((1,), (1,)), ((), ())),
            precision=lax.Precision.HIGH,
            preferred_element_type=jnp.float32,
        )
        for i in range(3)
    ]
    packed = jnp.concatenate(strips, axis=1)
    blocks = lax.all_to_all(packed.reshape(size, third // size, -1), "col", 0, 0)
    return jnp.sum(blocks, axis=0)


def halves(values):
    high = values.astype(jnp.bfloat16)
    return (high, (values - high.astype(jnp.float32)).astype(jnp.bfloat16))


def put_halves(refs, rows, columns, values):
    for ref, half in zip(refs, halves(values)):
        ref[rows, columns] = half


def dot_halves(left, rows, right, columns):
    left_high, left_low = left[0][rows, :], left[1][rows, :]
    right_high, right_low = right[0][:, columns], right[1][:, columns]
    return (
        wide_dot(left_high, right_high, 1, 0)
        + wide_dot(left_high, right_low, 1, 0)
        + wide_dot(left_low, right_high, 1, 0)
    )


def schulz_kernel(sweeps, packed, raw, out, gram, half, current, *pairs):
    gram_pair, square_pair, half_pair, current_pair = [pairs[i : i + 2] for i in range(0, 8, 2)]
    height = raw.shape[0]
    third = height // 3
    bands = [slice(i * third, (i + 1) * third) for i in range(3)]
    tails = [slice(i * third, height) for i in range(3)]
    everything = slice(0, height)

    def put_symmetric(pair, i, values):
        put_halves(pair, bands[i], tails[i], values)
        for j in range(i + 1, 3):
            block = values[:, (j - i) * third : (j - i + 1) * third]
            put_halves(pair, bands[j], bands[i], block.T)

    total = jnp.zeros((1, 1), jnp.float32)
    start = 0
    for i in range(3):
        strip = packed[:, start : start + height - i * third]
        start += height - i * third
        gram[bands[i], tails[i]] = strip
        rows = lax.broadcasted_iota(jnp.int32, (third, third), 0)
        columns = lax.broadcasted_iota(jnp.int32, (third, third), 1)
        diagonal = jnp.where(rows == columns, strip[:, :third], 0.0)
        total = total + jnp.sum(jnp.sum(diagonal, axis=1, keepdims=True), axis=0, keepdims=True)
    scale = 1.0 / (jnp.sqrt(total) + 1e-07)
    for i in range(3):
        values = gram[bands[i], tails[i]] * (scale * scale)
        gram[bands[i], tails[i]] = values
        put_symmetric(gram_pair, i, values)
        values = raw[bands[i], :] * scale
        current[bands[i], :] = values
        put_halves(current_pair, bands[i], everything, values)

    def sweep(index, carry):
        for i in range(3):
            product = dot_halves(gram_pair, bands[i], gram_pair, tails[i])
            square = schulz_second * gram[bands[i], tails[i]] + schulz_third * product
            put_symmetric(square_pair, i, square)
        for i in range(3):
            product = dot_halves(square_pair, bands[i], current_pair, everything)
            current[bands[i], :] = schulz_first * current[bands[i], :] + product

        @pl.when(index < sweeps - 1)
        def _():
            for i in range(3):
                put_halves(current_pair, bands[i], everything, current[bands[i], :])
                product = dot_halves(square_pair, bands[i], gram_pair, tails[i])
                values = schulz_first * gram[bands[i], tails[i]] + product
                half[bands[i], tails[i]] = values
                put_symmetric(half_pair, i, values)
            for i in range(3):
                product = dot_halves(square_pair, bands[i], half_pair, tails[i])
                values = schulz_first * half[bands[i], tails[i]] + product
                gram[bands[i], tails[i]] = values
                put_symmetric(gram_pair, i, values)

        return carry

    lax.fori_loop(0, sweeps, sweep, 0)
    out[...] = current[...].astype(out.dtype)


def schulz(raw, packed):
    height, width = raw.shape
    square_shape = (height, height)
    whole = [pltpu.VMEM(square_shape, jnp.float32)] * 2 + [pltpu.VMEM(raw.shape, jnp.float32)]
    pairs = [pltpu.VMEM(square_shape, jnp.bfloat16)] * 6 + [pltpu.VMEM(raw.shape, jnp.bfloat16)] * 2
    return kernel_call(
        functools.partial(schulz_kernel, 5),
        [packed, raw],
        [jax.ShapeDtypeStruct(raw.shape, jnp.bfloat16)],
        whole + pairs,
        2 * 3 * 14 * height * height * width,
    )[0]


def on_device(
    residual_in,
    cotangent,
    qkv_weight,
    proj_weight,
    up_weight,
    down_weight,
    norm_params,
    qkv_moment,
    proj_moment,
    up_moment,
    down_moment,
    norm_moment,
):
    tokens, width_row = residual_in.shape
    row_size = lax.axis_size("row")
    col_size = lax.axis_size("col")
    dp_size = lax.axis_size("dp")
    model_width = width_row * row_size
    levels = qkv_weight.shape[0]
    jobs = levels * kinds
    chunk = -(-tokens // (8 * col_size)) * 8
    padded = chunk * col_size
    sent_rows = -(-tokens // 16) * 16
    me = (lax.axis_index("dp") * row_size + lax.axis_index("row")) % jobs
    my_row = lax.axis_index("row")
    my_chunk = lax.axis_index("col") * chunk

    weights = (qkv_weight, proj_weight, up_weight, down_weight)
    moments = (qkv_moment, proj_moment, up_moment, down_moment)
    flipped = (False, True, False, True)

    def upright(array, kind_index, level_index):
        block = array[level_index]
        return block.T if flipped[kind_index] else block

    widths = [
        w.shape[1] if flipped[k] else w.shape[2] for k, w in enumerate(weights)
    ]
    widest = max(widths)

    def own_weights(level_index, which):
        parts = [upright(weights[k], k, level_index).astype(jnp.bfloat16) for k in which]
        return jnp.concatenate(parts, axis=1)

    def gathered_weights(own, which):
        whole = gather_by_pairs(own, "row")
        whole = whole.reshape(model_width, -1)
        result = []
        start = 0
        for k in which:
            result.append(whole[:, start : start + widths[k]])
            start += widths[k]
        return result

    def features_first(blocks):
        return blocks.transpose(1, 0, 2).reshape(blocks.shape[1], model_width)

    all_norms = gather_by_pairs(norm_params, "row")
    all_norms = all_norms.transpose(1, 2, 0, 3).reshape(levels, kinds, model_width)
    image_blocks = to_all(swap_row_col(residual_in), "col")
    position = lax.axis_index("col").astype(jnp.int32).reshape(1)
    heads = widths[0] // (3 * HD)

    def shaped(rows, columns, kind):
        return jax.ShapeDtypeStruct((rows, columns), kind)

    low_chunk = shaped(chunk, model_width, jnp.bfloat16)
    full_chunk = shaped(chunk, model_width, jnp.float32)
    low_chunks = [low_chunk] * col_size
    sent = shaped(sent_rows, widest, jnp.bfloat16)
    sent_model = shaped(sent_rows, model_width, jnp.bfloat16)
    whole_scratch = pltpu.VMEM((padded, model_width), jnp.float32)
    attention_flops = 2 * padded * (
        model_width * (widths[0] + widths[1]) + 2 * padded * widths[1]
    )
    perceptron_flops = 2 * padded * model_width * (widths[2] + widths[3])
    chunk_flops = 20 * chunk * model_width

    def norm_step(parts, stream, level_index, first_row):
        return kernel_call(
            functools.partial(norm_kernel, level_index, first_row, len(parts)),
            [*parts, stream, all_norms],
            [full_chunk, low_chunk],
            [],
            chunk_flops,
        )

    def norm_back_step(parts, stream, upstream, level_index, first_row):
        return kernel_call(
            functools.partial(norm_back_kernel, level_index, first_row, len(parts)),
            [*parts, stream, upstream, all_norms],
            [full_chunk, low_chunk, shaped(2, model_width, jnp.float32)],
            [],
            chunk_flops,
        )

    *chunks, stream = kernel_call(
        functools.partial(first_kernel, tokens),
        [image_blocks, all_norms],
        low_chunks + [full_chunk],
        [whole_scratch],
        20 * padded * model_width,
        position,
    )
    groups = ((0, 1), (2, 3))

    def weights_of(own_groups):
        return sum([gathered_weights(own, which) for own, which in zip(own_groups, groups)], [])

    own_groups = [[own_weights(i, which) for which in groups] for i in range(levels)]
    weight_sets = [weights_of(own_groups[0])] + [None] * (levels - 1)
    saved = []
    early = [None] * levels
    for level_index in range(levels):
        weight_qkv, weight_proj, weight_up, weight_down = weight_sets[level_index]
        stream_one = stream
        *parts, mixed, normed_one, attended = kernel_call(
            functools.partial(attend_kernel, tokens, heads),
            [*chunks, weight_qkv, weight_proj],
            low_chunks + [shaped(padded, widths[0], jnp.bfloat16), sent_model, sent],
            [whole_scratch, pltpu.VMEM((padded, widths[1]), jnp.float32)],
            attention_flops,
            position,
        )
        stream_two, normed = norm_step(swap_parts(parts), stream, level_index, 2)
        if level_index == 0:
            normed, own_groups[1:] = lax.optimization_barrier((normed, own_groups[1:]))
            for later in range(1, levels):
                weight_sets[later] = weights_of(own_groups[later])
        if level_index == levels - 1:
            normed, back_chunks = lax.optimization_barrier((normed, back_chunks))
        chunks = to_partners(normed)
        *parts, slope, normed_two, activated = kernel_call(
            functools.partial(mlp_kernel, tokens),
            [*chunks, weight_up, weight_down],
            low_chunks + [shaped(padded, widths[2], jnp.float32), sent_model, sent],
            [whole_scratch],
            perceptron_flops,
            position,
        )
        parts = swap_parts(parts)
        early[level_index] = (normed_one, attended, normed_two, activated)
        if level_index < levels - 1:
            stream, normed = norm_step(parts, stream_two, level_index + 1, 0)
            if level_index == 0:
                normed, late_me, cotangent = lax.optimization_barrier((normed, me, cotangent))
                cotangent_blocks = pad_rows(swap_row_col(cotangent), padded)
                cotangent_blocks = cotangent_blocks.reshape(col_size, chunk, width_row)
                upstream = features_first(lax.all_to_all(cotangent_blocks, "col", 0, 0))
                back_chunks = to_partners(upstream.astype(jnp.bfloat16))
            chunks = to_partners(normed)
        else:
            stream = stream_two
            for part in parts:
                stream = stream + part.astype(jnp.float32)
        saved.append((stream_one, stream_two, mixed, slope))

    def placed(chunk_values):
        blocks = chunk_values.reshape(chunk, col_size, width_row).transpose(1, 0, 2)
        col = lax.axis_index("col")
        received = [pick(blocks, col)]
        for k in range(1, col_size):
            received.append(from_partner(pick(blocks, col ^ k), k, ("col",)))
        whole = placed_blocks(received, [col ^ k for k in range(col_size)])
        return swap_row_col(whole.reshape(padded, width_row)[:tokens])

    groups_of_jobs = dp_size * row_size // jobs

    def spread(parts_of_levels):
        stack = jnp.stack([parts_of_levels[j % levels][j // levels] for j in range(jobs)])
        stack = jnp.concatenate([stack] * groups_of_jobs) if groups_of_jobs > 1 else stack
        return lax.all_to_all(stack, ("dp", "row"), 0, 0).reshape(-1, widest)

    upper = (late_me // row_size) % 2 == 1
    half = jobs // 2
    near_moments = []
    for j in range(half):
        low_job, high_job = [
            pad_columns(upright(moments[i // levels], i // levels, i % levels), widest)
            for i in (j, j + half)
        ]
        near_moments.append(jnp.where(upper, high_job, low_job))
    stacked_moment = jnp.stack(near_moments)
    own_moment = lax.all_to_all(stacked_moment, "row", 0, 0).reshape(model_width, widest)

    back_chunks, own_moment = lax.optimization_barrier((back_chunks, own_moment))
    early_all = spread(early)
    late = [None] * levels
    norm_sums = [None] * levels
    for level_index in reversed(range(levels)):
        weight_qkv, weight_proj, weight_up, weight_down = weight_sets[level_index]
        stream_one, stream_two, mixed, slope = saved[level_index]
        *parts, hidden_grad, back_two = kernel_call(
            mlp_back_kernel,
            [*back_chunks, slope, weight_up, weight_down],
            low_chunks + [sent, sent_model],
            [whole_scratch],
            perceptron_flops,
            position,
        )
        upstream, back_low, sums_two = norm_back_step(
            swap_parts(parts), stream_two, upstream, level_index, 2
        )
        if level_index == 0:
            back_low, early_all = lax.optimization_barrier((back_low, early_all))
        *parts, mixed_grad, back_one = kernel_call(
            functools.partial(attend_back_kernel, tokens, heads),
            [*to_partners(back_low), mixed, weight_qkv, weight_proj],
            low_chunks + [sent, sent_model],
            [whole_scratch, pltpu.VMEM((padded, widths[0]), jnp.float32)],
            3 * attention_flops,
            position,
        )
        late[level_index] = (mixed_grad, back_one, hidden_grad, back_two)
        if level_index == 0:
            late_all = spread(late)
        upstream, back_low, sums_one = norm_back_step(
            swap_parts(parts), stream_one, upstream, level_index, 0
        )
        norm_sums[level_index] = jnp.concatenate([sums_one, sums_two])

        if level_index:
            back_chunks = to_partners(back_low)

    norm_whole = sum_by_pairs(jnp.stack(norm_sums), "col")
    late_all, norm_whole, stream, upstream = lax.optimization_barrier(
        (late_all, norm_whole, stream, upstream)
    )

    turned = (me // levels) % 2 == 1
    model_side = jnp.where(turned, late_all, early_all)
    hidden_side = jnp.where(turned, early_all, late_all)
    own_grad = outer_grad(model_side, hidden_side)

    def returned(whole):
        blocks = whole.astype(jnp.bfloat16).reshape(row_size, width_row, widest)
        blocks = jnp.concatenate([blocks] * dp_size)
        received = lax.all_to_all(blocks, ("dp", "row"), 0, 0)
        return [received[j] for j in range(jobs)]

    own_raw = moment_decay * own_moment + own_grad
    for axis in ("row", "dp"):
        norm_whole = sum_by_pairs(norm_whole, axis)
    block_output = placed(stream)
    own_strip, norm_whole, block_output = lax.optimization_barrier(
        (gram_strips(own_raw), norm_whole, block_output)
    )
    norm_grad = lax.dynamic_slice_in_dim(norm_whole, my_row * width_row, width_row, 2)
    norm_moment_new = moment_decay * norm_moment + norm_grad
    input_grad = placed(upstream)
    gram = to_all(own_strip, "col").reshape(-1, own_strip.shape[1])
    gram, own_grad, input_grad = lax.optimization_barrier((gram, own_grad, input_grad))
    grads = returned(own_grad)
    orth_whole, grads = lax.optimization_barrier((schulz(own_raw, gram), grads))
    orths = [block.astype(jnp.float32) for block in returned(orth_whole)]
    grads = [block.astype(jnp.float32) for block in grads]

    grad_outs = []
    moment_outs = []
    new_outs = []
    for kind_index in range(kinds):
        grad_levels = []
        orth_levels = []
        for level_index in range(levels):
            job = kind_index * levels + level_index
            grad_here = grads[job][:, : widths[kind_index]]
            orth_here = orths[job][:, : widths[kind_index]]
            if flipped[kind_index]:
                grad_here = grad_here.T
                orth_here = orth_here.T
            grad_levels.append(grad_here)
            orth_levels.append(orth_here)
        grad_out = jnp.stack(grad_levels)
        grad_outs.append(grad_out)
        moment_outs.append(moment_decay * moments[kind_index] + grad_out)
        new_outs.append(weights[kind_index] - step_rates[kind_index] * jnp.stack(orth_levels))

    tokens_all = tokens * col_size * dp_size
    norm_new = norm_params - norm_rate / math.sqrt(tokens_all) * norm_moment_new
    return (
        block_output,
        input_grad,
        *grad_outs,
        norm_grad,
        *moment_outs,
        norm_moment_new,
        *new_outs,
        norm_new,
    )


def solution(mesh):
    tokens_spec = P(("dp", "col"), "row")
    wide = P(None, "row", "col")
    tall = P(None, "col", "row")
    norms = P(None, None, "row")
    return jax.shard_map(
        on_device,
        mesh=mesh,
        in_specs=(tokens_spec, tokens_spec) + (wide, tall, wide, tall, norms) * 2,
        out_specs=(tokens_spec, tokens_spec) + (wide, tall, wide, tall, norms) * 3,
        check_vma=False,
    )
```

```python
import functools
import math

import jax
import jax.numpy as jnp
from jax import lax
from jax.experimental import pallas as pl
from jax.experimental.pallas import tpu as pltpu
from jax.sharding import PartitionSpec as P

HD = 64

norm_epsilon = 1e-06
moment_decay = 0.9
norm_rate = 0.05
step_rates = (1.7, 5.6, 2.0, 1.0)
schulz_first = 3.4445
schulz_second = -4.775
schulz_third = 2.0315
kinds = 4


def outer_grad(left_side, right_side):
    return lax.dot_general(
        left_side, right_side, (((0,), (0,)), ((), ())), preferred_element_type=jnp.float32
    )


def pad_rows(values, rows):
    return jnp.pad(values, ((0, rows - values.shape[0]), (0, 0)))


def pad_columns(values, columns):
    return jnp.pad(values, ((0, 0), (0, columns - values.shape[1])))


def norm_parts_of(values):
    average = jnp.mean(values, axis=1, keepdims=True)
    square = jnp.mean(values * values, axis=1, keepdims=True)
    inverse = lax.rsqrt(square - average * average + norm_epsilon)
    return ((values - average) * inverse, inverse)


def norm_backward(grad_out, plain, inverse, gain_row):
    scaled = grad_out * gain_row
    first = jnp.mean(scaled, axis=1, keepdims=True)
    second = jnp.mean(scaled * plain, axis=1, keepdims=True)
    return inverse * (scaled - first - plain * second)


def wide_dot(left_side, right_side, left_dim, right_dim):
    return lax.dot_general(
        left_side,
        right_side,
        (((left_dim,), (right_dim,)), ((), ())),
        preferred_element_type=jnp.float32,
    )


def in_vmem(count):
    return [pl.BlockSpec(memory_space=pltpu.VMEM)] * count


def kernel_call(body, inputs, outputs, scratch, flops, position=None):
    specs = in_vmem(len(inputs))
    operands = list(inputs)
    if position is not None:
        specs = [pl.BlockSpec(memory_space=pltpu.SMEM)] + specs
        operands = [position] + operands
    moved = sum(math.prod(o.shape) * o.dtype.itemsize for o in list(inputs) + list(outputs))
    return pl.pallas_call(
        body,
        out_shape=list(outputs),
        in_specs=specs,
        out_specs=in_vmem(len(outputs)),
        scratch_shapes=scratch,
        compiler_params=pltpu.CompilerParams(vmem_limit_bytes=40 * 1024 * 1024),
        cost_estimate=pl.CostEstimate(flops=flops, bytes_accessed=moved, transcendentals=0),
    )(*operands)


def put_chunks(position_ref, chunk_refs, whole_ref):
    chunk = chunk_refs[0].shape[0]
    for k, chunk_ref in enumerate(chunk_refs):
        start = pl.multiple_of((position_ref[0] ^ k) * chunk, 8)
        whole_ref[pl.ds(start, chunk), :] = chunk_ref[...].astype(jnp.float32)


def take_chunks(position_ref, whole_ref, chunk_refs):
    chunk = chunk_refs[0].shape[0]
    for k, chunk_ref in enumerate(chunk_refs):
        start = pl.multiple_of((position_ref[0] ^ k) * chunk, 8)
        chunk_ref[...] = whole_ref[pl.ds(start, chunk), :].astype(chunk_ref.dtype)


def keep_rows(values, tokens):
    rows = lax.broadcasted_iota(jnp.int32, values.shape, 0)
    return jnp.where(rows < tokens, values, jnp.zeros_like(values))


def head_probs(mixed, head, tokens):
    start = head * 3 * HD
    query = mixed[:, start : start + HD]
    key = mixed[:, start + HD : start + 2 * HD]
    value = mixed[:, start + 2 * HD : start + 3 * HD]
    scores = wide_dot(query, key, 1, 1) * HD ** (-0.5)
    columns = lax.broadcasted_iota(jnp.int32, scores.shape, 1)
    scores = jnp.where(columns < tokens, scores, -jnp.inf)
    exps = jnp.exp(scores - jnp.max(scores, axis=1, keepdims=True))
    probs = exps / jnp.sum(exps, axis=1, keepdims=True)
    return (query, key, value, probs)


def attend_kernel(tokens, heads, position, *refs):
    size = (len(refs) - 7) // 2
    chunks, (w_qkv, w_proj) = refs[:size], refs[size : size + 2]
    outs = refs[size + 2 : 2 * size + 2]
    mixed_out, normed_out, att_out, whole, att_all = refs[2 * size + 2 :]
    put_chunks(position, chunks, whole)
    normed = keep_rows(whole[...], tokens).astype(jnp.bfloat16)
    normed_out[...] = normed[: normed_out.shape[0]]
    mixed = wide_dot(normed, w_qkv[...], 1, 0).astype(jnp.bfloat16)
    mixed_out[...] = mixed
    for head in range(heads):
        _, _, value, probs = head_probs(mixed, head, tokens)
        att_all[:, head * HD : (head + 1) * HD] = wide_dot(probs.astype(jnp.bfloat16), value, 1, 0)
    attended = keep_rows(att_all[...], tokens).astype(jnp.bfloat16)
    att_out[...] = jnp.zeros_like(att_out)
    att_out[:, : heads * HD] = attended[: att_out.shape[0]]
    whole[...] = wide_dot(attended, w_proj[...], 1, 1)
    take_chunks(position, whole, outs)


def attend_back_kernel(tokens, heads, position, *refs):
    size = (len(refs) - 7) // 2
    chunks, (mixed_ref, w_qkv, w_proj) = refs[:size], refs[size : size + 3]
    outs = refs[size + 3 : 2 * size + 3]
    mixed_grad_out, back_out, whole, mixed_grad = refs[2 * size + 3 :]
    put_chunks(position, chunks, whole)
    back = whole[...].astype(jnp.bfloat16)
    back_out[...] = back[: back_out.shape[0]]
    att_grad = wide_dot(back, w_proj[...], 1, 0).astype(jnp.bfloat16)
    mixed = mixed_ref[...]
    scaling = HD ** (-0.5)
    for head in range(heads):
        query, key, value, probs = head_probs(mixed, head, tokens)
        grad = att_grad[:, head * HD : (head + 1) * HD]
        probs_grad = wide_dot(grad, value, 1, 1)
        inner = jnp.sum(probs * probs_grad, axis=1, keepdims=True)
        scores_grad = (probs * (probs_grad - inner)).astype(jnp.bfloat16)
        start = head * 3 * HD
        mixed_grad[:, start : start + HD] = wide_dot(scores_grad, key, 1, 0) * scaling
        mixed_grad[:, start + HD : start + 2 * HD] = wide_dot(scores_grad, query, 0, 0) * scaling
        mixed_grad[:, start + 2 * HD : start + 3 * HD] = wide_dot(
            probs.astype(jnp.bfloat16), grad, 0, 0
        )
    grads = mixed_grad[...].astype(jnp.bfloat16)
    mixed_grad_out[...] = jnp.zeros_like(mixed_grad_out)
    mixed_grad_out[:, : grads.shape[1]] = grads[: mixed_grad_out.shape[0]]
    whole[...] = wide_dot(grads, w_qkv[...], 1, 1)
    take_chunks(position, whole, outs)


def norm_kernel(level_index, first_row, size, *refs):
    parts, (stream_ref, norms) = refs[:size], refs[size : size + 2]
    stream_out, normed_out = refs[size + 2 :]
    stream = stream_ref[...]
    for part in parts:
        stream = stream + part[...].astype(jnp.float32)
    stream_out[...] = stream
    plain, _ = norm_parts_of(stream)
    gain = norms[level_index, first_row : first_row + 1, :]
    bias = norms[level_index, first_row + 1 : first_row + 2, :]
    normed_out[...] = (plain * gain + bias).astype(jnp.bfloat16)


def norm_back_kernel(level_index, first_row, size, *refs):
    parts, (stream_ref, change_ref, base_ref, norms) = refs[:size], refs[size : size + 4]
    change_out, low_out, sums_out = refs[size + 4 :]
    grad = parts[0][...].astype(jnp.float32)
    for part in parts[1:]:
        grad = grad + part[...].astype(jnp.float32)
    plain, inverse = norm_parts_of(stream_ref[...])
    gain = norms[level_index, first_row : first_row + 1, :]
    change = change_ref[...] + norm_backward(grad, plain, inverse, gain)
    change_out[...] = change
    low_out[...] = (base_ref[...].astype(jnp.float32) + change).astype(jnp.bfloat16)
    sums_out[0:1, :] = jnp.sum(grad * plain, axis=0, keepdims=True)
    sums_out[1:2, :] = jnp.sum(grad, axis=0, keepdims=True)


def first_kernel(tokens, position, blocks, norms, *refs):
    count = (len(refs) - 2) // 2
    outs, back_outs, stream_out, whole = refs[:count], refs[count:-2], refs[-2], refs[-1]
    size, _, width = blocks.shape
    width = width // 2
    whole[...] = jnp.zeros_like(whole)
    for i in range(size):
        whole[0:tokens, i * width : (i + 1) * width] = blocks[i, :, width:].astype(jnp.float32)
    take_chunks(position, whole, back_outs)
    for i in range(size):
        whole[0:tokens, i * width : (i + 1) * width] = blocks[i, :, :width].astype(jnp.float32)
    chunk = stream_out.shape[0]
    start = pl.multiple_of(position[0] * chunk, 8)
    stream_out[...] = whole[pl.ds(start, chunk), :]
    plain, _ = norm_parts_of(whole[...])
    whole[...] = plain * norms[0, 0:1, :] + norms[0, 1:2, :]
    take_chunks(position, whole, outs)


def mlp_kernel(tokens, position, *refs):
    size = (len(refs) - 6) // 2
    chunks, (w_up, w_down) = refs[:size], refs[size : size + 2]
    outs = refs[size + 2 : 2 * size + 2]
    slope_out, normed_out, act_out, whole = refs[2 * size + 2 :]
    put_chunks(position, chunks, whole)
    normed = keep_rows(whole[...], tokens).astype(jnp.bfloat16)
    normed_out[...] = normed[: normed_out.shape[0]]
    hidden = wide_dot(normed, w_up[...], 1, 0)
    below = 0.5 + 0.5 * lax.erf(hidden * math.sqrt(0.5))
    slope_out[...] = below + hidden * jnp.exp(-0.5 * hidden * hidden) * (
        1.0 / math.sqrt(2.0 * math.pi)
    )
    activated = keep_rows(hidden * below, tokens).astype(jnp.bfloat16)
    act_out[...] = activated[: act_out.shape[0]]
    whole[...] = wide_dot(activated, w_down[...], 1, 1)
    take_chunks(position, whole, outs)


def mlp_back_kernel(position, *refs):
    size = (len(refs) - 6) // 2
    chunks, (slope, w_up, w_down) = refs[:size], refs[size : size + 3]
    outs = refs[size + 3 : 2 * size + 3]
    hidden_grad_out, back_out, whole = refs[2 * size + 3 :]
    put_chunks(position, chunks, whole)
    back = whole[...].astype(jnp.bfloat16)
    back_out[...] = back[: back_out.shape[0]]
    hidden_grad = (wide_dot(back, w_down[...], 1, 0) * slope[...]).astype(jnp.bfloat16)
    hidden_grad_out[...] = hidden_grad[: hidden_grad_out.shape[0]]
    whole[...] = wide_dot(hidden_grad, w_up[...], 1, 1)
    take_chunks(position, whole, outs)


def swap_row_col(values):
    size = lax.axis_size("row")
    pairs = [(i * size + j, j * size + i) for i in range(size) for j in range(size)]
    return lax.ppermute(values, ("row", "col"), pairs)


def from_partner(values, step, axes=("dp", "row"), wanted=None):
    count = math.prod(lax.axis_size(a) for a in axes)
    pairs = [(i, i ^ step) for i in range(count) if wanted is None or wanted(i ^ step)]
    return lax.ppermute(values, axes, pairs)


def pick(stacked, index):
    return lax.dynamic_index_in_dim(stacked, index, 0, keepdims=False)


def placed_blocks(blocks, places):
    result = jnp.zeros((len(blocks),) + blocks[0].shape, blocks[0].dtype)
    for block, place in zip(blocks, places):
        result = lax.dynamic_update_index_in_dim(result, block, place, 0)
    return result


def gather_by_pairs(values, axis, first=None):
    step = lax.axis_size(axis) // 2
    me = lax.axis_index(axis)
    blocks, places = [values], [me]
    while step:
        sent = blocks[0][None] if len(blocks) == 1 else jnp.stack(blocks)
        received = from_partner(sent, step, (axis,)) if first is None else first
        first = None
        blocks = blocks + [received[i] for i in range(len(blocks))]
        places = places + [p ^ step for p in places]
        step //= 2
    return placed_blocks(blocks, places)


def sum_by_pairs(values, axis):
    step = 1
    while step < lax.axis_size(axis):
        values = values + from_partner(values, step, (axis,))
        step *= 2
    return values


def to_all(block, axis):
    size = lax.axis_size(axis)
    return lax.all_to_all(jnp.broadcast_to(block[None], (size,) + block.shape), axis, 0, 0)


def to_partners(chunk):
    size = lax.axis_size("col")
    return [chunk] + [from_partner(chunk, k, ("col",)) for k in range(1, size)]


def swap_parts(parts):
    return [parts[0]] + [from_partner(parts[k], k, ("col",)) for k in range(1, len(parts))]


def gram_strips(raw):
    size = lax.axis_size("col")
    third = raw.shape[0] // 3
    strips = [
        lax.dot_general(
            raw[i * third : (i + 1) * third],
            raw[i * third :],
            (((1,), (1,)), ((), ())),
            precision=lax.Precision.HIGH,
            preferred_element_type=jnp.float32,
        )
        for i in range(3)
    ]
    packed = jnp.concatenate(strips, axis=1)
    blocks = lax.all_to_all(packed.reshape(size, third // size, -1), "col", 0, 0)
    return jnp.sum(blocks, axis=0)


def halves(values):
    high = values.astype(jnp.bfloat16)
    return (high, (values - high.astype(jnp.float32)).astype(jnp.bfloat16))


def put_halves(refs, rows, columns, values):
    for ref, half in zip(refs, halves(values)):
        ref[rows, columns] = half


def dot_halves(left, rows, right, columns):
    left_high, left_low = left[0][rows, :], left[1][rows, :]
    right_high, right_low = right[0][:, columns], right[1][:, columns]
    return (
        wide_dot(left_high, right_high, 1, 0)
        + wide_dot(left_high, right_low, 1, 0)
        + wide_dot(left_low, right_high, 1, 0)
    )


def schulz_kernel(sweeps, packed, raw, out, gram, half, current, *pairs):
    gram_pair, square_pair, half_pair, current_pair = [pairs[i : i + 2] for i in range(0, 8, 2)]
    height = raw.shape[0]
    third = height // 3
    bands = [slice(i * third, (i + 1) * third) for i in range(3)]
    tails = [slice(i * third, height) for i in range(3)]
    everything = slice(0, height)

    def put_symmetric(pair, i, values):
        put_halves(pair, bands[i], tails[i], values)
        for j in range(i + 1, 3):
            block = values[:, (j - i) * third : (j - i + 1) * third]
            put_halves(pair, bands[j], bands[i], block.T)

    total = jnp.zeros((1, 1), jnp.float32)
    start = 0
    for i in range(3):
        strip = packed[:, start : start + height - i * third]
        start += height - i * third
        gram[bands[i], tails[i]] = strip
        rows = lax.broadcasted_iota(jnp.int32, (third, third), 0)
        columns = lax.broadcasted_iota(jnp.int32, (third, third), 1)
        diagonal = jnp.where(rows == columns, strip[:, :third], 0.0)
        total = total + jnp.sum(jnp.sum(diagonal, axis=1, keepdims=True), axis=0, keepdims=True)
    scale = 1.0 / (jnp.sqrt(total) + 1e-07)
    for i in range(3):
        values = gram[bands[i], tails[i]] * (scale * scale)
        gram[bands[i], tails[i]] = values
        put_symmetric(gram_pair, i, values)
        values = raw[bands[i], :] * scale
        current[bands[i], :] = values
        put_halves(current_pair, bands[i], everything, values)

    def sweep(index, carry):
        for i in range(3):
            product = dot_halves(gram_pair, bands[i], gram_pair, tails[i])
            square = schulz_second * gram[bands[i], tails[i]] + schulz_third * product
            put_symmetric(square_pair, i, square)
        for i in range(3):
            product = dot_halves(square_pair, bands[i], current_pair, everything)
            current[bands[i], :] = schulz_first * current[bands[i], :] + product

        @pl.when(index < sweeps - 1)
        def _():
            for i in range(3):
                put_halves(current_pair, bands[i], everything, current[bands[i], :])
                product = dot_halves(square_pair, bands[i], gram_pair, tails[i])
                values = schulz_first * gram[bands[i], tails[i]] + product
                half[bands[i], tails[i]] = values
                put_symmetric(half_pair, i, values)
            for i in range(3):
                product = dot_halves(square_pair, bands[i], half_pair, tails[i])
                values = schulz_first * half[bands[i], tails[i]] + product
                gram[bands[i], tails[i]] = values
                put_symmetric(gram_pair, i, values)

        return carry

    lax.fori_loop(0, sweeps, sweep, 0)
    out[...] = current[...].astype(out.dtype)


def schulz(raw, packed):
    height, width = raw.shape
    square_shape = (height, height)
    whole = [pltpu.VMEM(square_shape, jnp.float32)] * 2 + [pltpu.VMEM(raw.shape, jnp.float32)]
    pairs = [pltpu.VMEM(square_shape, jnp.bfloat16)] * 6 + [pltpu.VMEM(raw.shape, jnp.bfloat16)] * 2
    return kernel_call(
        functools.partial(schulz_kernel, 5),
        [packed, raw],
        [jax.ShapeDtypeStruct(raw.shape, jnp.bfloat16)],
        whole + pairs,
        2 * 3 * 14 * height * height * width,
    )[0]


def finish_kernel(levels, flipped, rates, blocks, *refs):
    olds, outs = refs[: len(flipped)], refs[len(flipped) :]
    for kind_index, turned in enumerate(flipped):
        old, new = olds[kind_index], outs[kind_index]
        width = old.shape[1] if turned else old.shape[2]
        for level_index in range(levels):
            block = blocks[kind_index * levels + level_index].astype(jnp.float32)[:, :width]
            block = block.T if turned else block
            if rates is None:
                outs[len(flipped) + kind_index][level_index] = block
                new[level_index] = moment_decay * old[level_index] + block
            else:
                new[level_index] = old[level_index] - rates[kind_index] * block


def on_device(
    residual_in,
    cotangent,
    qkv_weight,
    proj_weight,
    up_weight,
    down_weight,
    norm_params,
    qkv_moment,
    proj_moment,
    up_moment,
    down_moment,
    norm_moment,
):
    tokens, width_row = residual_in.shape
    row_size = lax.axis_size("row")
    col_size = lax.axis_size("col")
    dp_size = lax.axis_size("dp")
    model_width = width_row * row_size
    levels = qkv_weight.shape[0]
    jobs = levels * kinds
    chunk = -(-tokens // (8 * col_size)) * 8
    padded = chunk * col_size
    sent_rows = -(-tokens // 16) * 16
    me = (lax.axis_index("dp") * row_size + lax.axis_index("row")) % jobs
    my_row = lax.axis_index("row")
    my_chunk = lax.axis_index("col") * chunk

    weights = (qkv_weight, proj_weight, up_weight, down_weight)
    moments = (qkv_moment, proj_moment, up_moment, down_moment)
    flipped = (False, True, False, True)

    def upright(array, kind_index, level_index):
        block = array[level_index]
        return block.T if flipped[kind_index] else block

    widths = [
        w.shape[1] if flipped[k] else w.shape[2] for k, w in enumerate(weights)
    ]
    widest = max(widths)

    def own_weights(level_index, which):
        parts = [upright(weights[k], k, level_index).astype(jnp.bfloat16) for k in which]
        return jnp.concatenate(parts, axis=1)

    def gathered_weights(own, which, first):
        whole = gather_by_pairs(own, "row", first)
        whole = whole.reshape(model_width, -1)
        result = []
        start = 0
        for k in which:
            result.append(whole[:, start : start + widths[k]])
            start += widths[k]
        return result

    def features_first(blocks):
        return blocks.transpose(1, 0, 2).reshape(blocks.shape[1], model_width)

    all_norms = gather_by_pairs(norm_params, "row")
    all_norms = all_norms.transpose(1, 2, 0, 3).reshape(levels, kinds, model_width)
    both_inputs = jnp.concatenate([residual_in, cotangent.astype(residual_in.dtype)], axis=1)
    image_blocks = to_all(swap_row_col(both_inputs), "col")
    position = lax.axis_index("col").astype(jnp.int32).reshape(1)
    heads = widths[0] // (3 * HD)

    def shaped(rows, columns, kind):
        return jax.ShapeDtypeStruct((rows, columns), kind)

    low_chunk = shaped(chunk, model_width, jnp.bfloat16)
    full_chunk = shaped(chunk, model_width, jnp.float32)
    low_chunks = [low_chunk] * col_size
    sent = shaped(sent_rows, widest, jnp.bfloat16)
    sent_model = shaped(sent_rows, model_width, jnp.bfloat16)
    whole_scratch = pltpu.VMEM((padded, model_width), jnp.float32)
    attention_flops = 2 * padded * (
        model_width * (widths[0] + widths[1]) + 2 * padded * widths[1]
    )
    perceptron_flops = 2 * padded * model_width * (widths[2] + widths[3])
    chunk_flops = 20 * chunk * model_width

    def norm_step(parts, stream, level_index, first_row):
        return kernel_call(
            functools.partial(norm_kernel, level_index, first_row, len(parts)),
            [*parts, stream, all_norms],
            [full_chunk, low_chunk],
            [],
            chunk_flops,
        )

    def norm_back_step(parts, stream, change, level_index, first_row):
        return kernel_call(
            functools.partial(norm_back_kernel, level_index, first_row, len(parts)),
            [*parts, stream, change, back_base, all_norms],
            [full_chunk, low_chunk, shaped(2, model_width, jnp.float32)],
            [],
            chunk_flops,
        )

    *chunks, stream = kernel_call(
        functools.partial(first_kernel, tokens),
        [image_blocks, all_norms],
        low_chunks + low_chunks + [full_chunk],
        [whole_scratch],
        20 * padded * model_width,
        position,
    )
    chunks, back_chunks = chunks[:col_size], chunks[col_size:]
    back_base = back_chunks[0]
    groups = ((0, 1), (2, 3))

    def first_steps(own_groups):
        return [from_partner(own[None], row_size // 2, ("row",)) for own in own_groups]

    def weights_of(own_groups, firsts):
        parts = zip(own_groups, groups, firsts)
        return sum([gathered_weights(own, which, first) for own, which, first in parts], [])

    own_groups = [[own_weights(i, which) for which in groups] for i in range(levels)]
    weight_sets = [weights_of(own_groups[0], first_steps(own_groups[0]))] + [None] * (levels - 1)
    saved = []
    early = [None] * levels
    for level_index in range(levels):
        weight_qkv, weight_proj, weight_up, weight_down = weight_sets[level_index]
        stream_one = stream
        *parts, mixed, normed_one, attended = kernel_call(
            functools.partial(attend_kernel, tokens, heads),
            [*chunks, weight_qkv, weight_proj],
            low_chunks + [shaped(padded, widths[0], jnp.bfloat16), sent_model, sent],
            [whole_scratch, pltpu.VMEM((padded, widths[1]), jnp.float32)],
            attention_flops,
            position,
        )
        stream_two, normed = norm_step(swap_parts(parts), stream, level_index, 2)
        if level_index == 0:
            normed, own_groups[1:] = lax.optimization_barrier((normed, own_groups[1:]))
            later_firsts = [first_steps(own) for own in own_groups[1:]]
        chunks = to_partners(normed)
        *parts, slope, normed_two, activated = kernel_call(
            functools.partial(mlp_kernel, tokens),
            [*chunks, weight_up, weight_down],
            low_chunks + [shaped(padded, widths[2], jnp.float32), sent_model, sent],
            [whole_scratch],
            perceptron_flops,
            position,
        )
        if level_index == 0:
            parts, later_firsts = lax.optimization_barrier((parts, later_firsts))
            for later in range(1, levels):
                weight_sets[later] = weights_of(own_groups[later], later_firsts[later - 1])
        parts = swap_parts(parts)
        early[level_index] = (normed_one, attended, normed_two, activated)
        if level_index < levels - 1:
            stream, normed = norm_step(parts, stream_two, level_index + 1, 0)
            if level_index == 0:
                normed, late_me = lax.optimization_barrier((normed, me))
            chunks = to_partners(normed)
        else:
            stream = stream_two
            for part in parts:
                stream = stream + part.astype(jnp.float32)
        saved.append((stream_one, stream_two, mixed, slope))

    def sent_to_owners(values):
        blocks = jnp.stack(
            [v.reshape(chunk, col_size, width_row).transpose(1, 0, 2) for v in values], axis=1
        )
        col = lax.axis_index("col")
        return [pick(blocks, col)] + [
            from_partner(pick(blocks, col ^ k), k, ("col",)) for k in range(1, col_size)
        ]

    def placed(received):
        col = lax.axis_index("col")
        whole = placed_blocks(received, [col ^ k for k in range(col_size)]).transpose(1, 0, 2, 3)
        return swap_row_col(whole.reshape(whole.shape[0], padded, width_row)[:, :tokens])

    groups_of_jobs = dp_size * row_size // jobs

    def spread(parts_of_levels, arrival, kind_arrival):
        order = [(i, k) for i in arrival for k in kind_arrival]
        blocks = [parts_of_levels[i][k] for i, k in order]
        stack = placed_blocks(blocks, [k * levels + i for i, k in order])
        stack = jnp.concatenate([stack] * groups_of_jobs) if groups_of_jobs > 1 else stack
        return lax.all_to_all(stack, ("dp", "row"), 0, 0).reshape(-1, widest)

    upper = (late_me // row_size) % 2 == 1
    half = jobs // 2
    near_moments = []
    for j in range(half):
        low_job, high_job = [
            pad_columns(upright(moments[i // levels], i // levels, i % levels), widest)
            for i in (j, j + half)
        ]
        near_moments.append(jnp.where(upper, high_job, low_job))
    stacked_moment = jnp.stack(near_moments)
    own_moment = lax.all_to_all(stacked_moment, "row", 0, 0).reshape(model_width, widest)

    back_chunks, own_moment = lax.optimization_barrier((back_chunks, own_moment))
    change = jnp.zeros((chunk, model_width), jnp.float32)
    early_all = spread(early, range(levels), range(kinds))
    late = [None] * levels
    norm_sums = [None] * levels
    for level_index in reversed(range(levels)):
        weight_qkv, weight_proj, weight_up, weight_down = weight_sets[level_index]
        stream_one, stream_two, mixed, slope = saved[level_index]
        *parts, hidden_grad, back_two = kernel_call(
            mlp_back_kernel,
            [*back_chunks, slope, weight_up, weight_down],
            low_chunks + [sent, sent_model],
            [whole_scratch],
            perceptron_flops,
            position,
        )
        change, back_low, sums_two = norm_back_step(
            swap_parts(parts), stream_two, change, level_index, 2
        )
        if level_index == 0:
            back_low, early_all = lax.optimization_barrier((back_low, early_all))
        *parts, mixed_grad, back_one = kernel_call(
            functools.partial(attend_back_kernel, tokens, heads),
            [*to_partners(back_low), mixed, weight_qkv, weight_proj],
            low_chunks + [sent, sent_model],
            [whole_scratch, pltpu.VMEM((padded, widths[0]), jnp.float32)],
            3 * attention_flops,
            position,
        )
        late[level_index] = (mixed_grad, back_one, hidden_grad, back_two)
        if level_index == 0:
            late_all = spread(late, reversed(range(levels)), (3, 2, 1, 0))
        change, back_low, sums_one = norm_back_step(
            swap_parts(parts), stream_one, change, level_index, 0
        )
        norm_sums[level_index] = jnp.concatenate([sums_one, sums_two])

        if level_index:
            back_chunks = to_partners(back_low)

    norm_whole = sum_by_pairs(jnp.stack(norm_sums), "col")
    late_all, norm_whole, stream, change = lax.optimization_barrier(
        (late_all, norm_whole, stream, change)
    )

    turned = (me // levels) % 2 == 1
    model_side = jnp.where(turned, late_all, early_all)
    hidden_side = jnp.where(turned, early_all, late_all)
    own_grad = outer_grad(model_side, hidden_side)

    def returned(whole):
        blocks = whole.astype(jnp.bfloat16).reshape(row_size, width_row, widest)
        blocks = jnp.concatenate([blocks] * dp_size)
        return lax.all_to_all(blocks, ("dp", "row"), 0, 0)[:jobs]

    own_raw = moment_decay * own_moment + own_grad
    for axis in ("row", "dp"):
        norm_whole = sum_by_pairs(norm_whole, axis)
    own_strip, norm_whole = lax.optimization_barrier((gram_strips(own_raw), norm_whole))
    norm_grad = lax.dynamic_slice_in_dim(norm_whole, my_row * width_row, width_row, 2)
    norm_moment_new = moment_decay * norm_moment + norm_grad
    gram = to_all(own_strip, "col").reshape(-1, own_strip.shape[1])
    gram, own_grad, stream, change = lax.optimization_barrier((gram, own_grad, stream, change))
    tokens_moved = sent_to_owners([stream, change])
    grads = returned(own_grad)
    orth_whole, grads, tokens_moved = lax.optimization_barrier(
        (schulz(own_raw, gram), grads, tokens_moved)
    )
    block_output, change = placed(tokens_moved)
    input_grad = cotangent + change
    orths = returned(orth_whole)

    def finished(blocks, olds, rates):
        shapes = [jax.ShapeDtypeStruct(old.shape, jnp.float32) for old in olds]
        return kernel_call(
            functools.partial(finish_kernel, levels, flipped, rates),
            [blocks, *olds],
            shapes if rates else shapes + shapes,
            [],
            2 * sum(math.prod(old.shape) for old in olds),
        )

    moment_and_grad = finished(grads, moments, None)
    moment_outs, grad_outs = moment_and_grad[:kinds], moment_and_grad[kinds:]
    new_outs = finished(orths, weights, step_rates)

    tokens_all = tokens * col_size * dp_size
    norm_new = norm_params - norm_rate / math.sqrt(tokens_all) * norm_moment_new
    return (
        block_output,
        input_grad,
        *grad_outs,
        norm_grad,
        *moment_outs,
        norm_moment_new,
        *new_outs,
        norm_new,
    )


def solution(mesh):
    tokens_spec = P(("dp", "col"), "row")
    wide = P(None, "row", "col")
    tall = P(None, "col", "row")
    norms = P(None, None, "row")
    return jax.shard_map(
        on_device,
        mesh=mesh,
        in_specs=(tokens_spec, tokens_spec) + (wide, tall, wide, tall, norms) * 2,
        out_specs=(tokens_spec, tokens_spec) + (wide, tall, wide, tall, norms) * 3,
        check_vma=False,
    )
```

```python
import functools
import math

import jax
import jax.numpy as jnp
from jax import lax
from jax.experimental import pallas as pl
from jax.experimental.pallas import tpu as pltpu
from jax.sharding import PartitionSpec as P

HD = 64

norm_epsilon = 1e-06
moment_decay = 0.9
norm_rate = 0.05
step_rates = (1.7, 5.6, 2.0, 1.0)
schulz_first = 3.4445
schulz_second = -4.775
schulz_third = 2.0315
kinds = 4
strip_count = 6


def outer_grad(left_side, right_side):
    return lax.dot_general(
        left_side, right_side, (((0,), (0,)), ((), ())), preferred_element_type=jnp.float32
    )


def pad_rows(values, rows):
    return jnp.pad(values, ((0, rows - values.shape[0]), (0, 0)))


def pad_columns(values, columns):
    return jnp.pad(values, ((0, 0), (0, columns - values.shape[1])))


def norm_parts_of(values):
    average = jnp.mean(values, axis=1, keepdims=True)
    square = jnp.mean(values * values, axis=1, keepdims=True)
    inverse = lax.rsqrt(square - average * average + norm_epsilon)
    return ((values - average) * inverse, inverse)


def norm_backward(grad_out, plain, inverse, gain_row):
    scaled = grad_out * gain_row
    first = jnp.mean(scaled, axis=1, keepdims=True)
    second = jnp.mean(scaled * plain, axis=1, keepdims=True)
    return inverse * (scaled - first - plain * second)


def wide_dot(left_side, right_side, left_dim, right_dim):
    return lax.dot_general(
        left_side,
        right_side,
        (((left_dim,), (right_dim,)), ((), ())),
        preferred_element_type=jnp.float32,
    )


def in_vmem(count):
    return [pl.BlockSpec(memory_space=pltpu.VMEM)] * count


def kernel_call(body, inputs, outputs, scratch, flops, position=None):
    specs = in_vmem(len(inputs))
    operands = list(inputs)
    if position is not None:
        specs = [pl.BlockSpec(memory_space=pltpu.SMEM)] + specs
        operands = [position] + operands
    moved = sum(math.prod(o.shape) * o.dtype.itemsize for o in list(inputs) + list(outputs))
    return pl.pallas_call(
        body,
        out_shape=list(outputs),
        in_specs=specs,
        out_specs=in_vmem(len(outputs)),
        scratch_shapes=scratch,
        compiler_params=pltpu.CompilerParams(vmem_limit_bytes=40 * 1024 * 1024),
        cost_estimate=pl.CostEstimate(flops=flops, bytes_accessed=moved, transcendentals=0),
    )(*operands)


def put_chunks(position_ref, chunk_refs, whole_ref):
    chunk = chunk_refs[0].shape[0]
    for k, chunk_ref in enumerate(chunk_refs):
        start = pl.multiple_of((position_ref[0] ^ k) * chunk, 8)
        whole_ref[pl.ds(start, chunk), :] = chunk_ref[...].astype(jnp.float32)


def take_chunks(position_ref, whole_ref, chunk_refs):
    chunk = chunk_refs[0].shape[0]
    for k, chunk_ref in enumerate(chunk_refs):
        start = pl.multiple_of((position_ref[0] ^ k) * chunk, 8)
        chunk_ref[...] = whole_ref[pl.ds(start, chunk), :].astype(chunk_ref.dtype)


def keep_rows(values, tokens):
    rows = lax.broadcasted_iota(jnp.int32, values.shape, 0)
    return jnp.where(rows < tokens, values, jnp.zeros_like(values))


def head_probs(mixed, head, tokens):
    start = head * 3 * HD
    query = mixed[:, start : start + HD]
    key = mixed[:, start + HD : start + 2 * HD]
    value = mixed[:, start + 2 * HD : start + 3 * HD]
    scores = wide_dot(query, key, 1, 1) * HD ** (-0.5)
    columns = lax.broadcasted_iota(jnp.int32, scores.shape, 1)
    scores = jnp.where(columns < tokens, scores, -jnp.inf)
    exps = jnp.exp(scores - jnp.max(scores, axis=1, keepdims=True))
    probs = exps / jnp.sum(exps, axis=1, keepdims=True)
    return (query, key, value, probs)


def attend_kernel(tokens, heads, position, *refs):
    size = (len(refs) - 7) // 2
    chunks, (w_qkv, w_proj) = refs[:size], refs[size : size + 2]
    outs = refs[size + 2 : 2 * size + 2]
    mixed_out, normed_out, att_out, whole, att_all = refs[2 * size + 2 :]
    put_chunks(position, chunks, whole)
    normed = keep_rows(whole[...], tokens).astype(jnp.bfloat16)
    normed_out[...] = normed[: normed_out.shape[0]]
    mixed = wide_dot(normed, w_qkv[...], 1, 0).astype(jnp.bfloat16)
    mixed_out[...] = mixed
    for head in range(heads):
        _, _, value, probs = head_probs(mixed, head, tokens)
        att_all[:, head * HD : (head + 1) * HD] = wide_dot(probs.astype(jnp.bfloat16), value, 1, 0)
    attended = keep_rows(att_all[...], tokens).astype(jnp.bfloat16)
    att_out[...] = jnp.zeros_like(att_out)
    att_out[:, : heads * HD] = attended[: att_out.shape[0]]
    whole[...] = wide_dot(attended, w_proj[...], 1, 1)
    take_chunks(position, whole, outs)


def attend_back_kernel(tokens, heads, position, *refs):
    size = (len(refs) - 7) // 2
    chunks, (mixed_ref, w_qkv, w_proj) = refs[:size], refs[size : size + 3]
    outs = refs[size + 3 : 2 * size + 3]
    mixed_grad_out, back_out, whole, mixed_grad = refs[2 * size + 3 :]
    put_chunks(position, chunks, whole)
    back = whole[...].astype(jnp.bfloat16)
    back_out[...] = back[: back_out.shape[0]]
    att_grad = wide_dot(back, w_proj[...], 1, 0).astype(jnp.bfloat16)
    mixed = mixed_ref[...]
    scaling = HD ** (-0.5)
    for head in range(heads):
        query, key, value, probs = head_probs(mixed, head, tokens)
        grad = att_grad[:, head * HD : (head + 1) * HD]
        probs_grad = wide_dot(grad, value, 1, 1)
        inner = jnp.sum(probs * probs_grad, axis=1, keepdims=True)
        scores_grad = (probs * (probs_grad - inner)).astype(jnp.bfloat16)
        start = head * 3 * HD
        mixed_grad[:, start : start + HD] = wide_dot(scores_grad, key, 1, 0) * scaling
        mixed_grad[:, start + HD : start + 2 * HD] = wide_dot(scores_grad, query, 0, 0) * scaling
        mixed_grad[:, start + 2 * HD : start + 3 * HD] = wide_dot(
            probs.astype(jnp.bfloat16), grad, 0, 0
        )
    grads = mixed_grad[...].astype(jnp.bfloat16)
    mixed_grad_out[...] = jnp.zeros_like(mixed_grad_out)
    mixed_grad_out[:, : grads.shape[1]] = grads[: mixed_grad_out.shape[0]]
    whole[...] = wide_dot(grads, w_qkv[...], 1, 1)
    take_chunks(position, whole, outs)


def norm_kernel(level_index, first_row, size, *refs):
    parts, (stream_ref, norms) = refs[:size], refs[size : size + 2]
    stream_out, normed_out = refs[size + 2 :]
    stream = stream_ref[...]
    for part in parts:
        stream = stream + part[...].astype(jnp.float32)
    stream_out[...] = stream
    plain, _ = norm_parts_of(stream)
    gain = norms[level_index, first_row : first_row + 1, :]
    bias = norms[level_index, first_row + 1 : first_row + 2, :]
    normed_out[...] = (plain * gain + bias).astype(jnp.bfloat16)


def norm_back_kernel(level_index, first_row, size, *refs):
    parts, (stream_ref, change_ref, base_ref, norms) = refs[:size], refs[size : size + 4]
    change_out, low_out, sums_out = refs[size + 4 :]
    grad = parts[0][...].astype(jnp.float32)
    for part in parts[1:]:
        grad = grad + part[...].astype(jnp.float32)
    plain, inverse = norm_parts_of(stream_ref[...])
    gain = norms[level_index, first_row : first_row + 1, :]
    change = change_ref[...] + norm_backward(grad, plain, inverse, gain)
    change_out[...] = change
    low_out[...] = (base_ref[...].astype(jnp.float32) + change).astype(jnp.bfloat16)
    sums_out[0:1, :] = jnp.sum(grad * plain, axis=0, keepdims=True)
    sums_out[1:2, :] = jnp.sum(grad, axis=0, keepdims=True)


def first_kernel(tokens, position, blocks, norms, *refs):
    count = (len(refs) - 2) // 2
    outs, back_outs, stream_out, whole = refs[:count], refs[count:-2], refs[-2], refs[-1]
    size, _, width = blocks.shape
    width = width // 2
    whole[...] = jnp.zeros_like(whole)
    for i in range(size):
        whole[0:tokens, i * width : (i + 1) * width] = blocks[i, :, width:].astype(jnp.float32)
    take_chunks(position, whole, back_outs)
    for i in range(size):
        whole[0:tokens, i * width : (i + 1) * width] = blocks[i, :, :width].astype(jnp.float32)
    chunk = stream_out.shape[0]
    start = pl.multiple_of(position[0] * chunk, 8)
    stream_out[...] = whole[pl.ds(start, chunk), :]
    plain, _ = norm_parts_of(whole[...])
    whole[...] = plain * norms[0, 0:1, :] + norms[0, 1:2, :]
    take_chunks(position, whole, outs)


def mlp_kernel(tokens, position, *refs):
    size = (len(refs) - 6) // 2
    chunks, (w_up, w_down) = refs[:size], refs[size : size + 2]
    outs = refs[size + 2 : 2 * size + 2]
    slope_out, normed_out, act_out, whole = refs[2 * size + 2 :]
    put_chunks(position, chunks, whole)
    normed = keep_rows(whole[...], tokens).astype(jnp.bfloat16)
    normed_out[...] = normed[: normed_out.shape[0]]
    hidden = wide_dot(normed, w_up[...], 1, 0)
    below = 0.5 + 0.5 * lax.erf(hidden * math.sqrt(0.5))
    slope_out[...] = below + hidden * jnp.exp(-0.5 * hidden * hidden) * (
        1.0 / math.sqrt(2.0 * math.pi)
    )
    activated = keep_rows(hidden * below, tokens).astype(jnp.bfloat16)
    act_out[...] = activated[: act_out.shape[0]]
    whole[...] = wide_dot(activated, w_down[...], 1, 1)
    take_chunks(position, whole, outs)


def mlp_back_kernel(position, *refs):
    size = (len(refs) - 6) // 2
    chunks, (slope, w_up, w_down) = refs[:size], refs[size : size + 3]
    outs = refs[size + 3 : 2 * size + 3]
    hidden_grad_out, back_out, whole = refs[2 * size + 3 :]
    put_chunks(position, chunks, whole)
    back = whole[...].astype(jnp.bfloat16)
    back_out[...] = back[: back_out.shape[0]]
    hidden_grad = (wide_dot(back, w_down[...], 1, 0) * slope[...]).astype(jnp.bfloat16)
    hidden_grad_out[...] = hidden_grad[: hidden_grad_out.shape[0]]
    whole[...] = wide_dot(hidden_grad, w_up[...], 1, 1)
    take_chunks(position, whole, outs)


def swap_row_col(values):
    size = lax.axis_size("row")
    pairs = [(i * size + j, j * size + i) for i in range(size) for j in range(size)]
    return lax.ppermute(values, ("row", "col"), pairs)


def from_partner(values, step, axes=("dp", "row"), wanted=None):
    count = math.prod(lax.axis_size(a) for a in axes)
    pairs = [(i, i ^ step) for i in range(count) if wanted is None or wanted(i ^ step)]
    return lax.ppermute(values, axes, pairs)


def pick(stacked, index):
    return lax.dynamic_index_in_dim(stacked, index, 0, keepdims=False)


def placed_blocks(blocks, places):
    result = jnp.zeros((len(blocks),) + blocks[0].shape, blocks[0].dtype)
    for block, place in zip(blocks, places):
        result = lax.dynamic_update_index_in_dim(result, block, place, 0)
    return result


def gather_by_pairs(values, axis, first=None):
    step = lax.axis_size(axis) // 2
    me = lax.axis_index(axis)
    blocks, places = [values], [me]
    while step:
        sent = blocks[0][None] if len(blocks) == 1 else jnp.stack(blocks)
        received = from_partner(sent, step, (axis,)) if first is None else first
        first = None
        blocks = blocks + [received[i] for i in range(len(blocks))]
        places = places + [p ^ step for p in places]
        step //= 2
    return placed_blocks(blocks, places)


def sum_by_pairs(values, axis):
    step = 1
    while step < lax.axis_size(axis):
        values = values + from_partner(values, step, (axis,))
        step *= 2
    return values


def to_all(block, axis):
    size = lax.axis_size(axis)
    return lax.all_to_all(jnp.broadcast_to(block[None], (size,) + block.shape), axis, 0, 0)


def to_partners(chunk):
    size = lax.axis_size("col")
    return [chunk] + [from_partner(chunk, k, ("col",)) for k in range(1, size)]


def swap_parts(parts):
    return [parts[0]] + [from_partner(parts[k], k, ("col",)) for k in range(1, len(parts))]


def gram_strips(raw):
    size = lax.axis_size("col")
    height = raw.shape[0]
    count = strip_count
    band = height // count
    strips = [
        lax.dot_general(
            raw[i * band : (i + 1) * band],
            raw[i * band :],
            (((1,), (1,)), ((), ())),
            precision=lax.Precision.HIGH,
            preferred_element_type=jnp.float32,
        )
        for i in range(count)
    ]
    packed = jnp.concatenate(strips, axis=1)
    blocks = lax.all_to_all(packed.reshape(size, band // size, -1), "col", 0, 0)
    return jnp.sum(blocks, axis=0)


def halves(values):
    high = values.astype(jnp.bfloat16)
    return (high, (values - high.astype(jnp.float32)).astype(jnp.bfloat16))


def put_halves(refs, rows, columns, values):
    for ref, half in zip(refs, halves(values)):
        ref[rows, columns] = half


def dot_halves(left, rows, right, columns):
    left_high, left_low = left[0][rows, :], left[1][rows, :]
    right_high, right_low = right[0][:, columns], right[1][:, columns]
    return (
        wide_dot(left_high, right_high, 1, 0)
        + wide_dot(left_high, right_low, 1, 0)
        + wide_dot(left_low, right_high, 1, 0)
    )


def schulz_kernel(sweeps, packed, raw, out, gram, half, current, *pairs):
    gram_pair, square_pair, half_pair, current_pair = [pairs[i : i + 2] for i in range(0, 8, 2)]
    height = raw.shape[0]
    third = height // 3
    bands = [slice(i * third, (i + 1) * third) for i in range(3)]
    tails = [slice(i * third, height) for i in range(3)]
    everything = slice(0, height)

    def put_symmetric(pair, i, values):
        put_halves(pair, bands[i], tails[i], values)
        for j in range(i + 1, 3):
            block = values[:, (j - i) * third : (j - i + 1) * third]
            put_halves(pair, bands[j], bands[i], block.T)

    total = jnp.zeros((1, 1), jnp.float32)
    start = 0
    band = height // strip_count
    for i in range(strip_count):
        strip = packed[:, start : start + height - i * band]
        start += height - i * band
        gram[i * band : (i + 1) * band, i * band :] = strip
        if i % 2 == 0:
            gram[(i + 1) * band : (i + 2) * band, i * band : (i + 1) * band] = strip[
                :, band : 2 * band
            ].T
        rows = lax.broadcasted_iota(jnp.int32, (band, band), 0)
        columns = lax.broadcasted_iota(jnp.int32, (band, band), 1)
        diagonal = jnp.where(rows == columns, strip[:, :band], 0.0)
        total = total + jnp.sum(jnp.sum(diagonal, axis=1, keepdims=True), axis=0, keepdims=True)
    scale = 1.0 / (jnp.sqrt(total) + 1e-07)
    for i in range(3):
        values = gram[bands[i], tails[i]] * (scale * scale)
        gram[bands[i], tails[i]] = values
        put_symmetric(gram_pair, i, values)
        values = raw[bands[i], :] * scale
        current[bands[i], :] = values
        put_halves(current_pair, bands[i], everything, values)

    def sweep(index, carry):
        for i in range(3):
            product = dot_halves(gram_pair, bands[i], gram_pair, tails[i])
            square = schulz_second * gram[bands[i], tails[i]] + schulz_third * product
            put_symmetric(square_pair, i, square)
        for i in range(3):
            product = dot_halves(square_pair, bands[i], current_pair, everything)
            current[bands[i], :] = schulz_first * current[bands[i], :] + product

        @pl.when(index < sweeps - 1)
        def _():
            for i in range(3):
                put_halves(current_pair, bands[i], everything, current[bands[i], :])
                product = dot_halves(square_pair, bands[i], gram_pair, tails[i])
                values = schulz_first * gram[bands[i], tails[i]] + product
                half[bands[i], tails[i]] = values
                put_symmetric(half_pair, i, values)
            for i in range(3):
                product = dot_halves(square_pair, bands[i], half_pair, tails[i])
                values = schulz_first * half[bands[i], tails[i]] + product
                gram[bands[i], tails[i]] = values
                put_symmetric(gram_pair, i, values)

        return carry

    lax.fori_loop(0, sweeps, sweep, 0)
    out[...] = current[...].astype(out.dtype)


def schulz(raw, packed):
    height, width = raw.shape
    square_shape = (height, height)
    whole = [pltpu.VMEM(square_shape, jnp.float32)] * 2 + [pltpu.VMEM(raw.shape, jnp.float32)]
    pairs = [pltpu.VMEM(square_shape, jnp.bfloat16)] * 6 + [pltpu.VMEM(raw.shape, jnp.bfloat16)] * 2
    return kernel_call(
        functools.partial(schulz_kernel, 5),
        [packed, raw],
        [jax.ShapeDtypeStruct(raw.shape, jnp.bfloat16)],
        whole + pairs,
        2 * 3 * 14 * height * height * width,
    )[0]


def finish_kernel(levels, flipped, rates, blocks, *refs):
    olds, outs = refs[: len(flipped)], refs[len(flipped) :]
    for kind_index, turned in enumerate(flipped):
        old, new = olds[kind_index], outs[kind_index]
        width = old.shape[1] if turned else old.shape[2]
        for level_index in range(levels):
            block = blocks[kind_index * levels + level_index].astype(jnp.float32)[:, :width]
            block = block.T if turned else block
            if rates is None:
                outs[len(flipped) + kind_index][level_index] = block
                new[level_index] = moment_decay * old[level_index] + block
            else:
                new[level_index] = old[level_index] - rates[kind_index] * block


def on_device(
    residual_in,
    cotangent,
    qkv_weight,
    proj_weight,
    up_weight,
    down_weight,
    norm_params,
    qkv_moment,
    proj_moment,
    up_moment,
    down_moment,
    norm_moment,
):
    tokens, width_row = residual_in.shape
    row_size = lax.axis_size("row")
    col_size = lax.axis_size("col")
    dp_size = lax.axis_size("dp")
    model_width = width_row * row_size
    levels = qkv_weight.shape[0]
    jobs = levels * kinds
    chunk = -(-tokens // (8 * col_size)) * 8
    padded = chunk * col_size
    sent_rows = -(-tokens // 16) * 16
    me = (lax.axis_index("dp") * row_size + lax.axis_index("row")) % jobs
    my_row = lax.axis_index("row")
    my_chunk = lax.axis_index("col") * chunk

    weights = (qkv_weight, proj_weight, up_weight, down_weight)
    moments = (qkv_moment, proj_moment, up_moment, down_moment)
    flipped = (False, True, False, True)

    def upright(array, kind_index, level_index):
        block = array[level_index]
        return block.T if flipped[kind_index] else block

    widths = [
        w.shape[1] if flipped[k] else w.shape[2] for k, w in enumerate(weights)
    ]
    widest = max(widths)

    def own_weights(level_index, which):
        parts = [upright(weights[k], k, level_index).astype(jnp.bfloat16) for k in which]
        return jnp.concatenate(parts, axis=1)

    def gathered_weights(own, which, first):
        whole = gather_by_pairs(own, "row", first)
        whole = whole.reshape(model_width, -1)
        result = []
        start = 0
        for k in which:
            result.append(whole[:, start : start + widths[k]])
            start += widths[k]
        return result

    def features_first(blocks):
        return blocks.transpose(1, 0, 2).reshape(blocks.shape[1], model_width)

    all_norms = gather_by_pairs(norm_params, "row")
    all_norms = all_norms.transpose(1, 2, 0, 3).reshape(levels, kinds, model_width)
    both_inputs = jnp.concatenate([residual_in, cotangent.astype(residual_in.dtype)], axis=1)
    image_blocks = to_all(swap_row_col(both_inputs), "col")
    position = lax.axis_index("col").astype(jnp.int32).reshape(1)
    heads = widths[0] // (3 * HD)

    def shaped(rows, columns, kind):
        return jax.ShapeDtypeStruct((rows, columns), kind)

    low_chunk = shaped(chunk, model_width, jnp.bfloat16)
    full_chunk = shaped(chunk, model_width, jnp.float32)
    low_chunks = [low_chunk] * col_size
    sent = shaped(sent_rows, widest, jnp.bfloat16)
    sent_model = shaped(sent_rows, model_width, jnp.bfloat16)
    whole_scratch = pltpu.VMEM((padded, model_width), jnp.float32)
    attention_flops = 2 * padded * (
        model_width * (widths[0] + widths[1]) + 2 * padded * widths[1]
    )
    perceptron_flops = 2 * padded * model_width * (widths[2] + widths[3])
    chunk_flops = 20 * chunk * model_width

    def norm_step(parts, stream, level_index, first_row):
        return kernel_call(
            functools.partial(norm_kernel, level_index, first_row, len(parts)),
            [*parts, stream, all_norms],
            [full_chunk, low_chunk],
            [],
            chunk_flops,
        )

    def norm_back_step(parts, stream, change, level_index, first_row):
        return kernel_call(
            functools.partial(norm_back_kernel, level_index, first_row, len(parts)),
            [*parts, stream, change, back_base, all_norms],
            [full_chunk, low_chunk, shaped(2, model_width, jnp.float32)],
            [],
            chunk_flops,
        )

    *chunks, stream = kernel_call(
        functools.partial(first_kernel, tokens),
        [image_blocks, all_norms],
        low_chunks + low_chunks + [full_chunk],
        [whole_scratch],
        20 * padded * model_width,
        position,
    )
    chunks, back_chunks = chunks[:col_size], chunks[col_size:]
    back_base = back_chunks[0]
    groups = ((0, 1), (2, 3))

    def first_steps(own_groups):
        return [from_partner(own[None], row_size // 2, ("row",)) for own in own_groups]

    def weights_of(own_groups, firsts):
        parts = zip(own_groups, groups, firsts)
        return sum([gathered_weights(own, which, first) for own, which, first in parts], [])

    own_groups = [[own_weights(i, which) for which in groups] for i in range(levels)]
    weight_sets = [weights_of(own_groups[0], first_steps(own_groups[0]))] + [None] * (levels - 1)
    saved = []
    early = [None] * levels
    for level_index in range(levels):
        weight_qkv, weight_proj = weight_sets[level_index][:2]
        if level_index == 0:
            weight_up, weight_down = weight_sets[0][2:]
        stream_one = stream
        *parts, mixed, normed_one, attended = kernel_call(
            functools.partial(attend_kernel, tokens, heads),
            [*chunks, weight_qkv, weight_proj],
            low_chunks + [shaped(padded, widths[0], jnp.bfloat16), sent_model, sent],
            [whole_scratch, pltpu.VMEM((padded, widths[1]), jnp.float32)],
            attention_flops,
            position,
        )
        if level_index == 1:
            parts, arrived = lax.optimization_barrier((parts, [f[1] for f in later_firsts]))
            for later, first in enumerate(arrived, 1):
                weight_sets[later] += gathered_weights(own_groups[later][1], groups[1], first)
            weight_up, weight_down = weight_sets[level_index][2:]
        stream_two, normed = norm_step(swap_parts(parts), stream, level_index, 2)
        if level_index == 0:
            normed, own_groups[1:] = lax.optimization_barrier((normed, own_groups[1:]))
            later_firsts = [first_steps(own) for own in own_groups[1:]]
        chunks = to_partners(normed)
        *parts, slope, normed_two, activated = kernel_call(
            functools.partial(mlp_kernel, tokens),
            [*chunks, weight_up, weight_down],
            low_chunks + [shaped(padded, widths[2], jnp.float32), sent_model, sent],
            [whole_scratch],
            perceptron_flops,
            position,
        )
        if level_index == 0:
            parts, arrived = lax.optimization_barrier((parts, [f[0] for f in later_firsts]))
            for later, first in enumerate(arrived, 1):
                weight_sets[later] = gathered_weights(own_groups[later][0], groups[0], first)
        parts = swap_parts(parts)
        early[level_index] = (normed_one, attended, normed_two, activated)
        if level_index < levels - 1:
            stream, normed = norm_step(parts, stream_two, level_index + 1, 0)
            if level_index == 0:
                normed, late_me = lax.optimization_barrier((normed, me))
            chunks = to_partners(normed)
        else:
            stream = stream_two
            for part in parts:
                stream = stream + part.astype(jnp.float32)
        saved.append((stream_one, stream_two, mixed, slope))

    def blocks_for_owners(values):
        blocks = jnp.stack(
            [v.reshape(chunk, col_size, width_row).transpose(1, 0, 2) for v in values], axis=1
        )
        col = lax.axis_index("col")
        return [pick(blocks, col ^ k) for k in range(col_size)]

    def placed(received):
        col = lax.axis_index("col")
        whole = placed_blocks(received, [col ^ k for k in range(col_size)]).transpose(1, 0, 2, 3)
        return swap_row_col(whole.reshape(whole.shape[0], padded, width_row)[:, :tokens])

    groups_of_jobs = dp_size * row_size // jobs

    def spread(parts_of_levels, arrival, kind_arrival):
        order = [(i, k) for i in arrival for k in kind_arrival]
        blocks = [parts_of_levels[i][k] for i, k in order]
        stack = placed_blocks(blocks, [k * levels + i for i, k in order])
        stack = jnp.concatenate([stack] * groups_of_jobs) if groups_of_jobs > 1 else stack
        return lax.all_to_all(stack, ("dp", "row"), 0, 0).reshape(-1, widest)

    upper = (late_me // row_size) % 2 == 1
    half = jobs // 2
    near_moments = []
    for j in range(half):
        low_job, high_job = [
            pad_columns(upright(moments[i // levels], i // levels, i % levels), widest)
            for i in (j, j + half)
        ]
        near_moments.append(jnp.where(upper, high_job, low_job))
    stacked_moment = jnp.stack(near_moments)
    own_moment = lax.all_to_all(stacked_moment, "row", 0, 0).reshape(model_width, widest)

    back_chunks, own_moment = lax.optimization_barrier((back_chunks, own_moment))
    change = jnp.zeros((chunk, model_width), jnp.float32)
    early_all = spread(early, range(levels), range(kinds))
    late = [None] * levels
    norm_sums = [None] * levels
    for level_index in reversed(range(levels)):
        weight_qkv, weight_proj, weight_up, weight_down = weight_sets[level_index]
        stream_one, stream_two, mixed, slope = saved[level_index]
        *parts, hidden_grad, back_two = kernel_call(
            mlp_back_kernel,
            [*back_chunks, slope, weight_up, weight_down],
            low_chunks + [sent, sent_model],
            [whole_scratch],
            perceptron_flops,
            position,
        )
        change, back_low, sums_two = norm_back_step(
            swap_parts(parts), stream_two, change, level_index, 2
        )
        if level_index == 0:
            back_low, early_all = lax.optimization_barrier((back_low, early_all))
        *parts, mixed_grad, back_one = kernel_call(
            functools.partial(attend_back_kernel, tokens, heads),
            [*to_partners(back_low), mixed, weight_qkv, weight_proj],
            low_chunks + [sent, sent_model],
            [whole_scratch, pltpu.VMEM((padded, widths[0]), jnp.float32)],
            3 * attention_flops,
            position,
        )
        late[level_index] = (mixed_grad, back_one, hidden_grad, back_two)
        if level_index == 0:
            late_all = spread(late, reversed(range(levels)), (3, 2, 1, 0))
        change, back_low, sums_one = norm_back_step(
            swap_parts(parts), stream_one, change, level_index, 0
        )
        norm_sums[level_index] = jnp.concatenate([sums_one, sums_two])

        if level_index:
            back_chunks = to_partners(back_low)

    norm_whole = sum_by_pairs(jnp.stack(norm_sums), "col")
    late_all, norm_whole, stream, change = lax.optimization_barrier(
        (late_all, norm_whole, stream, change)
    )

    turned = (me // levels) % 2 == 1
    model_side = jnp.where(turned, late_all, early_all)
    hidden_side = jnp.where(turned, early_all, late_all)
    own_grad = outer_grad(model_side, hidden_side)

    def blocks_to_return(whole):
        blocks = whole.astype(jnp.bfloat16).reshape(row_size, width_row, widest)
        return jnp.concatenate([blocks] * dp_size)

    def returned(blocks):
        return lax.all_to_all(blocks, ("dp", "row"), 0, 0)[:jobs]

    own_raw = moment_decay * own_moment + own_grad
    for axis in ("row", "dp"):
        norm_whole = sum_by_pairs(norm_whole, axis)
    tokens_moved = blocks_for_owners([stream, change])
    grad_blocks = blocks_to_return(own_grad)
    own_strip, norm_whole, tokens_moved, grad_blocks = lax.optimization_barrier(
        (gram_strips(own_raw), norm_whole, tokens_moved, grad_blocks)
    )
    norm_grad = lax.dynamic_slice_in_dim(norm_whole, my_row * width_row, width_row, 2)
    norm_moment_new = moment_decay * norm_moment + norm_grad
    gram = to_all(own_strip, "col").reshape(-1, own_strip.shape[1])
    gram, tokens_moved, grad_blocks = lax.optimization_barrier((gram, tokens_moved, grad_blocks))
    tokens_moved = swap_parts(tokens_moved)
    grads = returned(grad_blocks)
    orth_whole, grads, tokens_moved = lax.optimization_barrier(
        (schulz(own_raw, gram), grads, tokens_moved)
    )
    block_output, change = placed(tokens_moved)
    input_grad = cotangent + change
    orths = returned(blocks_to_return(orth_whole))

    def finished(blocks, olds, rates):
        tall = [f and old.shape[1] > old.shape[2] for f, old in zip(flipped, olds)]
        olds = [old.swapaxes(1, 2) if t else old for t, old in zip(tall, olds)]
        turned = tuple(f and not t for f, t in zip(flipped, tall))
        shapes = [jax.ShapeDtypeStruct(old.shape, jnp.float32) for old in olds]
        outs = kernel_call(
            functools.partial(finish_kernel, levels, turned, rates),
            [blocks, *olds],
            shapes if rates else shapes + shapes,
            [],
            2 * sum(math.prod(old.shape) for old in olds),
        )
        return [out.swapaxes(1, 2) if tall[i % kinds] else out for i, out in enumerate(outs)]

    moment_and_grad = finished(grads, moments, None)
    moment_outs, grad_outs = moment_and_grad[:kinds], moment_and_grad[kinds:]
    new_outs = finished(orths, weights, step_rates)

    tokens_all = tokens * col_size * dp_size
    norm_new = norm_params - norm_rate / math.sqrt(tokens_all) * norm_moment_new
    return (
        block_output,
        input_grad,
        *grad_outs,
        norm_grad,
        *moment_outs,
        norm_moment_new,
        *new_outs,
        norm_new,
    )


def solution(mesh):
    tokens_spec = P(("dp", "col"), "row")
    wide = P(None, "row", "col")
    tall = P(None, "col", "row")
    norms = P(None, None, "row")
    return jax.shard_map(
        on_device,
        mesh=mesh,
        in_specs=(tokens_spec, tokens_spec) + (wide, tall, wide, tall, norms) * 2,
        out_specs=(tokens_spec, tokens_spec) + (wide, tall, wide, tall, norms) * 3,
        check_vma=False,
    )
```

```python
import functools
import math

import jax
import jax.numpy as jnp
from jax import lax
from jax.experimental import pallas as pl
from jax.experimental.pallas import tpu as pltpu
from jax.sharding import PartitionSpec as P

HD = 64

norm_epsilon = 1e-06
moment_decay = 0.9
norm_rate = 0.05
step_rates = (1.7, 5.6, 2.0, 1.0)
schulz_first = 3.4445
schulz_second = -4.775
schulz_third = 2.0315
kinds = 4
strip_count = 6


def outer_grad(left_side, right_side):
    return lax.dot_general(
        left_side, right_side, (((0,), (0,)), ((), ())), preferred_element_type=jnp.float32
    )


def pad_rows(values, rows):
    return jnp.pad(values, ((0, rows - values.shape[0]), (0, 0)))


def pad_columns(values, columns):
    return jnp.pad(values, ((0, 0), (0, columns - values.shape[1])))


def norm_parts_of(values):
    average = jnp.mean(values, axis=1, keepdims=True)
    square = jnp.mean(values * values, axis=1, keepdims=True)
    inverse = lax.rsqrt(square - average * average + norm_epsilon)
    return ((values - average) * inverse, inverse)


def norm_backward(grad_out, plain, inverse, gain_row):
    scaled = grad_out * gain_row
    first = jnp.mean(scaled, axis=1, keepdims=True)
    second = jnp.mean(scaled * plain, axis=1, keepdims=True)
    return inverse * (scaled - first - plain * second)


def wide_dot(left_side, right_side, left_dim, right_dim):
    return lax.dot_general(
        left_side,
        right_side,
        (((left_dim,), (right_dim,)), ((), ())),
        preferred_element_type=jnp.float32,
    )


def in_vmem(count):
    return [pl.BlockSpec(memory_space=pltpu.VMEM)] * count


def kernel_call(body, inputs, outputs, scratch, flops, position=None):
    specs = in_vmem(len(inputs))
    operands = list(inputs)
    if position is not None:
        specs = [pl.BlockSpec(memory_space=pltpu.SMEM)] + specs
        operands = [position] + operands
    moved = sum(math.prod(o.shape) * o.dtype.itemsize for o in list(inputs) + list(outputs))
    return pl.pallas_call(
        body,
        out_shape=list(outputs),
        in_specs=specs,
        out_specs=in_vmem(len(outputs)),
        scratch_shapes=scratch,
        compiler_params=pltpu.CompilerParams(vmem_limit_bytes=40 * 1024 * 1024),
        cost_estimate=pl.CostEstimate(flops=flops, bytes_accessed=moved, transcendentals=0),
    )(*operands)


def put_chunks(position_ref, chunk_refs, whole_ref):
    chunk = chunk_refs[0].shape[0]
    for k, chunk_ref in enumerate(chunk_refs):
        start = pl.multiple_of((position_ref[0] ^ k) * chunk, 8)
        whole_ref[pl.ds(start, chunk), :] = chunk_ref[...].astype(jnp.float32)


def take_chunks(position_ref, whole_ref, chunk_refs):
    chunk = chunk_refs[0].shape[0]
    for k, chunk_ref in enumerate(chunk_refs):
        start = pl.multiple_of((position_ref[0] ^ k) * chunk, 8)
        chunk_ref[...] = whole_ref[pl.ds(start, chunk), :].astype(chunk_ref.dtype)


def put_weights(position_ref, block_refs, offsets, *weight_refs):
    for block_ref, offset in zip(block_refs, offsets):
        height = block_ref.shape[0]
        start = pl.multiple_of((position_ref[1] ^ offset) * height, 16)
        first = 0
        for weight_ref in weight_refs:
            width = weight_ref.shape[1]
            weight_ref[pl.ds(start, height), :] = block_ref[:, first : first + width]
            first += width


def keep_rows(values, tokens):
    rows = lax.broadcasted_iota(jnp.int32, values.shape, 0)
    return jnp.where(rows < tokens, values, jnp.zeros_like(values))


def head_probs(mixed, head, tokens):
    start = head * 3 * HD
    query = mixed[:, start : start + HD]
    key = mixed[:, start + HD : start + 2 * HD]
    value = mixed[:, start + 2 * HD : start + 3 * HD]
    scores = wide_dot(query, key, 1, 1) * HD ** (-0.5)
    columns = lax.broadcasted_iota(jnp.int32, scores.shape, 1)
    scores = jnp.where(columns < tokens, scores, -jnp.inf)
    exps = jnp.exp(scores - jnp.max(scores, axis=1, keepdims=True))
    probs = exps / jnp.sum(exps, axis=1, keepdims=True)
    return (query, key, value, probs)


def attend_kernel(tokens, heads, offsets, size, position, *refs):
    rows = len(offsets)
    chunks, blocks = refs[:size], refs[size : size + rows]
    outs = refs[size + rows : 2 * size + rows]
    mixed_out, normed_out, att_out, whole, att_all, w_qkv, w_proj = refs[2 * size + rows :]
    put_weights(position, blocks, offsets, w_qkv, w_proj)
    put_chunks(position, chunks, whole)
    normed = keep_rows(whole[...], tokens).astype(jnp.bfloat16)
    normed_out[...] = normed[: normed_out.shape[0]]
    mixed = wide_dot(normed, w_qkv[...], 1, 0).astype(jnp.bfloat16)
    mixed_out[...] = mixed
    for head in range(heads):
        _, _, value, probs = head_probs(mixed, head, tokens)
        att_all[:, head * HD : (head + 1) * HD] = wide_dot(probs.astype(jnp.bfloat16), value, 1, 0)
    attended = keep_rows(att_all[...], tokens).astype(jnp.bfloat16)
    att_out[...] = jnp.zeros_like(att_out)
    att_out[:, : heads * HD] = attended[: att_out.shape[0]]
    whole[...] = wide_dot(attended, w_proj[...], 1, 1)
    take_chunks(position, whole, outs)


def attend_back_kernel(tokens, heads, offsets, size, position, *refs):
    rows = len(offsets)
    chunks, mixed_ref, blocks = refs[:size], refs[size], refs[size + 1 : size + 1 + rows]
    outs = refs[size + 1 + rows : 2 * size + 1 + rows]
    mixed_grad_out, back_out, whole, mixed_grad, w_qkv, w_proj = refs[2 * size + 1 + rows :]
    put_weights(position, blocks, offsets, w_qkv, w_proj)
    put_chunks(position, chunks, whole)
    back = whole[...].astype(jnp.bfloat16)
    back_out[...] = back[: back_out.shape[0]]
    att_grad = wide_dot(back, w_proj[...], 1, 0).astype(jnp.bfloat16)
    mixed = mixed_ref[...]
    scaling = HD ** (-0.5)
    for head in range(heads):
        query, key, value, probs = head_probs(mixed, head, tokens)
        grad = att_grad[:, head * HD : (head + 1) * HD]
        probs_grad = wide_dot(grad, value, 1, 1)
        inner = jnp.sum(probs * probs_grad, axis=1, keepdims=True)
        scores_grad = (probs * (probs_grad - inner)).astype(jnp.bfloat16)
        start = head * 3 * HD
        mixed_grad[:, start : start + HD] = wide_dot(scores_grad, key, 1, 0) * scaling
        mixed_grad[:, start + HD : start + 2 * HD] = wide_dot(scores_grad, query, 0, 0) * scaling
        mixed_grad[:, start + 2 * HD : start + 3 * HD] = wide_dot(
            probs.astype(jnp.bfloat16), grad, 0, 0
        )
    grads = mixed_grad[...].astype(jnp.bfloat16)
    mixed_grad_out[...] = jnp.zeros_like(mixed_grad_out)
    mixed_grad_out[:, : grads.shape[1]] = grads[: mixed_grad_out.shape[0]]
    whole[...] = wide_dot(grads, w_qkv[...], 1, 1)
    take_chunks(position, whole, outs)


def norm_kernel(level_index, first_row, size, *refs):
    parts, (stream_ref, norms) = refs[:size], refs[size : size + 2]
    stream_out, normed_out = refs[size + 2 :]
    stream = stream_ref[...]
    for part in parts:
        stream = stream + part[...].astype(jnp.float32)
    stream_out[...] = stream
    plain, _ = norm_parts_of(stream)
    gain = norms[level_index, first_row : first_row + 1, :]
    bias = norms[level_index, first_row + 1 : first_row + 2, :]
    normed_out[...] = (plain * gain + bias).astype(jnp.bfloat16)


def norm_back_kernel(level_index, first_row, size, *refs):
    parts, (stream_ref, change_ref, base_ref, norms) = refs[:size], refs[size : size + 4]
    change_out, low_out, sums_out = refs[size + 4 :]
    grad = parts[0][...].astype(jnp.float32)
    for part in parts[1:]:
        grad = grad + part[...].astype(jnp.float32)
    plain, inverse = norm_parts_of(stream_ref[...])
    gain = norms[level_index, first_row : first_row + 1, :]
    change = change_ref[...] + norm_backward(grad, plain, inverse, gain)
    change_out[...] = change
    low_out[...] = (base_ref[...].astype(jnp.float32) + change).astype(jnp.bfloat16)
    sums_out[0:1, :] = jnp.sum(grad * plain, axis=0, keepdims=True)
    sums_out[1:2, :] = jnp.sum(grad, axis=0, keepdims=True)


def first_kernel(tokens, position, blocks, norms, *refs):
    count = (len(refs) - 2) // 2
    outs, back_outs, stream_out, whole = refs[:count], refs[count:-2], refs[-2], refs[-1]
    size, _, width = blocks.shape
    width = width // 2
    whole[...] = jnp.zeros_like(whole)
    for i in range(size):
        whole[0:tokens, i * width : (i + 1) * width] = blocks[i, :, width:].astype(jnp.float32)
    take_chunks(position, whole, back_outs)
    for i in range(size):
        whole[0:tokens, i * width : (i + 1) * width] = blocks[i, :, :width].astype(jnp.float32)
    chunk = stream_out.shape[0]
    start = pl.multiple_of(position[0] * chunk, 8)
    stream_out[...] = whole[pl.ds(start, chunk), :]
    plain, _ = norm_parts_of(whole[...])
    whole[...] = plain * norms[0, 0:1, :] + norms[0, 1:2, :]
    take_chunks(position, whole, outs)


def mlp_kernel(tokens, offsets, size, position, *refs):
    rows = len(offsets)
    chunks, blocks = refs[:size], refs[size : size + rows]
    outs = refs[size + rows : 2 * size + rows]
    slope_out, normed_out, act_out, whole, w_up, w_down = refs[2 * size + rows :]
    put_weights(position, blocks, offsets, w_up, w_down)
    put_chunks(position, chunks, whole)
    normed = keep_rows(whole[...], tokens).astype(jnp.bfloat16)
    normed_out[...] = normed[: normed_out.shape[0]]
    hidden = wide_dot(normed, w_up[...], 1, 0)
    below = 0.5 + 0.5 * lax.erf(hidden * math.sqrt(0.5))
    slope_out[...] = below + hidden * jnp.exp(-0.5 * hidden * hidden) * (
        1.0 / math.sqrt(2.0 * math.pi)
    )
    activated = keep_rows(hidden * below, tokens).astype(jnp.bfloat16)
    act_out[...] = activated[: act_out.shape[0]]
    whole[...] = wide_dot(activated, w_down[...], 1, 1)
    take_chunks(position, whole, outs)


def mlp_back_kernel(offsets, size, position, *refs):
    rows = len(offsets)
    chunks, slope, blocks = refs[:size], refs[size], refs[size + 1 : size + 1 + rows]
    outs = refs[size + 1 + rows : 2 * size + 1 + rows]
    hidden_grad_out, back_out, whole, w_up, w_down = refs[2 * size + 1 + rows :]
    put_weights(position, blocks, offsets, w_up, w_down)
    put_chunks(position, chunks, whole)
    back = whole[...].astype(jnp.bfloat16)
    back_out[...] = back[: back_out.shape[0]]
    hidden_grad = (wide_dot(back, w_down[...], 1, 0) * slope[...]).astype(jnp.bfloat16)
    hidden_grad_out[...] = hidden_grad[: hidden_grad_out.shape[0]]
    whole[...] = wide_dot(hidden_grad, w_up[...], 1, 1)
    take_chunks(position, whole, outs)


def swap_row_col(values):
    size = lax.axis_size("row")
    pairs = [(i * size + j, j * size + i) for i in range(size) for j in range(size)]
    return lax.ppermute(values, ("row", "col"), pairs)


def from_partner(values, step, axes=("dp", "row"), wanted=None):
    count = math.prod(lax.axis_size(a) for a in axes)
    pairs = [(i, i ^ step) for i in range(count) if wanted is None or wanted(i ^ step)]
    return lax.ppermute(values, axes, pairs)


def pick(stacked, index):
    return lax.dynamic_index_in_dim(stacked, index, 0, keepdims=False)


def placed_blocks(blocks, places):
    result = jnp.zeros((len(blocks),) + blocks[0].shape, blocks[0].dtype)
    for block, place in zip(blocks, places):
        result = lax.dynamic_update_index_in_dim(result, block, place, 0)
    return result


def gather_by_pairs(values, axis):
    step = lax.axis_size(axis) // 2
    me = lax.axis_index(axis)
    blocks, places = [values], [me]
    while step:
        sent = blocks[0][None] if len(blocks) == 1 else jnp.stack(blocks)
        received = from_partner(sent, step, (axis,))
        blocks = blocks + [received[i] for i in range(len(blocks))]
        places = places + [p ^ step for p in places]
        step //= 2
    return placed_blocks(blocks, places)


def sum_by_pairs(values, axis):
    step = 1
    while step < lax.axis_size(axis):
        values = values + from_partner(values, step, (axis,))
        step *= 2
    return values


def to_all(block, axis):
    size = lax.axis_size(axis)
    return lax.all_to_all(jnp.broadcast_to(block[None], (size,) + block.shape), axis, 0, 0)


def to_partners(chunk):
    size = lax.axis_size("col")
    return [chunk] + [from_partner(chunk, k, ("col",)) for k in range(1, size)]


def swap_parts(parts):
    return [parts[0]] + [from_partner(parts[k], k, ("col",)) for k in range(1, len(parts))]


def gram_strips(raw):
    size = lax.axis_size("col")
    height = raw.shape[0]
    count = strip_count
    band = height // count
    strips = [
        lax.dot_general(
            raw[i * band : (i + 1) * band],
            raw[i * band :],
            (((1,), (1,)), ((), ())),
            precision=lax.Precision.HIGH,
            preferred_element_type=jnp.float32,
        )
        for i in range(count)
    ]
    packed = jnp.concatenate(strips, axis=1)
    blocks = lax.all_to_all(packed.reshape(size, band // size, -1), "col", 0, 0)
    return jnp.sum(blocks, axis=0)


def halves(values):
    high = values.astype(jnp.bfloat16)
    return (high, (values - high.astype(jnp.float32)).astype(jnp.bfloat16))


def put_halves(refs, rows, columns, values):
    for ref, half in zip(refs, halves(values)):
        ref[rows, columns] = half


def dot_halves(left, rows, right, columns):
    left_high, left_low = left[0][rows, :], left[1][rows, :]
    right_high, right_low = right[0][:, columns], right[1][:, columns]
    return (
        wide_dot(left_high, right_high, 1, 0)
        + wide_dot(left_high, right_low, 1, 0)
        + wide_dot(left_low, right_high, 1, 0)
    )


def schulz_kernel(sweeps, packed, raw, out, gram, half, current, *pairs):
    gram_pair, square_pair, half_pair, current_pair = [pairs[i : i + 2] for i in range(0, 8, 2)]
    height = raw.shape[0]
    third = height // 3
    bands = [slice(i * third, (i + 1) * third) for i in range(3)]
    tails = [slice(i * third, height) for i in range(3)]
    everything = slice(0, height)

    def put_symmetric(pair, i, values):
        put_halves(pair, bands[i], tails[i], values)
        for j in range(i + 1, 3):
            block = values[:, (j - i) * third : (j - i + 1) * third]
            put_halves(pair, bands[j], bands[i], block.T)

    total = jnp.zeros((1, 1), jnp.float32)
    start = 0
    band = height // strip_count
    for i in range(strip_count):
        strip = packed[:, start : start + height - i * band]
        start += height - i * band
        gram[i * band : (i + 1) * band, i * band :] = strip
        if i % 2 == 0:
            gram[(i + 1) * band : (i + 2) * band, i * band : (i + 1) * band] = strip[
                :, band : 2 * band
            ].T
        rows = lax.broadcasted_iota(jnp.int32, (band, band), 0)
        columns = lax.broadcasted_iota(jnp.int32, (band, band), 1)
        diagonal = jnp.where(rows == columns, strip[:, :band], 0.0)
        total = total + jnp.sum(jnp.sum(diagonal, axis=1, keepdims=True), axis=0, keepdims=True)
    scale = 1.0 / (jnp.sqrt(total) + 1e-07)
    for i in range(3):
        values = gram[bands[i], tails[i]] * (scale * scale)
        gram[bands[i], tails[i]] = values
        put_symmetric(gram_pair, i, values)
        values = raw[bands[i], :] * scale
        current[bands[i], :] = values
        put_halves(current_pair, bands[i], everything, values)

    def sweep(index, carry):
        for i in range(3):
            product = dot_halves(gram_pair, bands[i], gram_pair, tails[i])
            square = schulz_second * gram[bands[i], tails[i]] + schulz_third * product
            put_symmetric(square_pair, i, square)
        for i in range(3):
            product = dot_halves(square_pair, bands[i], current_pair, everything)
            current[bands[i], :] = schulz_first * current[bands[i], :] + product

        @pl.when(index < sweeps - 1)
        def _():
            for i in range(3):
                put_halves(current_pair, bands[i], everything, current[bands[i], :])
                product = dot_halves(square_pair, bands[i], gram_pair, tails[i])
                values = schulz_first * gram[bands[i], tails[i]] + product
                half[bands[i], tails[i]] = values
                put_symmetric(half_pair, i, values)
            for i in range(3):
                product = dot_halves(square_pair, bands[i], half_pair, tails[i])
                values = schulz_first * half[bands[i], tails[i]] + product
                gram[bands[i], tails[i]] = values
                put_symmetric(gram_pair, i, values)

        return carry

    lax.fori_loop(0, sweeps, sweep, 0)
    out[...] = current[...].astype(out.dtype)


def schulz(raw, packed):
    height, width = raw.shape
    square_shape = (height, height)
    whole = [pltpu.VMEM(square_shape, jnp.float32)] * 2 + [pltpu.VMEM(raw.shape, jnp.float32)]
    pairs = [pltpu.VMEM(square_shape, jnp.bfloat16)] * 6 + [pltpu.VMEM(raw.shape, jnp.bfloat16)] * 2
    return kernel_call(
        functools.partial(schulz_kernel, 5),
        [packed, raw],
        [jax.ShapeDtypeStruct(raw.shape, jnp.bfloat16)],
        whole + pairs,
        2 * 3 * 14 * height * height * width,
    )[0]


def finish_kernel(levels, flipped, rates, blocks, *refs):
    olds, outs = refs[: len(flipped)], refs[len(flipped) :]
    for kind_index, turned in enumerate(flipped):
        old, new = olds[kind_index], outs[kind_index]
        width = old.shape[1] if turned else old.shape[2]
        for level_index in range(levels):
            block = blocks[kind_index * levels + level_index].astype(jnp.float32)[:, :width]
            block = block.T if turned else block
            if rates is None:
                outs[len(flipped) + kind_index][level_index] = block
                new[level_index] = moment_decay * old[level_index] + block
            else:
                new[level_index] = old[level_index] - rates[kind_index] * block


def on_device(
    residual_in,
    cotangent,
    qkv_weight,
    proj_weight,
    up_weight,
    down_weight,
    norm_params,
    qkv_moment,
    proj_moment,
    up_moment,
    down_moment,
    norm_moment,
):
    tokens, width_row = residual_in.shape
    row_size = lax.axis_size("row")
    col_size = lax.axis_size("col")
    dp_size = lax.axis_size("dp")
    model_width = width_row * row_size
    levels = qkv_weight.shape[0]
    jobs = levels * kinds
    chunk = -(-tokens // (8 * col_size)) * 8
    padded = chunk * col_size
    sent_rows = -(-tokens // 16) * 16
    me = (lax.axis_index("dp") * row_size + lax.axis_index("row")) % jobs
    my_row = lax.axis_index("row")
    my_chunk = lax.axis_index("col") * chunk

    weights = (qkv_weight, proj_weight, up_weight, down_weight)
    moments = (qkv_moment, proj_moment, up_moment, down_moment)
    flipped = (False, True, False, True)

    def upright(array, kind_index, level_index):
        block = array[level_index]
        return block.T if flipped[kind_index] else block

    widths = [
        w.shape[1] if flipped[k] else w.shape[2] for k, w in enumerate(weights)
    ]
    widest = max(widths)

    def own_weights(level_index, which):
        parts = [upright(weights[k], k, level_index).astype(jnp.bfloat16) for k in which]
        return jnp.concatenate(parts, axis=1)

    def first_step(own):
        return from_partner(own, row_size // 2, ("row",))

    offsets = [0]
    step = row_size // 2
    while step:
        offsets = offsets + [o ^ step for o in offsets]
        step //= 2
    offsets = tuple(offsets)

    def gathered_weights(own, first):
        blocks = [own, first]
        step = row_size // 4
        while step:
            blocks = blocks + [from_partner(block, step, ("row",)) for block in blocks]
            step //= 2
        return blocks

    def features_first(blocks):
        return blocks.transpose(1, 0, 2).reshape(blocks.shape[1], model_width)

    all_norms = gather_by_pairs(norm_params, "row")
    all_norms = all_norms.transpose(1, 2, 0, 3).reshape(levels, kinds, model_width)
    both_inputs = jnp.concatenate([residual_in, cotangent.astype(residual_in.dtype)], axis=1)
    image_blocks = to_all(swap_row_col(both_inputs), "col")
    position = jnp.stack([lax.axis_index("col"), my_row]).astype(jnp.int32)
    heads = widths[0] // (3 * HD)

    def shaped(rows, columns, kind):
        return jax.ShapeDtypeStruct((rows, columns), kind)

    low_chunk = shaped(chunk, model_width, jnp.bfloat16)
    full_chunk = shaped(chunk, model_width, jnp.float32)
    low_chunks = [low_chunk] * col_size
    sent = shaped(sent_rows, widest, jnp.bfloat16)
    sent_model = shaped(sent_rows, model_width, jnp.bfloat16)
    whole_scratch = pltpu.VMEM((padded, model_width), jnp.float32)
    attention_flops = 2 * padded * (
        model_width * (widths[0] + widths[1]) + 2 * padded * widths[1]
    )
    perceptron_flops = 2 * padded * model_width * (widths[2] + widths[3])
    chunk_flops = 20 * chunk * model_width

    def norm_step(parts, stream, level_index, first_row):
        return kernel_call(
            functools.partial(norm_kernel, level_index, first_row, len(parts)),
            [*parts, stream, all_norms],
            [full_chunk, low_chunk],
            [],
            chunk_flops,
        )

    def norm_back_step(parts, stream, change, level_index, first_row):
        return kernel_call(
            functools.partial(norm_back_kernel, level_index, first_row, len(parts)),
            [*parts, stream, change, back_base, all_norms],
            [full_chunk, low_chunk, shaped(2, model_width, jnp.float32)],
            [],
            chunk_flops,
        )

    *chunks, stream = kernel_call(
        functools.partial(first_kernel, tokens),
        [image_blocks, all_norms],
        low_chunks + low_chunks + [full_chunk],
        [whole_scratch],
        20 * padded * model_width,
        position,
    )
    chunks, back_chunks = chunks[:col_size], chunks[col_size:]
    back_base = back_chunks[0]
    groups = ((0, 1), (2, 3))

    own_groups = [[own_weights(i, which) for which in groups] for i in range(levels)]
    weight_sets = [[gathered_weights(own, first_step(own)) for own in own_groups[0]]]
    weight_sets += [[] for _ in range(1, levels)]
    attention_scratch = [pltpu.VMEM((model_width, w), jnp.bfloat16) for w in widths[:2]]
    perceptron_scratch = [pltpu.VMEM((model_width, w), jnp.bfloat16) for w in widths[2:]]
    saved = []
    early = [None] * levels
    for level_index in range(levels):
        stream_one = stream
        *parts, mixed, normed_one, attended = kernel_call(
            functools.partial(attend_kernel, tokens, heads, offsets, col_size),
            [*chunks, *weight_sets[level_index][0]],
            low_chunks + [shaped(padded, widths[0], jnp.bfloat16), sent_model, sent],
            [whole_scratch, pltpu.VMEM((padded, widths[1]), jnp.float32)] + attention_scratch,
            attention_flops,
            position,
        )
        if level_index == 1:
            parts, arrived = lax.optimization_barrier((parts, [f[1] for f in later_firsts]))
            for later, first in enumerate(arrived, 1):
                weight_sets[later].append(gathered_weights(own_groups[later][1], first))
        stream_two, normed = norm_step(swap_parts(parts), stream, level_index, 2)
        if level_index == 0:
            normed, own_groups[1:] = lax.optimization_barrier((normed, own_groups[1:]))
            later_firsts = [[first_step(own) for own in owns] for owns in own_groups[1:]]
        chunks = to_partners(normed)
        *parts, slope, normed_two, activated = kernel_call(
            functools.partial(mlp_kernel, tokens, offsets, col_size),
            [*chunks, *weight_sets[level_index][1]],
            low_chunks + [shaped(padded, widths[2], jnp.float32), sent_model, sent],
            [whole_scratch] + perceptron_scratch,
            perceptron_flops,
            position,
        )
        if level_index == 0:
            parts, arrived = lax.optimization_barrier((parts, [f[0] for f in later_firsts]))
            for later, first in enumerate(arrived, 1):
                weight_sets[later].append(gathered_weights(own_groups[later][0], first))
        parts = swap_parts(parts)
        early[level_index] = (normed_one, attended, normed_two, activated)
        if level_index < levels - 1:
            stream, normed = norm_step(parts, stream_two, level_index + 1, 0)
            if level_index == 0:
                normed, late_me = lax.optimization_barrier((normed, me))
            chunks = to_partners(normed)
        else:
            stream = stream_two
            for part in parts:
                stream = stream + part.astype(jnp.float32)
        saved.append((stream_one, stream_two, mixed, slope))

    def blocks_for_owners(values):
        blocks = jnp.stack(
            [v.reshape(chunk, col_size, width_row).transpose(1, 0, 2) for v in values], axis=1
        )
        col = lax.axis_index("col")
        return [pick(blocks, col ^ k) for k in range(col_size)]

    def placed(received):
        col = lax.axis_index("col")
        whole = placed_blocks(received, [col ^ k for k in range(col_size)]).transpose(1, 0, 2, 3)
        return swap_row_col(whole.reshape(whole.shape[0], padded, width_row)[:, :tokens])

    groups_of_jobs = dp_size * row_size // jobs

    def spread(parts_of_levels, arrival, kind_arrival):
        order = [(i, k) for i in arrival for k in kind_arrival]
        blocks = [parts_of_levels[i][k] for i, k in order]
        stack = placed_blocks(blocks, [k * levels + i for i, k in order])
        stack = jnp.concatenate([stack] * groups_of_jobs) if groups_of_jobs > 1 else stack
        return lax.all_to_all(stack, ("dp", "row"), 0, 0).reshape(-1, widest)

    upper = (late_me // row_size) % 2 == 1
    half = jobs // 2
    near_moments = []
    for j in range(half):
        low_job, high_job = [
            pad_columns(upright(moments[i // levels], i // levels, i % levels), widest)
            for i in (j, j + half)
        ]
        near_moments.append(jnp.where(upper, high_job, low_job))
    stacked_moment = jnp.stack(near_moments)
    own_moment = lax.all_to_all(stacked_moment, "row", 0, 0).reshape(model_width, widest)

    back_chunks, own_moment = lax.optimization_barrier((back_chunks, own_moment))
    change = jnp.zeros((chunk, model_width), jnp.float32)
    early_all = spread(early, range(levels), range(kinds))
    late = [None] * levels
    norm_sums = [None] * levels
    for level_index in reversed(range(levels)):
        stream_one, stream_two, mixed, slope = saved[level_index]
        *parts, hidden_grad, back_two = kernel_call(
            functools.partial(mlp_back_kernel, offsets, col_size),
            [*back_chunks, slope, *weight_sets[level_index][1]],
            low_chunks + [sent, sent_model],
            [whole_scratch] + perceptron_scratch,
            perceptron_flops,
            position,
        )
        change, back_low, sums_two = norm_back_step(
            swap_parts(parts), stream_two, change, level_index, 2
        )
        if level_index == 0:
            back_low, early_all = lax.optimization_barrier((back_low, early_all))
        *parts, mixed_grad, back_one = kernel_call(
            functools.partial(attend_back_kernel, tokens, heads, offsets, col_size),
            [*to_partners(back_low), mixed, *weight_sets[level_index][0]],
            low_chunks + [sent, sent_model],
            [whole_scratch, pltpu.VMEM((padded, widths[0]), jnp.float32)] + attention_scratch,
            3 * attention_flops,
            position,
        )
        late[level_index] = (mixed_grad, back_one, hidden_grad, back_two)
        if level_index == 0:
            late_all = spread(late, reversed(range(levels)), (3, 2, 1, 0))
        change, back_low, sums_one = norm_back_step(
            swap_parts(parts), stream_one, change, level_index, 0
        )
        norm_sums[level_index] = jnp.concatenate([sums_one, sums_two])

        if level_index:
            back_chunks = to_partners(back_low)

    norm_whole = sum_by_pairs(jnp.stack(norm_sums), "col")
    late_all, norm_whole, stream, change = lax.optimization_barrier(
        (late_all, norm_whole, stream, change)
    )

    turned = (me // levels) % 2 == 1
    model_side = jnp.where(turned, late_all, early_all)
    hidden_side = jnp.where(turned, early_all, late_all)
    own_grad = outer_grad(model_side, hidden_side)

    def blocks_to_return(whole):
        blocks = whole.astype(jnp.bfloat16).reshape(row_size, width_row, widest)
        return jnp.concatenate([blocks] * dp_size)

    def returned(blocks):
        return lax.all_to_all(blocks, ("dp", "row"), 0, 0)[:jobs]

    own_raw = moment_decay * own_moment + own_grad
    for axis in ("row", "dp"):
        norm_whole = sum_by_pairs(norm_whole, axis)
    tokens_moved = blocks_for_owners([stream, change])
    grad_blocks = blocks_to_return(own_grad)
    own_strip, norm_whole, tokens_moved, grad_blocks = lax.optimization_barrier(
        (gram_strips(own_raw), norm_whole, tokens_moved, grad_blocks)
    )
    norm_grad = lax.dynamic_slice_in_dim(norm_whole, my_row * width_row, width_row, 2)
    norm_moment_new = moment_decay * norm_moment + norm_grad
    gram = to_all(own_strip, "col").reshape(-1, own_strip.shape[1])
    gram, tokens_moved, grad_blocks = lax.optimization_barrier((gram, tokens_moved, grad_blocks))
    tokens_moved = swap_parts(tokens_moved)
    grads = returned(grad_blocks)
    orth_whole, grads, tokens_moved = lax.optimization_barrier(
        (schulz(own_raw, gram), grads, tokens_moved)
    )
    block_output, change = placed(tokens_moved)
    input_grad = cotangent + change
    orths = returned(blocks_to_return(orth_whole))

    def finished(blocks, olds, rates):
        tall = [f and old.shape[1] > old.shape[2] for f, old in zip(flipped, olds)]
        olds = [old.swapaxes(1, 2) if t else old for t, old in zip(tall, olds)]
        turned = tuple(f and not t for f, t in zip(flipped, tall))
        shapes = [jax.ShapeDtypeStruct(old.shape, jnp.float32) for old in olds]
        outs = kernel_call(
            functools.partial(finish_kernel, levels, turned, rates),
            [blocks, *olds],
            shapes if rates else shapes + shapes,
            [],
            2 * sum(math.prod(old.shape) for old in olds),
        )
        return [out.swapaxes(1, 2) if tall[i % kinds] else out for i, out in enumerate(outs)]

    moment_and_grad = finished(grads, moments, None)
    moment_outs, grad_outs = moment_and_grad[:kinds], moment_and_grad[kinds:]
    new_outs = finished(orths, weights, step_rates)

    tokens_all = tokens * col_size * dp_size
    norm_new = norm_params - norm_rate / math.sqrt(tokens_all) * norm_moment_new
    return (
        block_output,
        input_grad,
        *grad_outs,
        norm_grad,
        *moment_outs,
        norm_moment_new,
        *new_outs,
        norm_new,
    )


def solution(mesh):
    tokens_spec = P(("dp", "col"), "row")
    wide = P(None, "row", "col")
    tall = P(None, "col", "row")
    norms = P(None, None, "row")
    return jax.shard_map(
        on_device,
        mesh=mesh,
        in_specs=(tokens_spec, tokens_spec) + (wide, tall, wide, tall, norms) * 2,
        out_specs=(tokens_spec, tokens_spec) + (wide, tall, wide, tall, norms) * 3,
        check_vma=False,
    )
```

```python
import functools
import math

import jax
import jax.numpy as jnp
from jax import lax
from jax.experimental import pallas as pl
from jax.experimental.pallas import tpu as pltpu
from jax.sharding import PartitionSpec as P

HD = 64

norm_epsilon = 1e-06
moment_decay = 0.9
norm_rate = 0.05
step_rates = (1.7, 5.6, 2.0, 1.0)
schulz_first = 3.4445
schulz_second = -4.775
schulz_third = 2.0315
kinds = 4
strip_count = 6


def outer_grad(left_side, right_side):
    return lax.dot_general(
        left_side, right_side, (((0,), (0,)), ((), ())), preferred_element_type=jnp.float32
    )


def pad_rows(values, rows):
    return jnp.pad(values, ((0, rows - values.shape[0]), (0, 0)))


def pad_columns(values, columns):
    return jnp.pad(values, ((0, 0), (0, columns - values.shape[1])))


def norm_parts_of(values):
    average = jnp.mean(values, axis=1, keepdims=True)
    square = jnp.mean(values * values, axis=1, keepdims=True)
    inverse = lax.rsqrt(square - average * average + norm_epsilon)
    return ((values - average) * inverse, inverse)


def norm_backward(grad_out, plain, inverse, gain_row):
    scaled = grad_out * gain_row
    first = jnp.mean(scaled, axis=1, keepdims=True)
    second = jnp.mean(scaled * plain, axis=1, keepdims=True)
    return inverse * (scaled - first - plain * second)


def wide_dot(left_side, right_side, left_dim, right_dim):
    return lax.dot_general(
        left_side,
        right_side,
        (((left_dim,), (right_dim,)), ((), ())),
        preferred_element_type=jnp.float32,
    )


def in_vmem(count):
    return [pl.BlockSpec(memory_space=pltpu.VMEM)] * count


def kernel_call(body, inputs, outputs, scratch, flops, position=None):
    specs = in_vmem(len(inputs))
    operands = list(inputs)
    if position is not None:
        specs = [pl.BlockSpec(memory_space=pltpu.SMEM)] + specs
        operands = [position] + operands
    moved = sum(math.prod(o.shape) * o.dtype.itemsize for o in list(inputs) + list(outputs))
    return pl.pallas_call(
        body,
        out_shape=list(outputs),
        in_specs=specs,
        out_specs=in_vmem(len(outputs)),
        scratch_shapes=scratch,
        compiler_params=pltpu.CompilerParams(vmem_limit_bytes=40 * 1024 * 1024),
        cost_estimate=pl.CostEstimate(flops=flops, bytes_accessed=moved, transcendentals=0),
    )(*operands)


def put_chunks(position_ref, chunk_refs, whole_ref):
    chunk = chunk_refs[0].shape[0]
    for k, chunk_ref in enumerate(chunk_refs):
        start = pl.multiple_of((position_ref[0] ^ k) * chunk, 8)
        whole_ref[pl.ds(start, chunk), :] = chunk_ref[...].astype(jnp.float32)


def take_chunks(position_ref, whole_ref, chunk_refs):
    chunk = chunk_refs[0].shape[0]
    for k, chunk_ref in enumerate(chunk_refs):
        start = pl.multiple_of((position_ref[0] ^ k) * chunk, 8)
        chunk_ref[...] = whole_ref[pl.ds(start, chunk), :].astype(chunk_ref.dtype)


def keep_rows(values, tokens):
    rows = lax.broadcasted_iota(jnp.int32, values.shape, 0)
    return jnp.where(rows < tokens, values, jnp.zeros_like(values))


def head_probs(mixed, head, tokens):
    start = head * 3 * HD
    query = mixed[:, start : start + HD]
    key = mixed[:, start + HD : start + 2 * HD]
    value = mixed[:, start + 2 * HD : start + 3 * HD]
    scores = wide_dot(query, key, 1, 1) * HD ** (-0.5)
    columns = lax.broadcasted_iota(jnp.int32, scores.shape, 1)
    scores = jnp.where(columns < tokens, scores, -jnp.inf)
    exps = jnp.exp(scores - jnp.max(scores, axis=1, keepdims=True))
    probs = exps / jnp.sum(exps, axis=1, keepdims=True)
    return (query, key, value, probs)


def attend_kernel(tokens, heads, position, *refs):
    size = (len(refs) - 7) // 2
    chunks, (w_qkv, w_proj) = refs[:size], refs[size : size + 2]
    outs = refs[size + 2 : 2 * size + 2]
    mixed_out, normed_out, att_out, whole, att_all = refs[2 * size + 2 :]
    put_chunks(position, chunks, whole)
    normed = keep_rows(whole[...], tokens).astype(jnp.bfloat16)
    normed_out[...] = normed[: normed_out.shape[0]]
    mixed = wide_dot(normed, w_qkv[...], 1, 0).astype(jnp.bfloat16)
    mixed_out[...] = mixed
    for head in range(heads):
        _, _, value, probs = head_probs(mixed, head, tokens)
        att_all[:, head * HD : (head + 1) * HD] = wide_dot(probs.astype(jnp.bfloat16), value, 1, 0)
    attended = keep_rows(att_all[...], tokens).astype(jnp.bfloat16)
    att_out[...] = jnp.zeros_like(att_out)
    att_out[:, : heads * HD] = attended[: att_out.shape[0]]
    whole[...] = wide_dot(attended, w_proj[...], 1, 1)
    take_chunks(position, whole, outs)


def attend_back_kernel(tokens, heads, position, *refs):
    size = (len(refs) - 7) // 2
    chunks, (mixed_ref, w_qkv, w_proj) = refs[:size], refs[size : size + 3]
    outs = refs[size + 3 : 2 * size + 3]
    mixed_grad_out, back_out, whole, mixed_grad = refs[2 * size + 3 :]
    put_chunks(position, chunks, whole)
    back = whole[...].astype(jnp.bfloat16)
    back_out[...] = back[: back_out.shape[0]]
    att_grad = wide_dot(back, w_proj[...], 1, 0).astype(jnp.bfloat16)
    mixed = mixed_ref[...]
    scaling = HD ** (-0.5)
    for head in range(heads):
        query, key, value, probs = head_probs(mixed, head, tokens)
        grad = att_grad[:, head * HD : (head + 1) * HD]
        probs_grad = wide_dot(grad, value, 1, 1)
        inner = jnp.sum(probs * probs_grad, axis=1, keepdims=True)
        scores_grad = (probs * (probs_grad - inner)).astype(jnp.bfloat16)
        start = head * 3 * HD
        mixed_grad[:, start : start + HD] = wide_dot(scores_grad, key, 1, 0) * scaling
        mixed_grad[:, start + HD : start + 2 * HD] = wide_dot(scores_grad, query, 0, 0) * scaling
        mixed_grad[:, start + 2 * HD : start + 3 * HD] = wide_dot(
            probs.astype(jnp.bfloat16), grad, 0, 0
        )
    grads = mixed_grad[...].astype(jnp.bfloat16)
    mixed_grad_out[...] = jnp.zeros_like(mixed_grad_out)
    mixed_grad_out[:, : grads.shape[1]] = grads[: mixed_grad_out.shape[0]]
    whole[...] = wide_dot(grads, w_qkv[...], 1, 1)
    take_chunks(position, whole, outs)


def norm_kernel(level_index, first_row, size, *refs):
    parts, (stream_ref, norms) = refs[:size], refs[size : size + 2]
    stream_out, normed_out = refs[size + 2 :]
    stream = stream_ref[...]
    for part in parts:
        stream = stream + part[...].astype(jnp.float32)
    stream_out[...] = stream
    plain, _ = norm_parts_of(stream)
    gain = norms[level_index, first_row : first_row + 1, :]
    bias = norms[level_index, first_row + 1 : first_row + 2, :]
    normed_out[...] = (plain * gain + bias).astype(jnp.bfloat16)


def norm_back_kernel(level_index, first_row, size, *refs):
    parts, (stream_ref, change_ref, base_ref, norms) = refs[:size], refs[size : size + 4]
    change_out, low_out, sums_out = refs[size + 4 :]
    grad = parts[0][...].astype(jnp.float32)
    for part in parts[1:]:
        grad = grad + part[...].astype(jnp.float32)
    plain, inverse = norm_parts_of(stream_ref[...])
    gain = norms[level_index, first_row : first_row + 1, :]
    change = change_ref[...] + norm_backward(grad, plain, inverse, gain)
    change_out[...] = change
    low_out[...] = (base_ref[...].astype(jnp.float32) + change).astype(jnp.bfloat16)
    sums_out[0:1, :] = jnp.sum(grad * plain, axis=0, keepdims=True)
    sums_out[1:2, :] = jnp.sum(grad, axis=0, keepdims=True)


def first_kernel(tokens, position, blocks, norms, *refs):
    count = (len(refs) - 2) // 2
    outs, back_outs, stream_out, whole = refs[:count], refs[count:-2], refs[-2], refs[-1]
    size, _, width = blocks.shape
    width = width // 2
    whole[...] = jnp.zeros_like(whole)
    for i in range(size):
        whole[0:tokens, i * width : (i + 1) * width] = blocks[i, :, width:].astype(jnp.float32)
    take_chunks(position, whole, back_outs)
    for i in range(size):
        whole[0:tokens, i * width : (i + 1) * width] = blocks[i, :, :width].astype(jnp.float32)
    chunk = stream_out.shape[0]
    start = pl.multiple_of(position[0] * chunk, 8)
    stream_out[...] = whole[pl.ds(start, chunk), :]
    plain, _ = norm_parts_of(whole[...])
    whole[...] = plain * norms[0, 0:1, :] + norms[0, 1:2, :]
    take_chunks(position, whole, outs)


def mlp_kernel(tokens, position, *refs):
    size = (len(refs) - 6) // 2
    chunks, (w_up, w_down) = refs[:size], refs[size : size + 2]
    outs = refs[size + 2 : 2 * size + 2]
    slope_out, normed_out, act_out, whole = refs[2 * size + 2 :]
    put_chunks(position, chunks, whole)
    normed = keep_rows(whole[...], tokens).astype(jnp.bfloat16)
    normed_out[...] = normed[: normed_out.shape[0]]
    hidden = wide_dot(normed, w_up[...], 1, 0)
    below = 0.5 + 0.5 * lax.erf(hidden * math.sqrt(0.5))
    slope_out[...] = below + hidden * jnp.exp(-0.5 * hidden * hidden) * (
        1.0 / math.sqrt(2.0 * math.pi)
    )
    activated = keep_rows(hidden * below, tokens).astype(jnp.bfloat16)
    act_out[...] = activated[: act_out.shape[0]]
    whole[...] = wide_dot(activated, w_down[...], 1, 1)
    take_chunks(position, whole, outs)


def mlp_back_kernel(position, *refs):
    size = (len(refs) - 6) // 2
    chunks, (slope, w_up, w_down) = refs[:size], refs[size : size + 3]
    outs = refs[size + 3 : 2 * size + 3]
    hidden_grad_out, back_out, whole = refs[2 * size + 3 :]
    put_chunks(position, chunks, whole)
    back = whole[...].astype(jnp.bfloat16)
    back_out[...] = back[: back_out.shape[0]]
    hidden_grad = (wide_dot(back, w_down[...], 1, 0) * slope[...]).astype(jnp.bfloat16)
    hidden_grad_out[...] = hidden_grad[: hidden_grad_out.shape[0]]
    whole[...] = wide_dot(hidden_grad, w_up[...], 1, 1)
    take_chunks(position, whole, outs)


def swap_row_col(values):
    size = lax.axis_size("row")
    pairs = [(i * size + j, j * size + i) for i in range(size) for j in range(size)]
    return lax.ppermute(values, ("row", "col"), pairs)


def from_partner(values, step, axes=("dp", "row"), wanted=None):
    count = math.prod(lax.axis_size(a) for a in axes)
    pairs = [(i, i ^ step) for i in range(count) if wanted is None or wanted(i ^ step)]
    return lax.ppermute(values, axes, pairs)


def pick(stacked, index):
    return lax.dynamic_index_in_dim(stacked, index, 0, keepdims=False)


def placed_blocks(blocks, places):
    result = jnp.zeros((len(blocks),) + blocks[0].shape, blocks[0].dtype)
    for block, place in zip(blocks, places):
        result = lax.dynamic_update_index_in_dim(result, block, place, 0)
    return result


def gather_by_pairs(values, axis, first=None):
    step = lax.axis_size(axis) // 2
    me = lax.axis_index(axis)
    blocks, places = [values], [me]
    while step:
        sent = blocks[0][None] if len(blocks) == 1 else jnp.stack(blocks)
        received = from_partner(sent, step, (axis,)) if first is None else first
        first = None
        blocks = blocks + [received[i] for i in range(len(blocks))]
        places = places + [p ^ step for p in places]
        step //= 2
    return placed_blocks(blocks, places)


def sum_by_pairs(values, axis):
    step = 1
    while step < lax.axis_size(axis):
        values = values + from_partner(values, step, (axis,))
        step *= 2
    return values


def to_all(block, axis):
    size = lax.axis_size(axis)
    return lax.all_to_all(jnp.broadcast_to(block[None], (size,) + block.shape), axis, 0, 0)


def to_partners(chunk):
    size = lax.axis_size("col")
    return [chunk] + [from_partner(chunk, k, ("col",)) for k in range(1, size)]


def swap_parts(parts):
    return [parts[0]] + [from_partner(parts[k], k, ("col",)) for k in range(1, len(parts))]


def gram_strips(raw):
    size = lax.axis_size("col")
    height = raw.shape[0]
    count = strip_count
    band = height // count
    strips = [
        lax.dot_general(
            raw[i * band : (i + 1) * band],
            raw[i * band :],
            (((1,), (1,)), ((), ())),
            precision=lax.Precision.HIGH,
            preferred_element_type=jnp.float32,
        )
        for i in range(count)
    ]
    packed = jnp.concatenate(strips, axis=1)
    blocks = lax.all_to_all(packed.reshape(size, band // size, -1), "col", 0, 0)
    return jnp.sum(blocks, axis=0)


def halves(values):
    high = values.astype(jnp.bfloat16)
    return (high, (values - high.astype(jnp.float32)).astype(jnp.bfloat16))


def put_halves(refs, rows, columns, values):
    for ref, half in zip(refs, halves(values)):
        ref[rows, columns] = half


def dot_halves(left, rows, right, columns):
    left_high, left_low = left[0][rows, :], left[1][rows, :]
    right_high, right_low = right[0][:, columns], right[1][:, columns]
    return (
        wide_dot(left_high, right_high, 1, 0)
        + wide_dot(left_high, right_low, 1, 0)
        + wide_dot(left_low, right_high, 1, 0)
    )


def schulz_kernel(sweeps, packed, raw, out, gram, half, current, *pairs):
    gram_pair, square_pair, half_pair, current_pair = [pairs[i : i + 2] for i in range(0, 8, 2)]
    height = raw.shape[0]
    third = height // 3
    bands = [slice(i * third, (i + 1) * third) for i in range(3)]
    tails = [slice(i * third, height) for i in range(3)]
    everything = slice(0, height)

    def put_symmetric(pair, i, values):
        put_halves(pair, bands[i], tails[i], values)
        for j in range(i + 1, 3):
            block = values[:, (j - i) * third : (j - i + 1) * third]
            put_halves(pair, bands[j], bands[i], block.T)

    total = jnp.zeros((1, 1), jnp.float32)
    start = 0
    band = height // strip_count
    for i in range(strip_count):
        strip = packed[:, start : start + height - i * band]
        start += height - i * band
        gram[i * band : (i + 1) * band, i * band :] = strip
        if i % 2 == 0:
            gram[(i + 1) * band : (i + 2) * band, i * band : (i + 1) * band] = strip[
                :, band : 2 * band
            ].T
        rows = lax.broadcasted_iota(jnp.int32, (band, band), 0)
        columns = lax.broadcasted_iota(jnp.int32, (band, band), 1)
        diagonal = jnp.where(rows == columns, strip[:, :band], 0.0)
        total = total + jnp.sum(jnp.sum(diagonal, axis=1, keepdims=True), axis=0, keepdims=True)
    scale = 1.0 / (jnp.sqrt(total) + 1e-07)
    for i in range(3):
        values = gram[bands[i], tails[i]] * (scale * scale)
        gram[bands[i], tails[i]] = values
        put_symmetric(gram_pair, i, values)
        values = raw[bands[i], :] * scale
        current[bands[i], :] = values
        put_halves(current_pair, bands[i], everything, values)

    def sweep(index, carry):
        for i in range(3):
            product = dot_halves(gram_pair, bands[i], gram_pair, tails[i])
            square = schulz_second * gram[bands[i], tails[i]] + schulz_third * product
            put_symmetric(square_pair, i, square)
        for i in range(3):
            product = dot_halves(square_pair, bands[i], current_pair, everything)
            current[bands[i], :] = schulz_first * current[bands[i], :] + product

        @pl.when(index < sweeps - 1)
        def _():
            for i in range(3):
                put_halves(current_pair, bands[i], everything, current[bands[i], :])
                product = dot_halves(square_pair, bands[i], gram_pair, tails[i])
                values = schulz_first * gram[bands[i], tails[i]] + product
                half[bands[i], tails[i]] = values
                put_symmetric(half_pair, i, values)
            for i in range(3):
                product = dot_halves(square_pair, bands[i], half_pair, tails[i])
                values = schulz_first * half[bands[i], tails[i]] + product
                gram[bands[i], tails[i]] = values
                put_symmetric(gram_pair, i, values)

        return carry

    lax.fori_loop(0, sweeps, sweep, 0)
    out[...] = current[...].astype(out.dtype)


def schulz(raw, packed):
    height, width = raw.shape
    square_shape = (height, height)
    whole = [pltpu.VMEM(square_shape, jnp.float32)] * 2 + [pltpu.VMEM(raw.shape, jnp.float32)]
    pairs = [pltpu.VMEM(square_shape, jnp.bfloat16)] * 6 + [pltpu.VMEM(raw.shape, jnp.bfloat16)] * 2
    return kernel_call(
        functools.partial(schulz_kernel, 5),
        [packed, raw],
        [jax.ShapeDtypeStruct(raw.shape, jnp.bfloat16)],
        whole + pairs,
        2 * 3 * 14 * height * height * width,
    )[0]


def finish_kernel(levels, flipped, rates, blocks, *refs):
    olds, outs = refs[: len(flipped)], refs[len(flipped) :]
    for kind_index, turned in enumerate(flipped):
        old, new = olds[kind_index], outs[kind_index]
        width = old.shape[1] if turned else old.shape[2]
        for level_index in range(levels):
            block = blocks[kind_index * levels + level_index].astype(jnp.float32)[:, :width]
            block = block.T if turned else block
            if rates is None:
                outs[len(flipped) + kind_index][level_index] = block
                new[level_index] = moment_decay * old[level_index] + block
            else:
                new[level_index] = old[level_index] - rates[kind_index] * block


def on_device(
    residual_in,
    cotangent,
    qkv_weight,
    proj_weight,
    up_weight,
    down_weight,
    norm_params,
    qkv_moment,
    proj_moment,
    up_moment,
    down_moment,
    norm_moment,
):
    tokens, width_row = residual_in.shape
    row_size = lax.axis_size("row")
    col_size = lax.axis_size("col")
    dp_size = lax.axis_size("dp")
    model_width = width_row * row_size
    levels = qkv_weight.shape[0]
    jobs = levels * kinds
    chunk = -(-tokens // (8 * col_size)) * 8
    padded = chunk * col_size
    sent_rows = -(-tokens // 16) * 16
    me = (lax.axis_index("dp") * row_size + lax.axis_index("row")) % jobs
    my_row = lax.axis_index("row")
    my_chunk = lax.axis_index("col") * chunk

    weights = (qkv_weight, proj_weight, up_weight, down_weight)
    moments = (qkv_moment, proj_moment, up_moment, down_moment)
    flipped = (False, True, False, True)

    def upright(array, kind_index, level_index):
        block = array[level_index]
        return block.T if flipped[kind_index] else block

    widths = [
        w.shape[1] if flipped[k] else w.shape[2] for k, w in enumerate(weights)
    ]
    widest = max(widths)

    def own_weights(level_index, which):
        parts = [upright(weights[k], k, level_index).astype(jnp.bfloat16) for k in which]
        return jnp.concatenate(parts, axis=1)

    def gathered_weights(own, which, first):
        whole = gather_by_pairs(own, "row", first)
        whole = whole.reshape(model_width, -1)
        result = []
        start = 0
        for k in which:
            result.append(whole[:, start : start + widths[k]])
            start += widths[k]
        return result

    def features_first(blocks):
        return blocks.transpose(1, 0, 2).reshape(blocks.shape[1], model_width)

    all_norms = gather_by_pairs(norm_params, "row")
    all_norms = all_norms.transpose(1, 2, 0, 3).reshape(levels, kinds, model_width)
    both_inputs = jnp.concatenate([residual_in, cotangent.astype(residual_in.dtype)], axis=1)
    image_blocks = to_all(swap_row_col(both_inputs), "col")
    position = lax.axis_index("col").astype(jnp.int32).reshape(1)
    heads = widths[0] // (3 * HD)

    def shaped(rows, columns, kind):
        return jax.ShapeDtypeStruct((rows, columns), kind)

    low_chunk = shaped(chunk, model_width, jnp.bfloat16)
    full_chunk = shaped(chunk, model_width, jnp.float32)
    low_chunks = [low_chunk] * col_size
    sent = shaped(sent_rows, widest, jnp.bfloat16)
    sent_model = shaped(sent_rows, model_width, jnp.bfloat16)
    whole_scratch = pltpu.VMEM((padded, model_width), jnp.float32)
    attention_flops = 2 * padded * (
        model_width * (widths[0] + widths[1]) + 2 * padded * widths[1]
    )
    perceptron_flops = 2 * padded * model_width * (widths[2] + widths[3])
    chunk_flops = 20 * chunk * model_width

    def norm_step(parts, stream, level_index, first_row):
        return kernel_call(
            functools.partial(norm_kernel, level_index, first_row, len(parts)),
            [*parts, stream, all_norms],
            [full_chunk, low_chunk],
            [],
            chunk_flops,
        )

    def norm_back_step(parts, stream, change, level_index, first_row):
        return kernel_call(
            functools.partial(norm_back_kernel, level_index, first_row, len(parts)),
            [*parts, stream, change, back_base, all_norms],
            [full_chunk, low_chunk, shaped(2, model_width, jnp.float32)],
            [],
            chunk_flops,
        )

    *chunks, stream = kernel_call(
        functools.partial(first_kernel, tokens),
        [image_blocks, all_norms],
        low_chunks + low_chunks + [full_chunk],
        [whole_scratch],
        20 * padded * model_width,
        position,
    )
    chunks, back_chunks = chunks[:col_size], chunks[col_size:]
    back_base = back_chunks[0]
    groups = ((0, 1), (2, 3))

    def first_steps(own_groups):
        return [from_partner(own[None], row_size // 2, ("row",)) for own in own_groups]

    def weights_of(own_groups, firsts):
        parts = zip(own_groups, groups, firsts)
        return sum([gathered_weights(own, which, first) for own, which, first in parts], [])

    own_groups = [[own_weights(i, which) for which in groups] for i in range(levels)]
    weight_sets = [weights_of(own_groups[0], first_steps(own_groups[0]))] + [None] * (levels - 1)
    saved = []
    early = [None] * levels
    for level_index in range(levels):
        weight_qkv, weight_proj = weight_sets[level_index][:2]
        if level_index == 0:
            weight_up, weight_down = weight_sets[0][2:]
        stream_one = stream
        *parts, mixed, normed_one, attended = kernel_call(
            functools.partial(attend_kernel, tokens, heads),
            [*chunks, weight_qkv, weight_proj],
            low_chunks + [shaped(padded, widths[0], jnp.bfloat16), sent_model, sent],
            [whole_scratch, pltpu.VMEM((padded, widths[1]), jnp.float32)],
            attention_flops,
            position,
        )
        if level_index == 1:
            parts, arrived = lax.optimization_barrier((parts, [f[1] for f in later_firsts]))
            for later, first in enumerate(arrived, 1):
                weight_sets[later] += gathered_weights(own_groups[later][1], groups[1], first)
            weight_up, weight_down = weight_sets[level_index][2:]
        stream_two, normed = norm_step(swap_parts(parts), stream, level_index, 2)
        if level_index == 0:
            normed, own_groups[1:] = lax.optimization_barrier((normed, own_groups[1:]))
            later_firsts = [first_steps(own) for own in own_groups[1:]]
        chunks = to_partners(normed)
        *parts, slope, normed_two, activated = kernel_call(
            functools.partial(mlp_kernel, tokens),
            [*chunks, weight_up, weight_down],
            low_chunks + [shaped(padded, widths[2], jnp.float32), sent_model, sent],
            [whole_scratch],
            perceptron_flops,
            position,
        )
        if level_index == 0:
            parts, arrived = lax.optimization_barrier((parts, [f[0] for f in later_firsts]))
            for later, first in enumerate(arrived, 1):
                weight_sets[later] = gathered_weights(own_groups[later][0], groups[0], first)
        parts = swap_parts(parts)
        early[level_index] = (normed_one, attended, normed_two, activated)
        if level_index < levels - 1:
            stream, normed = norm_step(parts, stream_two, level_index + 1, 0)
            if level_index == 0:
                normed, late_me = lax.optimization_barrier((normed, me))
            chunks = to_partners(normed)
        else:
            stream = stream_two
            for part in parts:
                stream = stream + part.astype(jnp.float32)
        saved.append((stream_one, stream_two, mixed, slope))

    def blocks_for_owners(values):
        blocks = jnp.stack(
            [v.reshape(chunk, col_size, width_row).transpose(1, 0, 2) for v in values], axis=1
        )
        col = lax.axis_index("col")
        return [pick(blocks, col ^ k) for k in range(col_size)]

    def placed(received):
        col = lax.axis_index("col")
        whole = placed_blocks(received, [col ^ k for k in range(col_size)]).transpose(1, 0, 2, 3)
        return swap_row_col(whole.reshape(whole.shape[0], padded, width_row)[:, :tokens])

    groups_of_jobs = dp_size * row_size // jobs

    def spread(parts_of_levels, arrival, kind_arrival):
        order = [(i, k) for i in arrival for k in kind_arrival]
        blocks = [parts_of_levels[i][k] for i, k in order]
        stack = placed_blocks(blocks, [k * levels + i for i, k in order])
        stack = jnp.concatenate([stack] * groups_of_jobs) if groups_of_jobs > 1 else stack
        return lax.all_to_all(stack, ("dp", "row"), 0, 0).reshape(-1, widest)

    upper = (late_me // row_size) % 2 == 1
    half = jobs // 2
    near_moments = []
    for j in range(half):
        low_job, high_job = [
            pad_columns(upright(moments[i // levels], i // levels, i % levels), widest)
            for i in (j, j + half)
        ]
        near_moments.append(jnp.where(upper, high_job, low_job))
    stacked_moment = jnp.stack(near_moments)
    own_moment = lax.all_to_all(stacked_moment, "row", 0, 0).reshape(model_width, widest)

    back_chunks, own_moment = lax.optimization_barrier((back_chunks, own_moment))
    change = jnp.zeros((chunk, model_width), jnp.float32)
    early_all = spread(early, range(levels), range(kinds))
    late = [None] * levels
    norm_sums = [None] * levels
    for level_index in reversed(range(levels)):
        weight_qkv, weight_proj, weight_up, weight_down = weight_sets[level_index]
        stream_one, stream_two, mixed, slope = saved[level_index]
        *parts, hidden_grad, back_two = kernel_call(
            mlp_back_kernel,
            [*back_chunks, slope, weight_up, weight_down],
            low_chunks + [sent, sent_model],
            [whole_scratch],
            perceptron_flops,
            position,
        )
        change, back_low, sums_two = norm_back_step(
            swap_parts(parts), stream_two, change, level_index, 2
        )
        if level_index == 0:
            back_low, early_all = lax.optimization_barrier((back_low, early_all))
        *parts, mixed_grad, back_one = kernel_call(
            functools.partial(attend_back_kernel, tokens, heads),
            [*to_partners(back_low), mixed, weight_qkv, weight_proj],
            low_chunks + [sent, sent_model],
            [whole_scratch, pltpu.VMEM((padded, widths[0]), jnp.float32)],
            3 * attention_flops,
            position,
        )
        late[level_index] = (mixed_grad, back_one, hidden_grad, back_two)
        if level_index == 0:
            late_all = spread(late, reversed(range(levels)), (3, 2, 1, 0))
        change, back_low, sums_one = norm_back_step(
            swap_parts(parts), stream_one, change, level_index, 0
        )
        norm_sums[level_index] = jnp.concatenate([sums_one, sums_two])

        if level_index:
            back_chunks = to_partners(back_low)

    norm_whole = sum_by_pairs(jnp.stack(norm_sums), "col")
    late_all, norm_whole, stream, change = lax.optimization_barrier(
        (late_all, norm_whole, stream, change)
    )

    turned = (me // levels) % 2 == 1
    model_side = jnp.where(turned, late_all, early_all)
    hidden_side = jnp.where(turned, early_all, late_all)
    own_grad = outer_grad(model_side, hidden_side)

    def blocks_to_return(whole):
        blocks = whole.astype(jnp.bfloat16).reshape(row_size, width_row, widest)
        return jnp.concatenate([blocks] * dp_size)

    def returned(blocks):
        return lax.all_to_all(blocks, ("dp", "row"), 0, 0)[:jobs]

    own_raw = moment_decay * own_moment + own_grad
    for axis in ("row", "dp"):
        norm_whole = sum_by_pairs(norm_whole, axis)
    tokens_moved = blocks_for_owners([stream, change])
    grad_blocks = blocks_to_return(own_grad)
    own_strip, norm_whole, tokens_moved, grad_blocks = lax.optimization_barrier(
        (gram_strips(own_raw), norm_whole, tokens_moved, grad_blocks)
    )
    norm_grad = lax.dynamic_slice_in_dim(norm_whole, my_row * width_row, width_row, 2)
    norm_moment_new = moment_decay * norm_moment + norm_grad
    gram = to_all(own_strip, "col").reshape(-1, own_strip.shape[1])
    gram, tokens_moved, grad_blocks = lax.optimization_barrier((gram, tokens_moved, grad_blocks))
    grads = returned(grad_blocks)
    orth_whole, grads, tokens_moved = lax.optimization_barrier(
        (schulz(own_raw, gram), grads, tokens_moved)
    )
    block_output, change = placed(swap_parts(tokens_moved))
    input_grad = cotangent + change
    orths = returned(blocks_to_return(orth_whole))

    def finished(blocks, olds, rates):
        tall = [f and old.shape[1] > old.shape[2] for f, old in zip(flipped, olds)]
        olds = [old.swapaxes(1, 2) if t else old for t, old in zip(tall, olds)]
        turned = tuple(f and not t for f, t in zip(flipped, tall))
        shapes = [jax.ShapeDtypeStruct(old.shape, jnp.float32) for old in olds]
        outs = kernel_call(
            functools.partial(finish_kernel, levels, turned, rates),
            [blocks, *olds],
            shapes if rates else shapes + shapes,
            [],
            2 * sum(math.prod(old.shape) for old in olds),
        )
        return [out.swapaxes(1, 2) if tall[i % kinds] else out for i, out in enumerate(outs)]

    moment_and_grad = finished(grads, moments, None)
    moment_outs, grad_outs = moment_and_grad[:kinds], moment_and_grad[kinds:]
    new_outs = finished(orths, weights, step_rates)

    tokens_all = tokens * col_size * dp_size
    norm_new = norm_params - norm_rate / math.sqrt(tokens_all) * norm_moment_new
    return (
        block_output,
        input_grad,
        *grad_outs,
        norm_grad,
        *moment_outs,
        norm_moment_new,
        *new_outs,
        norm_new,
    )


def solution(mesh):
    tokens_spec = P(("dp", "col"), "row")
    wide = P(None, "row", "col")
    tall = P(None, "col", "row")
    norms = P(None, None, "row")
    return jax.shard_map(
        on_device,
        mesh=mesh,
        in_specs=(tokens_spec, tokens_spec) + (wide, tall, wide, tall, norms) * 2,
        out_specs=(tokens_spec, tokens_spec) + (wide, tall, wide, tall, norms) * 3,
        check_vma=False,
    )
```
